32 devices in a mesh: dp: 8 (over y, x, core), mlp: 4 (over z).
Axes of the slice: x: 2, y: 2, z: 4, core: 2. Of those that a mesh axis runs over, the one named last changes fastest.
Arguments:
- pixels: bfloat16 [8, 12, 196, 768], P('dp'), may hold values from -6 to 6
- lengths: int32 [8], P('dp'), may hold values from 4 to 12
- frame_mask: int32 [8, 12], P('dp'), may hold values 0 or 1
- time_index: int32 [8, 12], P('dp'), may hold values from 0 to 7
- label_valid: int32 [8, 400], P('dp'), may hold values from 0 to 1
- targets: float32 [8, 400], P('dp'), may hold values from 0 to 1
- owners: int32 [272], replicated, may hold values from 0 to 31, as said below
- slot_weight: float32 [13824, 768], P(('dp', 'mlp')), may hold values from -0.21875 to 0.21875
- slot_moment1: float32 [13824, 768], P(('dp', 'mlp')), may hold values from -4.7683716e-07 to 4.7683716e-07
- slot_moment2: float32 [13824, 768], P(('dp', 'mlp')), may hold values from 9.520937e-17 to 3.8083747e-16
- tables: float32 [220, 768], replicated
- table_moment1: float32 [220, 768], replicated, may hold values from -1.4305115e-06 to 1.4305115e-06
- table_moment2: float32 [220, 768], replicated, may hold values from 9.520937e-16 to 3.808375e-15
- head_weight: float32 [768, 400], replicated, may hold values from -0.625 to 0.625
- head_moment1: float32 [768, 400], replicated, may hold values from -4.7683716e-07 to 4.7683716e-07
- head_moment2: float32 [768, 400], replicated, may hold values from 9.520937e-17 to 3.8083747e-16
Outputs:
- loss_sum: float32 [], replicated
- label_total: float32 [], replicated
- grad_norm: float32 [], replicated
- new_slot_weight: float32 [13824, 768], P(('dp', 'mlp'))
- new_slot_moment1: float32 [13824, 768], P(('dp', 'mlp'))
- new_slot_moment2: float32 [13824, 768], P(('dp', 'mlp'))
- new_tables: float32 [220, 768], replicated
- new_table_moment1: float32 [220, 768], replicated
- new_table_moment2: float32 [220, 768], replicated
- new_head: float32 [768, 400], replicated
- new_head_moment1: float32 [768, 400], replicated
- new_head_moment2: float32 [768, 400], replicated
The draws below stay inside these ranges and needn't reach their ends.
Inputs may be any that keep to these rules, and one draw needn't show every extreme that they name: `owners`: shared block b < 144 is owned by a device with mlp index b % 4; block 144 + j * 2 * (D // 48) + k is owned by a device with mlp index j. No device owns more than 9 blocks and some device owns exactly 9.
All inputs are finite; a program needn't handle non-finite values. No bound on the sum of `frame_mask` on one device may be relied on, other than what follows from the above.
Results may differ from the reference program's by a relative error of at most 0.0065.
Values may be sent and summed in bfloat16 or wider, within the bound.
No kernel may reach another device: no remote copies, remote signals or barrier semaphores. Data moves between devices by JAX's collectives and lax.ppermute only.
A program may use at most 384 MiB of HBM per device.

```python
import math
import jax
import jax.numpy as jnp
import numpy as np
from jax import lax

D = 768
HEADS = 12
HEAD_DIM = 64
CLS = 400
PATCHES = 196
FRAMES = 12
MIN_LEN = 4
TROWS = 8
BR = 48
STEP = 10
CLIPS = 8
SLOT = 9
NV = 220
NPARAM = 10503168
N_DP = 8
N_MLP = 4
DEVICES = 32


def draw_label_valid(key, part):
    key = jax.random.fold_in(key, 7)
    levels = jax.random.randint(key, (CLIPS, CLS), 0, 4 * CLIPS)
    bounds = CLIPS + 2 * jnp.arange(CLIPS)[:, None]
    return (levels < bounds).astype(jnp.int32)


def draw_owners(key, part):
    key = jax.random.fold_in(key, 3)
    per_tile = D // BR
    shared = 9 * per_tile
    slot_count = N_DP * SLOT
    owners = jnp.zeros((shared + 2 * per_tile * N_MLP,), jnp.int32)
    for member in range(N_MLP):
        member_key = jax.random.fold_in(key, member)
        chosen = jax.random.randint(jax.random.fold_in(member_key, 1), (), 0, N_DP)
        places = jnp.arange(slot_count)
        scores = jax.random.randint(member_key, (slot_count,), 0, 65536) * slot_count + places
        scores = jnp.where(places // SLOT == chosen, places - slot_count, scores)
        ranking = jnp.argsort(scores)
        blocks = np.concatenate([np.arange(member, shared, N_MLP), shared + member * 2 * per_tile + np.arange(2 * per_tile)])
        devices = ranking[:blocks.shape[0]] // SLOT
        owners = owners.at[blocks].set((devices * N_MLP + member).astype(jnp.int32))
    return owners


def draw_tables(key, part):
    key = jax.random.fold_in(key, 11)
    row_ids = jnp.arange(NV)[:, None]
    gain_rows = (row_ids == 1) | (row_ids == 6) | (row_ids == 11) | (row_ids == 14)
    normal_draw = jax.random.normal(key, (NV, D), jnp.float32)
    spread = jax.random.uniform(jax.random.fold_in(key, 1), (NV, D), jnp.float32, 0.6, 1.4)
    return jnp.where(gain_rows, spread, jnp.where(row_ids < 16, 0.3 * normal_draw, 0.5 * normal_draw))


def set_ends(entries, own_key, smallest, high):
    longest = entries.shape.index(max(entries.shape))
    spots = []
    for shift in (0, 1):
        where = [jax.random.randint(jax.random.fold_in(own_key, axis), (), 0, length) for axis, length in enumerate(entries.shape)]
        where[longest] = (where[longest] + shift) % entries.shape[longest]
        spots.append(tuple(where))
    return entries.at[spots[0]].set(smallest).at[spots[1]].set(high)


def level_of(rng, dims, shards, least, top_value):
    def one(dim, blocks):
        steps = jax.random.uniform(jax.random.fold_in(jax.random.fold_in(rng, 6), dim), (blocks,), jnp.float32, least / len(shards), top_value / len(shards))
        return jnp.repeat(jnp.exp(steps), dims[dim] // blocks).reshape((-1,) + (1,) * (len(dims) - dim - 1))

    level = one(*shards[0])
    for cut in shards[1:]:
        level = level * one(*cut)
    return level


def gaussian(own_key, dims, scale, bound, cuts=(), held_as=jnp.bfloat16):
    entries = jax.random.normal(own_key, dims, jnp.float32) * scale
    if len(cuts) > 0:
        entries = level_of(own_key, dims, cuts, -0.22, 0.18) * entries
    return jnp.clip(entries, min=-bound, max=bound).astype(held_as)


def setup_inputs(seed: int = 0) -> dict:
    splits = jax.random.split(jax.random.key(seed), 17)
    return {
        "pixels": gaussian(splits[0], (CLIPS, FRAMES, PATCHES, D), 1.0, 6.0, ((0, 8),)),
        "lengths": set_ends(jax.random.randint(splits[1], (CLIPS,), MIN_LEN, FRAMES + 1), jax.random.fold_in(splits[1], 1), MIN_LEN, FRAMES).astype(jnp.int32),
        "frame_mask": set_ends((jax.random.randint(splits[2], (CLIPS, FRAMES), 0, 8) < 7).astype(jnp.int32), jax.random.fold_in(splits[2], 1), 0, 1),
        "time_index": set_ends(jax.random.randint(splits[3], (CLIPS, FRAMES), 0, TROWS), jax.random.fold_in(splits[3], 1), 0, TROWS - 1).astype(jnp.int32),
        "label_valid": draw_label_valid(jax.random.fold_in(splits[16], 71), 0),
        "targets": jnp.clip(1.0 * jax.random.uniform(splits[5], (CLIPS, CLS), jnp.float32) ** level_of(splits[5], (CLIPS, CLS), ((0, 8),), -0.2, 0.2), 0.0, 1.0),
        "owners": draw_owners(jax.random.fold_in(splits[16], 71), 0),
        "slot_weight": gaussian(splits[7], (DEVICES * SLOT * BR, D), D ** -0.5, 0.21875, ((0, 32),), jnp.float32),
        "slot_moment1": gaussian(splits[8], (DEVICES * SLOT * BR, D), (0.0001 * NPARAM ** -0.5), 4.76837158203125e-07, ((0, 32),), jnp.float32),
        "slot_moment2": jnp.clip(jnp.exp(math.log(3.8083747450010097e-16) - 1.3862944 * jax.random.uniform(splits[9], (DEVICES * SLOT * BR, D), jnp.float32) ** level_of(splits[9], (DEVICES * SLOT * BR, D), ((0, 32),), -0.2, 0.2)), 9.520936862502524e-17, 3.8083747450010097e-16),
        "tables": draw_tables(jax.random.fold_in(splits[16], 71), 0),
        "table_moment1": gaussian(splits[11], (NV, D), (0.0003 * NPARAM ** -0.5), 1.430511474609375e-06, (), jnp.float32),
        "table_moment2": jnp.clip(jnp.exp(jax.random.uniform(splits[12], (NV, D), jnp.float32, math.log(9.520937259549218e-16), math.log(3.808374903819687e-15))), 9.520937259549218e-16, 3.808374903819687e-15),
        "head_weight": gaussian(splits[13], (D, CLS), (D // 8) ** -0.5, 0.625, (), jnp.float32),
        "head_moment1": gaussian(splits[14], (D, CLS), (0.0001 * NPARAM ** -0.5), 4.76837158203125e-07, (), jnp.float32),
        "head_moment2": jnp.clip(jnp.exp(jax.random.uniform(splits[15], (D, CLS), jnp.float32, math.log(9.520936862502524e-17), math.log(3.8083747450010097e-16))), 9.520936862502524e-17, 3.8083747450010097e-16),
    }


@jax.custom_vjp
def low(v):
    return lax.optimization_barrier(v.astype(jnp.bfloat16)).astype(jnp.float32)

@jax.custom_vjp
def low_back(v):
    return v

def low_keep(v):
    return (low(v), None)

def low_pass(kept, grad):
    return (grad,)

def back_keep(v):
    return (v, None)

def back_low(kept, grad):
    return (low(grad),)
low.defvjp(low_keep, low_pass)
low_back.defvjp(back_keep, back_low)
ln_eps = 1e-06
beta_one = 0.9
beta_two = 0.999
learn_rate = 0.05
table_rate = 0.4
decay_rate = 0.05
adam_eps = 1e-08
clip_max = 0.001
highest = lax.Precision.HIGHEST

def matmul(left, right):
    return jnp.dot(left, right, precision=highest, preferred_element_type=jnp.float32)

def layer_norm(values, gain, shift):
    centred = values - lax.optimization_barrier(jnp.mean(values, axis=-1, keepdims=True))
    return centred * lax.rsqrt(lax.optimization_barrier(jnp.mean(centred * centred, axis=-1, keepdims=True)) + ln_eps) * gain + shift

def block_ranks(owners):
    total_blocks = owners.shape[0]
    same_owner = owners[:, None] == owners[None, :]
    earlier = jnp.arange(total_blocks)[None, :] < jnp.arange(total_blocks)[:, None]
    return lax.optimization_barrier(jnp.sum((same_owner & earlier).astype(jnp.int32), axis=1)).astype(jnp.int32)

def adamw(weight, gradient, moment_one, moment_two, weight_decay, rate):
    first_new = beta_one * moment_one + (1.0 - beta_one) * gradient
    second_new = beta_two * moment_two + (1.0 - beta_two) * gradient * gradient
    mean_hat = first_new / (1.0 - beta_one ** STEP)
    var_hat = second_new / (1.0 - beta_two ** STEP)
    updated = weight - rate * (mean_hat / (jnp.sqrt(var_hat) + adam_eps) + weight_decay * weight)
    return (updated, first_new, second_new)

def attention(normed_b, tile_set, bias_set, temporal, allowed):
    head_shape = (FRAMES, PATCHES, HEADS, HEAD_DIM)
    queries = low(low_back(matmul(normed_b, tile_set[0]) + bias_set[0])).reshape(head_shape)
    key_rows = low(low_back(matmul(normed_b, tile_set[1]))).reshape(head_shape)
    valued = low(low_back(matmul(normed_b, tile_set[2]) + bias_set[1])).reshape(head_shape)
    if temporal:
        einsum_forms = ('fphd,gphd->phfg', 'phfg,gphd->fphd')
    else:
        einsum_forms = ('fphd,fqhd->fhpq', 'fhpq,fqhd->fphd')
    scores = low_back(jnp.einsum(einsum_forms[0], queries, key_rows, precision=highest) * HEAD_DIM ** (-0.5))
    if temporal:
        scores = jnp.where(allowed[None, None], scores, -1e+30)
    softmax_w = low(jax.nn.softmax(scores, axis=-1))
    merged = jnp.einsum(einsum_forms[1], softmax_w, valued, precision=highest).reshape(FRAMES * PATCHES, D)
    merged = low(low_back(merged))
    return low_back(matmul(merged, tile_set[3])) + bias_set[2]

def clip_loss(params, pixels, length, frame_mask, time_index, valid, target):
    shared, ups, downs, tables, head = params
    shared = low(shared)
    ups = low(ups)
    downs = low(downs)
    head_b = low(head)
    pix_rows = pixels.reshape(FRAMES * PATCHES, D)
    slot_pos = jnp.arange(FRAMES)
    frame_live = slot_pos < length
    key_ok = frame_live & (frame_mask == 1)
    allowed = key_ok[None, :] | (slot_pos[:, None] == slot_pos[None, :])
    pos_rows = tables[16:16 + PATCHES]
    time_rows = tables[16 + PATCHES:][time_index]
    offsets = tables[0] + pos_rows[None, :, :] + time_rows[:, None, :]
    stream = low_back(matmul(pix_rows, shared[0])) + offsets.reshape(FRAMES * PATCHES, D)
    for temporal, tile_base, row_base in ((True, 1, 1), (False, 5, 6)):
        normed_b = low(layer_norm(stream, tables[row_base], tables[row_base + 1]))
        stream = stream + attention(normed_b, shared[tile_base:tile_base + 4], tables[row_base + 2:row_base + 5], temporal, allowed)
    normed_b = low(layer_norm(stream, tables[11], tables[12]))
    summed = jnp.zeros_like(stream)
    for member in range(N_MLP):
        hidden_in = low_back(normed_b)
        upper = low_back(matmul(hidden_in, ups[member]))
        active = low(jax.nn.gelu(upper))
        summed = summed + low(low_back(matmul(active, downs[member])))
    stream = stream + summed + tables[13]
    final = layer_norm(stream, tables[14], tables[15]).reshape(FRAMES, PATCHES, D)
    frame_weight = jnp.where(frame_live, 1.0 / (length * PATCHES).astype(jnp.float32), 0.0)
    pooled = lax.optimization_barrier(jnp.sum(final * frame_weight[:, None, None], axis=(0, 1)))
    logits = low_back(matmul(low(pooled)[None, :], head_b))[0]
    return jnp.sum(valid * (jax.nn.softplus(logits) - target * logits))

def reference(pixels, lengths, frame_mask, time_index, label_valid, targets, owners, slot_weight, slot_moment1, slot_moment2, tables, table_moment1, table_moment2, head_weight, head_moment1, head_moment2):
    per_tile = D // BR
    shared_blocks = 9 * per_tile
    slot_index = (owners * SLOT + block_ranks(owners)).astype(jnp.int32)
    blocks = slot_weight.reshape(DEVICES * SLOT, BR, D)[slot_index]
    shared = blocks[:shared_blocks].reshape(9, D, D)
    paired = blocks[shared_blocks:].reshape(N_MLP, 2, D, D)
    params = (shared, paired[:, 0], paired[:, 1], tables, head_weight)
    valid_f = label_valid.astype(jnp.float32)
    label_total = jnp.sum(valid_f)
    scale_back = 1.0 / jnp.maximum(label_total, 1.0)

    def one_clip(carry, items):
        grads, loss_total = carry
        clip_pixels, length, clip_mask, clip_time, valid, target = items
        value, pullback = jax.vjp(lambda param_set: clip_loss(param_set, clip_pixels.astype(jnp.float32), length, clip_mask, clip_time, valid, target), params)
        grad_new = pullback(scale_back)[0]
        return ((jax.tree.map(jnp.add, grads, grad_new), loss_total + value), None)
    zeros_init = jax.tree.map(jnp.zeros_like, params)
    (grads, loss_sum), unused = lax.scan(one_clip, (zeros_init, jnp.float32(0.0)), (pixels, lengths, frame_mask, time_index, valid_f, targets))
    grad_shared, grad_up, grad_down, grad_tables, grad_head = grads
    block_grads = jnp.concatenate([grad_shared.reshape(-1, BR, D), jnp.stack([grad_up, grad_down], axis=1).reshape(-1, BR, D)])
    slot_grads = jnp.zeros((DEVICES * SLOT, BR, D), jnp.float32).at[slot_index].set(block_grads).reshape(DEVICES * SLOT * BR, D)
    squares = jnp.sum(slot_grads * slot_grads) + jnp.sum(grad_tables * grad_tables) + jnp.sum(grad_head * grad_head)
    grad_norm = jnp.sqrt(squares)
    factor = jnp.minimum(1.0, clip_max / (grad_norm + 1e-06))
    new_slots = adamw(slot_weight, slot_grads * factor, slot_moment1, slot_moment2, decay_rate, learn_rate)
    new_tabs = adamw(tables, grad_tables * factor, table_moment1, table_moment2, 0.0, table_rate)
    new_heads = adamw(head_weight, grad_head * factor, head_moment1, head_moment2, decay_rate, learn_rate)
    return (loss_sum, label_total, grad_norm, new_slots[0], new_slots[1], new_slots[2], new_tabs[0], new_tabs[1], new_tabs[2], new_heads[0], new_heads[1], new_heads[2])
```

```python
from functools import partial

import jax
import jax.numpy as jnp
from jax import lax
from jax.experimental import pallas as pl
from jax.experimental.pallas import tpu as pltpu
from jax.sharding import PartitionSpec as P

HEADS = 12
HEAD_DIM = 64
TROWS = 8
BR = 48
STEP = 10
GROUP = 16
PAIR = 2 * HEAD_DIM
GROUPS_AT_ONCE = 2
FRAMES_AT_ONCE = 2
VMEM_BYTES = 58 * 2**20

ln_eps = 1e-06
beta_one = 0.9
beta_two = 0.999
learn_rate = 0.05
table_rate = 0.4
decay_rate = 0.05
adam_eps = 1e-08
clip_max = 0.001
highest = lax.Precision.HIGHEST
f32 = jnp.float32
bf16 = jnp.bfloat16
gelu_a = 0.7978845608028654
gelu_b = 0.044715
masked = -1e30


def mm(left, right):
    return jnp.dot(left, right, preferred_element_type=f32)


def mm_nt(left, right):
    return lax.dot_general(left, right, (((1,), (1,)), ((), ())), preferred_element_type=f32)


def mm_tn(left, right):
    return lax.dot_general(left, right, (((0,), (0,)), ((), ())), preferred_element_type=f32)


def normed(values):
    centred = values - jnp.mean(values, axis=-1, keepdims=True)
    rstd = lax.rsqrt(jnp.mean(centred * centred, axis=-1, keepdims=True) + ln_eps)
    return centred * rstd, rstd


def norm_back(grad, xhat, rstd, gain):
    scaled = grad * gain
    return rstd * (
        scaled
        - jnp.mean(scaled, axis=-1, keepdims=True)
        - xhat * jnp.mean(scaled * xhat, axis=-1, keepdims=True)
    )


def fold(values):
    return jnp.sum(values.reshape(-1, 8, values.shape[-1]), axis=0)


def low_lanes():
    lane = lax.broadcasted_iota(jnp.int32, (1, PAIR), 1)
    low = jnp.where(lane < HEAD_DIM, 1.0, 0.0)
    return low.astype(bf16), (1.0 - low).astype(bf16)


def pick_half(stacked):
    rows = stacked.shape[0] // 2
    lane = lax.broadcasted_iota(jnp.int32, (rows, PAIR), 1)
    return jnp.where(lane < HEAD_DIM, stacked[:rows], stacked[rows:])


def fetch(slots_ref, source, target, sem, first, across):
    width = source.shape[2]
    per_tile = width // BR

    def one(i, carry):
        tile, row = i // per_tile, pl.multiple_of((i % per_tile) * BR, 16)
        place = pl.ds(row, BR)
        if across:
            into = target.at[place, pl.ds(pl.multiple_of(tile * width, width), width)]
        else:
            into = target.at[pl.ds(pl.multiple_of(tile * width, 16) + row, BR)]
        block = first(tile) * per_tile + i % per_tile
        pltpu.make_async_copy(source.at[slots_ref[block]], into, sem).start()
        return carry

    count = target.shape[0] * target.shape[1] // (width * width)
    lax.fori_loop(0, count * per_tile, one, 0)


def arrive(target, sem):
    pltpu.make_async_copy(target, target, sem).wait()


def attend(load, store, extra_q, extra_k):
    low, high = low_lanes()
    for pair in range(HEADS // 2):
        lanes = slice(pair * PAIR, (pair + 1) * PAIR)
        queries, keys, values = load(lanes)
        both = jnp.concatenate([queries * low, queries * high], axis=0)
        scores = mm_nt(
            jnp.concatenate([both, extra_q[...]], axis=1),
            jnp.concatenate([keys, extra_k[: keys.shape[0]]], axis=1),
        )
        top = jnp.max(scores, axis=-1, keepdims=True)
        weights = jnp.exp(scores - top).astype(bf16)
        summed = mm(weights, jnp.concatenate([values, jnp.ones_like(values)], axis=1))
        merged = pick_half(summed[:, :PAIR]) / pick_half(summed[:, PAIR:])
        store(lanes, merged.astype(bf16))


def attend_back(load, store, extra_q, extra_k):
    low, high = low_lanes()
    for pair in range(HEADS // 2):
        lanes = slice(pair * PAIR, (pair + 1) * PAIR)
        queries, keys, values, grads = load(lanes)
        rows = queries.shape[0]
        both_k = jnp.concatenate([keys * low, keys * high], axis=0)
        both_v = jnp.concatenate([values * low, values * high], axis=0)
        scores = mm_nt(
            jnp.concatenate([both_k, extra_k[...]], axis=1),
            jnp.concatenate([queries, extra_q[:rows]], axis=1),
        )
        back = mm_nt(both_v, grads)
        soft, inner = [], []
        for half in (slice(0, rows), slice(rows, 2 * rows)):
            part = scores[half]
            weights = jnp.exp(part - jnp.max(part, axis=0, keepdims=True))
            weights = weights * (1.0 / jnp.sum(weights, axis=0, keepdims=True))
            delta = back[half] - jnp.sum(weights * back[half], axis=0, keepdims=True)
            soft.append(weights.astype(bf16))
            inner.append((weights * delta).astype(bf16))
        soft = jnp.concatenate(soft, axis=0)
        inner = jnp.concatenate(inner, axis=0)
        store(
            lanes,
            (mm_tn(inner, both_k) * HEAD_DIM ** (-0.5)).astype(bf16),
            pick_half(mm(inner, queries)).astype(bf16),
            pick_half(mm(soft, grads)).astype(bf16),
        )


def project(hidden, rows, tiles):
    width = hidden.shape[1]
    joint = mm(hidden, tiles[...])
    queries = (joint[:, :width] + rows[2:3]).astype(bf16) * jnp.asarray(HEAD_DIM ** (-0.5), bf16)
    keys = joint[:, width : 2 * width].astype(bf16)
    values = (joint[:, 2 * width :] + rows[3:4]).astype(bf16)
    return queries, keys, values


def keep_norm(stream, rows, at, hid_ref, hat_ref, rstd_ref, here, cut):
    xhat, rstd = normed(stream)
    hat_ref[here] = xhat.astype(bf16).reshape(cut)
    rstd_ref[here] = jnp.broadcast_to(rstd, (rstd.shape[0], 128)).reshape(cut[:-1] + (128,))
    hidden = (xhat * rows[at : at + 1] + rows[at + 1 : at + 2]).astype(bf16)
    if hid_ref is not None:
        hid_ref[here] = hidden.reshape(cut)
    return xhat, hidden


def by_groups(block, total, work):
    step = pl.program_id(0)
    full, rest = total // block, total % block
    if rest == 0:
        work(block)
    else:
        pl.when(step < full)(lambda: work(block))
        pl.when(step == full)(lambda: work(rest))


def time_forward(
    total, slots, gathered, pixels, pos, trow, rows, extra_q, extra_k,
    x1_ref, hid_ref, hat_ref, rstd_ref, q_ref, k_ref, v_ref, o_ref,
    embed, joint, out, base, sems,
):
    frames, span, width = x1_ref.shape

    @pl.when(pl.program_id(0) == 0)
    def _():
        fetch(slots, gathered, embed, sems.at[0], lambda t: t, False)
        fetch(slots, gathered, joint, sems.at[1], lambda t: t + 1, True)
        fetch(slots, gathered, out, sems.at[2], lambda t: t + 4, False)
        arrive(embed, sems.at[0])
        arrive(joint, sems.at[1])
        arrive(out, sems.at[2])

    def work(count):
        cut = (frames, count * GROUP, width)
        flat = (frames * count * GROUP, width)
        here = slice(0, count * GROUP)
        every = (slice(None), here)
        offset = (pos[here][None] + trow[...][:, None]).reshape(flat)
        stream = mm(pixels[:, here].reshape(flat), embed[...]) + offset
        base[: flat[0]] = stream
        rows_now = rows[...]
        unused, hidden = keep_norm(stream, rows_now, 0, hid_ref, hat_ref, rstd_ref, every, cut)
        queries, keys, values = project(hidden, rows_now, joint)
        q_ref[:, here] = queries.reshape(cut)
        k_ref[:, here] = keys.reshape(cut)
        v_ref[:, here] = values.reshape(cut)
        for g in range(count):
            part = slice(g * GROUP, (g + 1) * GROUP)

            def load(lanes):
                return tuple(
                    ref[:, part, lanes].reshape(frames * GROUP, PAIR)
                    for ref in (q_ref, k_ref, v_ref)
                )

            def store(lanes, merged):
                o_ref[:, part, lanes] = merged.reshape(frames, GROUP, PAIR)

            attend(load, store, extra_q, extra_k)
        merged = o_ref[:, here].reshape(flat)
        stream = base[: flat[0]] + mm(merged, out[...]) + rows_now[4:5]
        x1_ref[:, here] = stream.reshape(cut)

    by_groups(span // GROUP, total, work)


def space_forward(
    slots, frame_weight, member, patches, gathered, x1, rows, low_rows, extra_q, extra_k,
    hid1_ref, hat1_ref, rstd1_ref, q_ref, k_ref, v_ref, o_ref,
    hid2_ref, hat2_ref, rstd2_ref, hat3_ref, rstd3_ref, gp_ref, act_ref, pool_ref,
    joint, out, ups, downs, acts, sems,
):
    step = pl.program_id(0)
    members = gp_ref.shape[0]
    cut = x1.shape
    span, count, width = cut
    flat = (span * count, width)
    every = (slice(None),)

    @pl.when(step == 0)
    def _():
        fetch(slots, gathered, joint, sems.at[0], lambda t: t + 5, True)
        fetch(slots, gathered, out, sems.at[1], lambda t: t + 8, False)
        fetch(slots, gathered, ups, sems.at[2], lambda t: 2 * t + 9, True)
        fetch(slots, gathered, downs, sems.at[3], lambda t: 2 * t + 10, False)
        pool_ref[...] = jnp.zeros_like(pool_ref)
        arrive(joint, sems.at[0])
        arrive(out, sems.at[1])

    rows_now = rows[...]
    unused, hidden = keep_norm(
        x1[...].reshape(flat), rows_now, 0, hid1_ref, hat1_ref, rstd1_ref, every, cut
    )
    queries, keys, values = project(hidden, rows_now, joint)
    q_ref[...] = queries.reshape(cut)
    k_ref[...] = keys.reshape(cut)
    v_ref[...] = values.reshape(cut)
    for f in range(span):

        def load(lanes):
            return q_ref[f, :, lanes], k_ref[f, :, lanes], v_ref[f, :, lanes]

        def store(lanes, merged):
            o_ref[f, :, lanes] = merged

        attend(load, store, extra_q, extra_k)
    merged = o_ref[...].reshape(flat)
    stream = x1[...].reshape(flat) + mm(merged, out[...]) + rows_now[4:5]
    low_now = low_rows[...]
    unused, hidden = keep_norm(stream, low_now, 0, hid2_ref, hat2_ref, rstd2_ref, every, cut)

    @pl.when(step == 0)
    def _():
        arrive(ups, sems.at[2])
        arrive(downs, sems.at[3])

    for j in range(members):
        lanes = slice(j * width, (j + 1) * width)
        upper = mm(hidden, ups[:, lanes])
        cubic = gelu_a * gelu_b * (upper * upper)
        gate = 0.5 + 0.5 * jnp.tanh(upper * (gelu_a + cubic))
        active = upper * gate
        slope = gate + active * (1.0 - gate) * (2.0 * gelu_a + 6.0 * cubic)
        gp_ref[j] = slope.astype(bf16).reshape(cut)
        acts[:, lanes] = active.astype(bf16)
        stream = stream + mm(acts[:, lanes], downs[lanes])
    own = pl.ds(pl.multiple_of(member[0] * width, 128), width)
    act_ref[...] = acts[:, own].reshape(cut)
    stream = stream + low_now[2:3]
    xhat, rstd = normed(stream)
    hat3_ref[...] = xhat.astype(bf16).reshape(cut)
    rstd3_ref[...] = jnp.broadcast_to(rstd, (flat[0], 128)).reshape(span, count, 128)
    final = xhat * low_now[3:4] + low_now[4:5]
    row = lax.broadcasted_iota(jnp.int32, (count, 1), 0)
    for f in range(span):
        part = jnp.where(row < patches, final[f * count : (f + 1) * count], 0.0)
        pool_ref[...] += fold(part) * frame_weight[step * span + f]


def mlp_backward(
    slots, frame_weight, member, patches, gathered, pool, head, valid, targets, total,
    hid2, hat2, rstd2, hat3, rstd3, gp, act, low_rows,
    dx2_ref, up_ref, down_ref, rows_ref, small_ref,
    ups, downs, dus, spread, up_sum, down_sum, row_sums, sems,
):
    step = pl.program_id(0)
    members = gp.shape[0]
    cut = hid2.shape
    span, count, width = cut
    flat = (span * count, width)

    @pl.when(step == 0)
    def _():
        fetch(slots, gathered, downs, sems.at[1], lambda t: 2 * t + 10, False)
        fetch(slots, gathered, ups, sems.at[0], lambda t: 2 * t + 9, True)
        pooled = jnp.sum(pool[...], axis=0, keepdims=True).astype(bf16)
        pooled8 = jnp.broadcast_to(pooled, (8, width))
        logits = mm(pooled8, head[...])
        valid_f = valid[...]
        target = targets[...]
        soft = jnp.maximum(logits, 0.0) + jnp.log(1.0 + jnp.exp(-jnp.abs(logits)))
        loss = jnp.sum(valid_f * (soft - target * logits), axis=1, keepdims=True)
        sig = 1.0 / (1.0 + jnp.exp(-logits))
        grad = (valid_f * (sig - target) / jnp.maximum(total[0], 1.0)).astype(bf16)
        spread[...] = mm_nt(grad, head[...])
        small_ref[...] = jnp.zeros_like(small_ref)
        small_ref[0:1, :] = pooled.astype(f32)
        small_ref[1:2, 0 : grad.shape[1]] = grad[0:1].astype(f32)
        small_ref[2:3, 0:128] = jnp.broadcast_to(loss[0:1], (1, 128))
        up_sum[...] = jnp.zeros_like(up_sum)
        down_sum[...] = jnp.zeros_like(down_sum)
        row_sums[...] = jnp.zeros_like(row_sums)
        arrive(downs, sems.at[1])

    low_now = low_rows[...]
    row = lax.broadcasted_iota(jnp.int32, (count, 1), 0)
    weight = jnp.concatenate(
        [jnp.where(row < patches, frame_weight[step * span + f], 0.0) for f in range(span)]
    )
    grad_final = spread[0:1] * weight
    xhat = hat3[...].reshape(flat).astype(f32)
    rstd = rstd3[...].reshape(flat[0], 128)[:, 0:1]
    row_sums[3] += fold(grad_final * xhat)
    row_sums[4] += fold(grad_final)
    grad_top = norm_back(grad_final, xhat, rstd, low_now[3:4])
    row_sums[2] += fold(grad_top)
    grad_b = grad_top.astype(bf16)

    for j in range(members):
        lanes = slice(j * width, (j + 1) * width)
        du = mm_nt(grad_b, downs[lanes]) * gp[j].reshape(flat).astype(f32)
        dus[:, lanes] = du.astype(bf16)

    @pl.when(step == 0)
    def _():
        arrive(ups, sems.at[0])

    grad_hidden = mm_nt(dus[...], ups[...])
    own = pl.ds(pl.multiple_of(member[0] * width, 128), width)
    up_sum[...] += mm_tn(hid2[...].reshape(flat), dus[:, own])
    down_sum[...] += mm_tn(act[...].reshape(flat), grad_b)
    xhat = hat2[...].reshape(flat).astype(f32)
    rstd = rstd2[...].reshape(flat[0], 128)[:, 0:1]
    row_sums[0] += fold(grad_hidden * xhat)
    row_sums[1] += fold(grad_hidden)
    dx2_ref[...] = (grad_top + norm_back(grad_hidden, xhat, rstd, low_now[0:1])).reshape(cut)

    @pl.when(step == pl.num_programs(0) - 1)
    def _():
        up_ref[...] = up_sum[...].astype(bf16)
        down_ref[...] = down_sum[...].astype(bf16)
        rows_ref[...] = jnp.zeros_like(rows_ref)
        for i in range(5):
            rows_ref[i : i + 1] = jnp.sum(row_sums[i], axis=0, keepdims=True)


def close_attention(
    grad_stream, grad_b, hidden, xhat, rstd, grads, merged, rows_now, picked, ones, joint,
    joint_sum, out_sum, row_sums,
):
    grad_hidden = mm_nt(grads, joint[...])
    hidden_t = mm_nt(picked, hidden).astype(bf16) + ones
    merged_t = mm_nt(picked, merged).astype(bf16) + ones
    joint_sum[...] += mm(hidden_t, grads)
    out_sum[...] += mm(merged_t, grad_b)
    xhat = xhat.astype(f32)
    row_sums[0] += fold(grad_hidden * xhat)
    row_sums[1] += fold(grad_hidden)
    return grad_stream + norm_back(grad_hidden, xhat, rstd[:, 0:1], rows_now[0:1])


def ones_row(picked):
    row = lax.broadcasted_iota(jnp.int32, (picked.shape[0], 1), 0)
    return jnp.where(row == picked.shape[0] - 16, 1.0, 0.0).astype(bf16)


def clear(*refs):
    for ref in refs:
        ref[...] = jnp.zeros_like(ref)


def finish_attention(tile_ref, at, rows_ref, joint_sum, out_sum, row_sums):
    share = tile_ref.shape[1]
    width = tile_ref.shape[2]
    rows_ref[...] = jnp.zeros_like(rows_ref)
    for i in range(3):
        tile_ref[at + i] = joint_sum[:share, i * width : (i + 1) * width].astype(bf16)
    tile_ref[at + 3] = out_sum[:share].astype(bf16)
    for i in range(2):
        rows_ref[i : i + 1] = jnp.sum(row_sums[i], axis=0, keepdims=True)
    rows_ref[2:3] = joint_sum[share : share + 1, :width]
    rows_ref[3:4] = joint_sum[share : share + 1, 2 * width :]
    rows_ref[4:5] = out_sum[share : share + 1]


def space_backward(
    slots, gathered, dx2, hid1, hat1, rstd1, q, k, v, o, rows, picked, extra_q, extra_k,
    dx1_ref, tile_ref, rows_ref, joint, out, joint_sum, out_sum, row_sums, grads, outer, sems,
):
    step = pl.program_id(0)
    cut = hid1.shape
    span, count, width = cut
    flat = (span * count, width)

    @pl.when(step == 0)
    def _():
        fetch(slots, gathered, out, sems.at[1], lambda t: t + 8, False)
        fetch(slots, gathered, joint, sems.at[0], lambda t: t + 5, True)
        clear(joint_sum, out_sum, row_sums)
        arrive(out, sems.at[1])
        arrive(joint, sems.at[0])

    grad_b = dx2[...].reshape(flat).astype(bf16)
    outer[...] = mm_nt(grad_b, out[...]).astype(bf16)
    for f in range(span):
        here = slice(f * count, (f + 1) * count)

        def load(lanes):
            return q[f, :, lanes], k[f, :, lanes], v[f, :, lanes], outer[here, lanes]

        def store(lanes, *parts):
            for i, part in enumerate(parts):
                grads[here, i * width + lanes.start : i * width + lanes.stop] = part

        attend_back(load, store, extra_q, extra_k)
    picked_now = picked[...]
    dx1_ref[...] = close_attention(
        dx2[...].reshape(flat), grad_b, hid1[...].reshape(flat), hat1[...].reshape(flat),
        rstd1[...].reshape(flat[0], 128), grads[...], o[...].reshape(flat), rows[...],
        picked_now, ones_row(picked_now), joint, joint_sum, out_sum, row_sums,
    ).reshape(cut)

    @pl.when(step == pl.num_programs(0) - 1)
    def _():
        finish_attention(tile_ref, 0, rows_ref, joint_sum, out_sum, row_sums)


def time_backward(
    total, slots, gathered, dx1, hid0, hat0, rstd0, q, k, v, o, pixels, rows, picked,
    extra_q, extra_k,
    tile_ref, rows_ref, pos_ref, frame_ref,
    joint, out, joint_sum, out_sum, embed_sum, row_sums, grads, outer, sems,
):
    step = pl.program_id(0)
    frames, span, width = hid0.shape

    @pl.when(step == 0)
    def _():
        fetch(slots, gathered, out, sems.at[1], lambda t: t + 4, False)
        fetch(slots, gathered, joint, sems.at[0], lambda t: t + 1, True)
        clear(joint_sum, out_sum, embed_sum, row_sums, frame_ref)
        arrive(out, sems.at[1])
        arrive(joint, sems.at[0])

    def work(groups):
        cut = (frames, groups * GROUP, width)
        flat = (frames * groups * GROUP, width)
        small = (frames, GROUP, PAIR)
        here = slice(0, groups * GROUP)
        grad_b = dx1[:, here].reshape(flat).astype(bf16)
        outer[:, here] = mm_nt(grad_b, out[...]).astype(bf16).reshape(cut)
        for g in range(groups):
            part = slice(g * GROUP, (g + 1) * GROUP)

            def load(lanes):
                return tuple(
                    ref[:, part, lanes].reshape(frames * GROUP, PAIR)
                    for ref in (q, k, v, outer)
                )

            def store(lanes, *parts):
                for i, value in enumerate(parts):
                    span_now = slice(i * width + lanes.start, i * width + lanes.stop)
                    grads[:, part, span_now] = value.reshape(small)

            attend_back(load, store, extra_q, extra_k)
        picked_now = picked[...]
        grad = close_attention(
            dx1[:, here].reshape(flat), grad_b, hid0[:, here].reshape(flat),
            hat0[:, here].reshape(flat), rstd0[:, here].reshape(flat[0], 128),
            grads[:, here].reshape(flat[0], 3 * width), o[:, here].reshape(flat), rows[...],
            picked_now, ones_row(picked_now), joint, joint_sum, out_sum, row_sums,
        )
        pix_t = mm_nt(picked_now, pixels[:, here].reshape(flat)).astype(bf16)
        embed_sum[...] += mm(pix_t, grad.astype(bf16))
        cube = grad.reshape(cut)
        pos_ref[here] = jnp.sum(cube, axis=0)
        frame_ref[...] += jnp.sum(cube, axis=1)

    by_groups(span // GROUP, total, work)

    @pl.when(step == pl.num_programs(0) - 1)
    def _():
        finish_attention(tile_ref, 1, rows_ref, joint_sum, out_sum, row_sums)
        tile_ref[0] = embed_sum[: tile_ref.shape[1]].astype(bf16)


def pack(dests, core, *refs):
    sources, table_ref, keep_ref, send_ref, sems = refs[:-4], refs[-4], refs[-3], refs[-2], refs[-1]
    slots = (keep_ref.shape[1] - table_ref.shape[1]) // BR

    def route(source, chunk, place, sem):
        mine = chunk % 2 == core[0]

        @pl.when(mine)
        def _():
            pltpu.make_async_copy(source, keep_ref.at[chunk // 2, place], sem).start()

        @pl.when(jnp.logical_not(mine))
        def _():
            pltpu.make_async_copy(source, send_ref.at[chunk // 2, place], sem).start()

    first = 0
    for n, source in enumerate(sources):

        def one(i, carry, source=source, first=first, n=n):
            dest = dests[first + i]
            row = pl.multiple_of((dest % slots) * BR, 16)
            route(source.at[i], dest // slots, pl.ds(row, BR), sems.at[n])
            return carry

        lax.fori_loop(0, source.shape[0], one, 0)
        first += source.shape[0]

    def one_table(i, carry):
        place = pl.ds(slots * BR, table_ref.shape[1])
        route(table_ref.at[i], i, place, sems.at[len(sources)])
        return carry

    lax.fori_loop(0, table_ref.shape[0], one_table, 0)
    for n, source in enumerate(sources + (table_ref,)):
        pltpu.make_async_copy(source, source, sems.at[n]).wait()


def swap(value, axis, hop):
    size = lax.axis_size(axis)
    return lax.ppermute(value, axis, [(i, i ^ hop) for i in range(size)])


def halve(kept, sent, axis):
    size = lax.axis_size(axis)
    place = lax.axis_index(axis)
    bits = size.bit_length() - 1
    rows, width = kept.shape[1:]
    middle = (width // 256) * 128
    met = swap(sent, axis, 1)
    cut = (2,) * (bits - 1) + (rows, width)
    kept, met = kept.reshape(cut), met.reshape(cut)
    ascending = list(range(1, bits))
    parts = [
        [kept[..., :middle], met[..., :middle], ascending],
        [kept[..., middle:], met[..., middle:], ascending[::-1]],
    ]
    parts = [(left.astype(f32) + right.astype(f32), order) for left, right, order in parts]
    for stage in range(bits - 1):
        outgoing, staying = [], []
        for value, order in parts:
            alive = sorted(order[stage:], reverse=True)
            at = alive.index(order[stage])
            bit = (place >> order[stage]) & 1
            outgoing.append(lax.dynamic_index_in_dim(value, 1 - bit, at, False).astype(bf16))
            staying.append(lax.dynamic_index_in_dim(value, bit, at, False))
        arrived = [
            swap(value, axis, 1 << order[stage]) for value, (unused, order) in zip(outgoing, parts)
        ]
        parts = [
            (stay + come.astype(f32), order)
            for stay, come, (unused, order) in zip(staying, arrived, parts)
        ]
    return jnp.concatenate([parts[0][0], parts[1][0]], axis=-1)


def block_ranks(owners):
    total_blocks = owners.shape[0]
    same_owner = owners[:, None] == owners[None, :]
    earlier = jnp.arange(total_blocks)[None, :] < jnp.arange(total_blocks)[:, None]
    return jnp.sum((same_owner & earlier).astype(jnp.int32), axis=1)


def adamw(weight, gradient, moment_one, moment_two, weight_decay, rate):
    first_new = beta_one * moment_one + (1.0 - beta_one) * gradient
    second_new = beta_two * moment_two + (1.0 - beta_two) * gradient * gradient
    mean_hat = first_new / (1.0 - beta_one**STEP)
    var_hat = second_new / (1.0 - beta_two**STEP)
    updated = weight - rate * (mean_hat / (jnp.sqrt(var_hat) + adam_eps) + weight_decay * weight)
    return (updated, first_new, second_new)


def local(
    pixels,
    lengths,
    frame_mask,
    time_index,
    label_valid,
    targets,
    owners,
    slot_weight,
    slot_moment1,
    slot_moment2,
    tables,
    table_moment1,
    table_moment2,
    head_weight,
    head_moment1,
    head_moment2,
):
    dp_count = lax.axis_size("dp")
    mlp_count = lax.axis_size("mlp")
    member = lax.axis_index("mlp").astype(jnp.int32)
    width = slot_weight.shape[1]
    per_tile = width // BR
    slots = slot_weight.shape[0] // BR
    shared_blocks = 9 * per_tile
    frames, patches = pixels.shape[1], pixels.shape[2]
    padded = -(-patches // GROUP) * GROUP
    groups = padded // GROUP
    classes = head_weight.shape[1]
    class_pad = -(-classes // 128) * 128
    params = pltpu.CompilerParams(vmem_limit_bytes=VMEM_BYTES)
    any_spec = pl.BlockSpec(memory_space=pl.ANY)

    gathered = lax.all_gather(slot_weight.astype(bf16), ("dp", "mlp"), axis=0, tiled=True)
    gathered = gathered.reshape(-1, BR, width)
    slot_index = (owners * slots + block_ranks(owners)).astype(jnp.int32)

    pix = jnp.pad(pixels[0], ((0, 0), (0, padded - patches), (0, 0)))
    slot_pos = jnp.arange(frames)
    frame_live = slot_pos < lengths[0]
    key_ok = frame_live & (frame_mask[0] == 1)
    allowed = key_ok[None, :] | (slot_pos[:, None] == slot_pos[None, :])
    extra_lane = jnp.arange(HEAD_DIM)
    flat_id = jnp.arange(frames * GROUP)
    frame_id, patch_id = flat_id // GROUP, flat_id % GROUP
    lane_frame = jnp.clip(extra_lane - GROUP, 0, frames - 1)
    in_patch = (extra_lane < GROUP)[None, :]
    in_frame = ((extra_lane >= GROUP) & (extra_lane < GROUP + frames))[None, :]
    same_patch = patch_id[:, None] == extra_lane[None, :]
    same_frame = frame_id[:, None] == lane_frame[None, :]
    time_q = (in_patch & same_patch) | (in_frame & same_frame)
    time_k = (in_patch & ~same_patch) | (in_frame & ~allowed.T[frame_id][:, lane_frame])
    is_pad = (jnp.arange(padded) >= patches)[:, None]
    space_q = jnp.broadcast_to(extra_lane[None, :] == 0, (padded, HEAD_DIM))
    space_k = is_pad & (extra_lane[None, :] == 0)

    def widen(flags, value):
        block = jnp.where(flags, value, 0.0).astype(bf16)
        block = jnp.pad(block, ((0, 0), (0, PAIR - HEAD_DIM)))
        return jnp.concatenate([block, block])

    time_q, time_k = widen(time_q, 1.0), widen(time_k, masked)
    space_q, space_k = widen(space_q, 1.0), widen(space_k, masked)
    time_hot = (time_index[0][:, None] == jnp.arange(TROWS)[None, :]).astype(f32)
    trow = jnp.einsum("ft,td->fd", time_hot, tables[16 + patches :], precision=highest)
    pos = jnp.pad(tables[16 : 16 + patches] + tables[0], ((0, padded - patches), (0, 0)))
    frame_weight = jnp.where(
        frame_live, 1.0 / (lengths[0] * patches).astype(f32), 0.0
    ).astype(f32)
    valid_f = label_valid.astype(f32)
    label_total = lax.psum(jnp.sum(valid_f), "dp")
    share = width // mlp_count
    pick_row = jnp.arange(share)
    pick_feature = (pick_row // BR) * (BR * mlp_count) + member * BR + pick_row % BR
    picked = (pick_feature[:, None] == jnp.arange(width)[None, :]).astype(bf16)
    picked = jnp.pad(picked, ((0, 16), (0, 0)))
    member_s = member[None]
    time_rows = jnp.pad(tables[1:6], ((0, 3), (0, 0)))
    space_rows = jnp.pad(tables[6:11], ((0, 3), (0, 0)))
    low_rows = jnp.pad(tables[11:16], ((0, 3), (0, 0)))

    cube32 = jax.ShapeDtypeStruct((frames, padded, width), f32)
    cube16 = jax.ShapeDtypeStruct((frames, padded, width), bf16)
    thin32 = jax.ShapeDtypeStruct((frames, padded, 128), f32)
    row32 = jax.ShapeDtypeStruct((8, width), f32)
    group_rows = GROUPS_AT_ONCE * GROUP
    frame_rows = FRAMES_AT_ONCE * padded
    group_spec = pl.BlockSpec((frames, group_rows, width), lambda g, *_: (0, g, 0))
    group_thin = pl.BlockSpec((frames, group_rows, 128), lambda g, *_: (0, g, 0))
    patch_spec = pl.BlockSpec((group_rows, width), lambda g, *_: (g, 0))
    frame_spec = pl.BlockSpec((FRAMES_AT_ONCE, padded, width), lambda f, *_: (f, 0, 0))
    frame_thin = pl.BlockSpec((FRAMES_AT_ONCE, padded, 128), lambda f, *_: (f, 0, 0))
    gp_spec = pl.BlockSpec(
        (mlp_count, FRAMES_AT_ONCE, padded, width), lambda f, *_: (0, f, 0, 0)
    )
    time_grid = (-(-groups // GROUPS_AT_ONCE),)
    space_grid = (frames // FRAMES_AT_ONCE,)

    def whole(*shape):
        return pl.BlockSpec(shape, lambda i, *_: (0,) * len(shape))

    rows_spec = whole(8, width)
    time_extra = whole(2 * frames * GROUP, PAIR)
    space_extra = whole(2 * padded, PAIR)
    pick_spec = whole(share + 16, width)

    def call(kernel, name, scalars, grid, ins, in_specs, outs, out_specs, scratch):
        return pl.pallas_call(
            kernel,
            grid_spec=pltpu.PrefetchScalarGridSpec(
                num_scalar_prefetch=len(scalars),
                grid=grid,
                in_specs=[any_spec] + in_specs,
                out_specs=out_specs,
                scratch_shapes=scratch,
            ),
            out_shape=outs,
            compiler_params=params,
            name=name,
        )(*scalars, gathered, *ins)

    def tile_bufs(*shapes):
        return [pltpu.VMEM((rows * width, cols * width), bf16) for rows, cols in shapes]

    x1, hid0, hat0, rstd0, q_t, k_t, v_t, o_t = call(
        partial(time_forward, groups),
        "time_forward",
        [slot_index],
        time_grid,
        [pix, pos, trow, time_rows, time_q, time_k],
        [group_spec, patch_spec, whole(frames, width), rows_spec, time_extra, time_extra],
        [cube32, cube16, cube16, thin32] + [cube16] * 4,
        [group_spec] * 3 + [group_thin] + [group_spec] * 4,
        tile_bufs((1, 1), (1, 3), (1, 1))
        + [pltpu.VMEM((frames * group_rows, width), f32), pltpu.SemaphoreType.DMA((3,))],
    )
    (hid1, hat1, rstd1, q_s, k_s, v_s, o_s, hid2, hat2, rstd2, hat3, rstd3, gp, act, pool) = call(
        lambda s, fw, m, *refs: space_forward(s, fw, m, patches, *refs),
        "space_forward",
        [slot_index, frame_weight, member_s],
        space_grid,
        [x1, space_rows, low_rows, space_q, space_k],
        [frame_spec, rows_spec, rows_spec, space_extra, space_extra],
        [cube16, cube16, thin32]
        + [cube16] * 4
        + [cube16, cube16, thin32, cube16, thin32]
        + [jax.ShapeDtypeStruct((mlp_count, frames, padded, width), bf16), cube16, row32],
        [frame_spec, frame_spec, frame_thin]
        + [frame_spec] * 4
        + [frame_spec, frame_spec, frame_thin, frame_spec, frame_thin]
        + [gp_spec, frame_spec, rows_spec],
        tile_bufs((1, 3), (1, 1), (1, mlp_count), (mlp_count, 1))
        + [pltpu.VMEM((frame_rows, mlp_count * width), bf16), pltpu.SemaphoreType.DMA((4,))],
    )

    head_b = jnp.pad(head_weight.astype(bf16), ((0, 0), (0, class_pad - classes)))
    valid_p = jnp.pad(valid_f, ((0, 0), (0, class_pad - classes)))
    targets_p = jnp.pad(targets, ((0, 0), (0, class_pad - classes)))
    square16 = jax.ShapeDtypeStruct((width, width), bf16)
    dx2, grad_up, grad_down, rows_low, small = call(
        lambda s, fw, m, *refs: mlp_backward(s, fw, m, patches, *refs),
        "mlp_backward",
        [slot_index, frame_weight, member_s],
        space_grid,
        [
            pool, head_b, valid_p, targets_p, label_total[None],
            hid2, hat2, rstd2, hat3, rstd3, gp, act, low_rows,
        ],
        [
            rows_spec, whole(width, class_pad), whole(1, class_pad), whole(1, class_pad),
            pl.BlockSpec(memory_space=pltpu.SMEM),
            frame_spec, frame_spec, frame_thin, frame_spec, frame_thin, gp_spec, frame_spec,
            rows_spec,
        ],
        [cube32, square16, square16, row32, row32],
        [frame_spec, whole(width, width), whole(width, width), rows_spec, rows_spec],
        tile_bufs((1, mlp_count), (mlp_count, 1))
        + [
            pltpu.VMEM((frame_rows, mlp_count * width), bf16),
            pltpu.VMEM((8, width), f32),
            pltpu.VMEM((width, width), f32),
            pltpu.VMEM((width, width), f32),
            pltpu.VMEM((5, 8, width), f32),
            pltpu.SemaphoreType.DMA((2,)),
        ],
    )

    sums = [
        pltpu.VMEM((share + 16, 3 * width), f32),
        pltpu.VMEM((share + 16, width), f32),
    ]
    dx1, tiles_space, rows_space = call(
        space_backward,
        "space_backward",
        [slot_index],
        space_grid,
        [dx2, hid1, hat1, rstd1, q_s, k_s, v_s, o_s, space_rows, picked, space_q, space_k],
        [frame_spec] * 3
        + [frame_thin]
        + [frame_spec] * 4
        + [rows_spec, pick_spec, space_extra, space_extra],
        [cube32, jax.ShapeDtypeStruct((4, share, width), bf16), row32],
        [frame_spec, whole(4, share, width), rows_spec],
        tile_bufs((1, 3), (1, 1))
        + sums
        + [
            pltpu.VMEM((2, 8, width), f32),
            pltpu.VMEM((frame_rows, 3 * width), bf16),
            pltpu.VMEM((frame_rows, width), bf16),
            pltpu.SemaphoreType.DMA((2,)),
        ],
    )
    tiles_time, rows_time, grad_pos, grad_frames = call(
        partial(time_backward, groups),
        "time_backward",
        [slot_index],
        time_grid,
        [dx1, hid0, hat0, rstd0, q_t, k_t, v_t, o_t, pix, time_rows, picked, time_q, time_k],
        [group_spec] * 3
        + [group_thin]
        + [group_spec] * 5
        + [rows_spec, pick_spec, time_extra, time_extra],
        [
            jax.ShapeDtypeStruct((5, share, width), bf16),
            row32,
            jax.ShapeDtypeStruct((padded, width), f32),
            jax.ShapeDtypeStruct((frames, width), f32),
        ],
        [whole(5, share, width), rows_spec, patch_spec, whole(frames, width)],
        tile_bufs((1, 3), (1, 1))
        + sums
        + [
            pltpu.VMEM((share + 16, width), f32),
            pltpu.VMEM((2, 8, width), f32),
            pltpu.VMEM((frames, group_rows, 3 * width), bf16),
            pltpu.VMEM((frames, group_rows, width), bf16),
            pltpu.SemaphoreType.DMA((2,)),
        ],
    )

    grad_time = jnp.einsum("ft,fd->td", time_hot, grad_frames, precision=highest)
    table_rows = tables.shape[0]
    table_part = jnp.concatenate(
        [
            jnp.sum(grad_frames, axis=0, keepdims=True),
            rows_time[:5],
            rows_space[:5],
            rows_low[:5],
            grad_pos[:patches],
            grad_time,
        ]
    )
    rows_each = -(-table_rows // (dp_count * mlp_count))
    table_part = jnp.pad(
        table_part, ((0, rows_each * dp_count * mlp_count - table_rows), (0, 0))
    ).reshape(dp_count, mlp_count, rows_each, width)
    table_part = lax.dynamic_index_in_dim(table_part, member, 1, False).astype(bf16)
    table_part = jnp.pad(table_part, ((0, 0), (0, 16 - rows_each), (0, 0)))

    sources = [
        part.reshape(-1, BR, width) for part in (tiles_time, tiles_space, grad_up, grad_down)
    ]
    shared_here = shared_blocks // mlp_count
    here_ids = jnp.arange(shared_here + 2 * per_tile)
    block_of = jnp.where(
        here_ids < shared_here,
        here_ids * mlp_count + member,
        here_ids - shared_here + shared_blocks + member * 2 * per_tile,
    )
    here_slots = slot_index[block_of]
    dests = (here_slots // (slots * mlp_count)) * slots + here_slots % slots
    place = lax.axis_index("dp").astype(jnp.int32)
    chunk = jax.ShapeDtypeStruct((dp_count // 2, slots * BR + 16, width), bf16)
    kept, sent = pl.pallas_call(
        pack,
        grid_spec=pltpu.PrefetchScalarGridSpec(
            num_scalar_prefetch=2,
            grid=(1,),
            in_specs=[pl.BlockSpec(memory_space=pltpu.VMEM)] * 5,
            out_specs=[any_spec] * 2,
            scratch_shapes=[pltpu.SemaphoreType.DMA((5,))],
        ),
        out_shape=[chunk, chunk],
        compiler_params=params,
        name="pack",
    )(dests, (place % 2)[None], *sources, table_part)
    summed = halve(kept, sent, "dp")
    my_slots = (place * mlp_count + member) * slots + jnp.arange(slots)
    filled = jnp.any(slot_index[:, None] == my_slots[None, :], axis=0)
    filled = jnp.repeat(filled, BR)[:, None]
    own_grad = jnp.where(filled, summed[: slots * BR], 0.0)
    squares_own = jnp.sum(own_grad * own_grad)
    block = jnp.concatenate(
        [
            jnp.pad(summed[slots * BR : slots * BR + rows_each], ((0, 7 - rows_each), (0, 0))),
            jnp.broadcast_to(squares_own, (1, width)),
            small,
        ]
    )
    blocks = lax.all_gather(block, "dp", axis=0)
    grad_head = jnp.einsum("cd,ck->dk", blocks[:, 8], blocks[:, 9, :classes], precision=highest)
    loss_sum = jnp.sum(blocks[:, 10, 0])
    blocks = lax.all_gather(blocks[:, :8], "mlp", axis=1)
    grad_tables = blocks[:, :, :rows_each].reshape(-1, width)[:table_rows]
    grad_norm = jnp.sqrt(
        jnp.sum(blocks[:, :, 7, 0])
        + jnp.sum(grad_tables * grad_tables)
        + jnp.sum(grad_head * grad_head)
    )
    factor = jnp.minimum(1.0, clip_max / (grad_norm + 1e-06))
    new_slots = adamw(
        slot_weight, own_grad * factor, slot_moment1, slot_moment2, decay_rate, learn_rate
    )
    new_tabs = adamw(tables, grad_tables * factor, table_moment1, table_moment2, 0.0, table_rate)
    new_heads = adamw(
        head_weight, grad_head * factor, head_moment1, head_moment2, decay_rate, learn_rate
    )
    return (
        loss_sum,
        label_total,
        grad_norm,
        new_slots[0],
        new_slots[1],
        new_slots[2],
        new_tabs[0],
        new_tabs[1],
        new_tabs[2],
        new_heads[0],
        new_heads[1],
        new_heads[2],
    )


def solution(mesh):
    return jax.shard_map(
        local,
        mesh=mesh,
        in_specs=(
            P("dp", None, None, None),
            P("dp"),
            P("dp", None),
            P("dp", None),
            P("dp", None),
            P("dp", None),
            P(),
            P(("dp", "mlp"), None),
            P(("dp", "mlp"), None),
            P(("dp", "mlp"), None),
            P(),
            P(),
            P(),
            P(),
            P(),
            P(),
        ),
        out_specs=(
            P(),
            P(),
            P(),
            P(("dp", "mlp"), None),
            P(("dp", "mlp"), None),
            P(("dp", "mlp"), None),
            P(),
            P(),
            P(),
            P(),
            P(),
            P(),
        ),
        check_vma=False,
    )
```

```python
from functools import partial

import jax
import jax.numpy as jnp
from jax import lax
from jax.experimental import pallas as pl
from jax.experimental.pallas import tpu as pltpu
from jax.sharding import PartitionSpec as P

HEADS = 12
HEAD_DIM = 64
TROWS = 8
BR = 48
STEP = 10
GROUP = 16
PAIR = 2 * HEAD_DIM
GROUPS_AT_ONCE = 2
FRAMES_AT_ONCE = 2
VMEM_BYTES = 58 * 2**20

ln_eps = 1e-06
beta_one = 0.9
beta_two = 0.999
learn_rate = 0.05
table_rate = 0.4
decay_rate = 0.05
adam_eps = 1e-08
clip_max = 0.001
highest = lax.Precision.HIGHEST
f32 = jnp.float32
bf16 = jnp.bfloat16
gelu_a = 0.7978845608028654
gelu_b = 0.044715
masked = -1e30


def mm(left, right):
    return jnp.dot(left, right, preferred_element_type=f32)


def mm_nt(left, right):
    return lax.dot_general(left, right, (((1,), (1,)), ((), ())), preferred_element_type=f32)


def mm_tn(left, right):
    return lax.dot_general(left, right, (((0,), (0,)), ((), ())), preferred_element_type=f32)


def normed(values):
    centred = values - jnp.mean(values, axis=-1, keepdims=True)
    rstd = lax.rsqrt(jnp.mean(centred * centred, axis=-1, keepdims=True) + ln_eps)
    return centred * rstd, rstd


def norm_back(grad, xhat, rstd, gain):
    scaled = grad * gain
    return rstd * (
        scaled
        - jnp.mean(scaled, axis=-1, keepdims=True)
        - xhat * jnp.mean(scaled * xhat, axis=-1, keepdims=True)
    )


def fold(values):
    return jnp.sum(values.reshape(-1, 8, values.shape[-1]), axis=0)


def low_lanes():
    lane = lax.broadcasted_iota(jnp.int32, (1, PAIR), 1)
    low = jnp.where(lane < HEAD_DIM, 1.0, 0.0)
    return low.astype(bf16), (1.0 - low).astype(bf16)


def pick_half(stacked):
    rows = stacked.shape[0] // 2
    lane = lax.broadcasted_iota(jnp.int32, (rows, PAIR), 1)
    return jnp.where(lane < HEAD_DIM, stacked[:rows], stacked[rows:])


def fetch(slots_ref, source, target, sem, first, across):
    width = source.shape[2]
    per_tile = width // BR

    def one(i, carry):
        tile, row = i // per_tile, pl.multiple_of((i % per_tile) * BR, 16)
        place = pl.ds(row, BR)
        if across:
            into = target.at[place, pl.ds(pl.multiple_of(tile * width, width), width)]
        else:
            into = target.at[pl.ds(pl.multiple_of(tile * width, 16) + row, BR)]
        block = first(tile) * per_tile + i % per_tile
        pltpu.make_async_copy(source.at[slots_ref[block]], into, sem).start()
        return carry

    count = target.shape[0] * target.shape[1] // (width * width)
    lax.fori_loop(0, count * per_tile, one, 0)


def arrive(target, sem):
    pltpu.make_async_copy(target, target, sem).wait()


def attend(load, store, extra_q, extra_k):
    low, high = low_lanes()
    for pair in range(HEADS // 2):
        lanes = slice(pair * PAIR, (pair + 1) * PAIR)
        queries, keys, values = load(lanes)
        both = jnp.concatenate([queries * low, queries * high], axis=0)
        scores = mm_nt(
            jnp.concatenate([both, extra_q[...]], axis=1),
            jnp.concatenate([keys, extra_k[: keys.shape[0]]], axis=1),
        )
        top = jnp.max(scores, axis=-1, keepdims=True)
        weights = jnp.exp(scores - top).astype(bf16)
        summed = mm(weights, jnp.concatenate([values, jnp.ones_like(values)], axis=1))
        merged = pick_half(summed[:, :PAIR]) / pick_half(summed[:, PAIR:])
        store(lanes, merged.astype(bf16))


def attend_back(load, store, extra_q, extra_k):
    low, high = low_lanes()
    for pair in range(HEADS // 2):
        lanes = slice(pair * PAIR, (pair + 1) * PAIR)
        queries, keys, values, grads = load(lanes)
        rows = queries.shape[0]
        both_k = jnp.concatenate([keys * low, keys * high], axis=0)
        both_v = jnp.concatenate([values * low, values * high], axis=0)
        scores = mm_nt(
            jnp.concatenate([both_k, extra_k[...]], axis=1),
            jnp.concatenate([queries, extra_q[:rows]], axis=1),
        )
        back = mm_nt(both_v, grads)
        soft, inner = [], []
        for half in (slice(0, rows), slice(rows, 2 * rows)):
            part = scores[half]
            weights = jnp.exp(part - jnp.max(part, axis=0, keepdims=True))
            weights = weights * (1.0 / jnp.sum(weights, axis=0, keepdims=True))
            delta = back[half] - jnp.sum(weights * back[half], axis=0, keepdims=True)
            soft.append(weights.astype(bf16))
            inner.append((weights * delta).astype(bf16))
        soft = jnp.concatenate(soft, axis=0)
        inner = jnp.concatenate(inner, axis=0)
        store(
            lanes,
            (mm_tn(inner, both_k) * HEAD_DIM ** (-0.5)).astype(bf16),
            pick_half(mm(inner, queries)).astype(bf16),
            pick_half(mm(soft, grads)).astype(bf16),
        )


def project(hidden, rows, tiles):
    width = hidden.shape[1]
    joint = mm(hidden, tiles[...])
    queries = (joint[:, :width] + rows[2:3]).astype(bf16) * jnp.asarray(HEAD_DIM ** (-0.5), bf16)
    keys = joint[:, width : 2 * width].astype(bf16)
    values = (joint[:, 2 * width :] + rows[3:4]).astype(bf16)
    return queries, keys, values


def keep_norm(stream, rows, at, hid_ref, hat_ref, rstd_ref, here, cut):
    xhat, rstd = normed(stream)
    hat_ref[here] = xhat.astype(bf16).reshape(cut)
    rstd_ref[here] = jnp.broadcast_to(rstd, (rstd.shape[0], 128)).reshape(cut[:-1] + (128,))
    hidden = (xhat * rows[at : at + 1] + rows[at + 1 : at + 2]).astype(bf16)
    if hid_ref is not None:
        hid_ref[here] = hidden.reshape(cut)
    return xhat, hidden


def by_groups(block, total, work):
    step = pl.program_id(0)
    full, rest = total // block, total % block
    if rest == 0:
        work(block)
    else:
        pl.when(step < full)(lambda: work(block))
        pl.when(step == full)(lambda: work(rest))


def time_forward(
    total, slots, gathered, pixels, pos, trow, rows, extra_q, extra_k,
    x1_ref, hid_ref, hat_ref, rstd_ref, q_ref, k_ref, v_ref, o_ref,
    embed, joint, out, base, sems,
):
    frames, span, width = x1_ref.shape

    @pl.when(pl.program_id(0) == 0)
    def _():
        fetch(slots, gathered, embed, sems.at[0], lambda t: t, False)
        fetch(slots, gathered, joint, sems.at[1], lambda t: t + 1, True)
        fetch(slots, gathered, out, sems.at[2], lambda t: t + 4, False)
        arrive(embed, sems.at[0])
        arrive(joint, sems.at[1])
        arrive(out, sems.at[2])

    def work(count):
        cut = (frames, count * GROUP, width)
        flat = (frames * count * GROUP, width)
        here = slice(0, count * GROUP)
        every = (slice(None), here)
        offset = (pos[here][None] + trow[...][:, None]).reshape(flat)
        stream = mm(pixels[:, here].reshape(flat), embed[...]) + offset
        base[: flat[0]] = stream
        rows_now = rows[...]
        unused, hidden = keep_norm(stream, rows_now, 0, hid_ref, hat_ref, rstd_ref, every, cut)
        queries, keys, values = project(hidden, rows_now, joint)
        q_ref[:, here] = queries.reshape(cut)
        k_ref[:, here] = keys.reshape(cut)
        v_ref[:, here] = values.reshape(cut)
        for g in range(count):
            part = slice(g * GROUP, (g + 1) * GROUP)

            def load(lanes):
                return tuple(
                    ref[:, part, lanes].reshape(frames * GROUP, PAIR)
                    for ref in (q_ref, k_ref, v_ref)
                )

            def store(lanes, merged):
                o_ref[:, part, lanes] = merged.reshape(frames, GROUP, PAIR)

            attend(load, store, extra_q, extra_k)
        merged = o_ref[:, here].reshape(flat)
        stream = base[: flat[0]] + mm(merged, out[...]) + rows_now[4:5]
        x1_ref[:, here] = stream.reshape(cut)

    by_groups(span // GROUP, total, work)


def space_forward(
    slots, frame_weight, member, patches, gathered, x1, rows, low_rows, extra_q, extra_k,
    hid1_ref, hat1_ref, rstd1_ref, q_ref, k_ref, v_ref, o_ref,
    hid2_ref, hat2_ref, rstd2_ref, hat3_ref, rstd3_ref, gp_ref, act_ref, pool_ref,
    joint, out, ups, downs, acts, sems,
):
    step = pl.program_id(0)
    members = gp_ref.shape[0]
    cut = x1.shape
    span, count, width = cut
    flat = (span * count, width)
    every = (slice(None),)

    @pl.when(step == 0)
    def _():
        fetch(slots, gathered, joint, sems.at[0], lambda t: t + 5, True)
        fetch(slots, gathered, out, sems.at[1], lambda t: t + 8, False)
        fetch(slots, gathered, ups, sems.at[2], lambda t: 2 * t + 9, True)
        fetch(slots, gathered, downs, sems.at[3], lambda t: 2 * t + 10, False)
        pool_ref[...] = jnp.zeros_like(pool_ref)
        arrive(joint, sems.at[0])
        arrive(out, sems.at[1])

    rows_now = rows[...]
    unused, hidden = keep_norm(
        x1[...].reshape(flat), rows_now, 0, hid1_ref, hat1_ref, rstd1_ref, every, cut
    )
    queries, keys, values = project(hidden, rows_now, joint)
    q_ref[...] = queries.reshape(cut)
    k_ref[...] = keys.reshape(cut)
    v_ref[...] = values.reshape(cut)
    for f in range(span):

        def load(lanes):
            return q_ref[f, :, lanes], k_ref[f, :, lanes], v_ref[f, :, lanes]

        def store(lanes, merged):
            o_ref[f, :, lanes] = merged

        attend(load, store, extra_q, extra_k)
    merged = o_ref[...].reshape(flat)
    stream = x1[...].reshape(flat) + mm(merged, out[...]) + rows_now[4:5]
    low_now = low_rows[...]
    unused, hidden = keep_norm(stream, low_now, 0, hid2_ref, hat2_ref, rstd2_ref, every, cut)

    @pl.when(step == 0)
    def _():
        arrive(ups, sems.at[2])
        arrive(downs, sems.at[3])

    for j in range(members):
        lanes = slice(j * width, (j + 1) * width)
        upper = mm(hidden, ups[:, lanes])
        cubic = gelu_a * gelu_b * (upper * upper)
        gate = 0.5 + 0.5 * jnp.tanh(upper * (gelu_a + cubic))
        active = upper * gate
        slope = gate + active * (1.0 - gate) * (2.0 * gelu_a + 6.0 * cubic)
        gp_ref[j] = slope.astype(bf16).reshape(cut)
        acts[:, lanes] = active.astype(bf16)
        stream = stream + mm(acts[:, lanes], downs[lanes])
    for i in range(2):
        own = pl.ds(pl.multiple_of((member[0] ^ i) * width, 128), width)
        act_ref[i] = acts[:, own].reshape(cut)
    stream = stream + low_now[2:3]
    xhat, rstd = normed(stream)
    hat3_ref[...] = xhat.astype(bf16).reshape(cut)
    rstd3_ref[...] = jnp.broadcast_to(rstd, (flat[0], 128)).reshape(span, count, 128)
    final = xhat * low_now[3:4] + low_now[4:5]
    row = lax.broadcasted_iota(jnp.int32, (count, 1), 0)
    for f in range(span):
        part = jnp.where(row < patches, final[f * count : (f + 1) * count], 0.0)
        pool_ref[...] += fold(part) * frame_weight[step * span + f]


def mlp_backward(
    slots, frame_weight, member, patches, gathered, pool, pool_other, head, valid, targets, total,
    hid2, hat2, rstd2, hat3, rstd3, gp, act, low_rows,
    dx2_ref, own_ref, other_ref, rows_ref, small_ref,
    ups, downs, dus, spread, up_sum, down_sum, row_sums, sems,
):
    step = pl.program_id(0)
    members = gp.shape[0]
    cut = hid2.shape
    span, count, width = cut
    flat = (span * count, width)

    @pl.when(step == 0)
    def _():
        fetch(slots, gathered, downs, sems.at[1], lambda t: 2 * t + 10, False)
        fetch(slots, gathered, ups, sems.at[0], lambda t: 2 * t + 9, True)
        pooled = jnp.sum(pool[...] + pool_other[...], axis=0, keepdims=True).astype(bf16)
        pooled8 = jnp.broadcast_to(pooled, (8, width))
        logits = mm(pooled8, head[...])
        valid_f = valid[...]
        target = targets[...]
        soft = jnp.maximum(logits, 0.0) + jnp.log(1.0 + jnp.exp(-jnp.abs(logits)))
        loss = jnp.sum(valid_f * (soft - target * logits), axis=1, keepdims=True)
        sig = 1.0 / (1.0 + jnp.exp(-logits))
        grad = (valid_f * (sig - target) / jnp.maximum(total[0], 1.0)).astype(bf16)
        spread[...] = mm_nt(grad, head[...])
        small_ref[...] = jnp.zeros_like(small_ref)
        small_ref[0:1, :] = pooled.astype(f32)
        small_ref[1:2, 0 : grad.shape[1]] = grad[0:1].astype(f32)
        small_ref[2:3, 0:128] = jnp.broadcast_to(loss[0:1], (1, 128))
        up_sum[...] = jnp.zeros_like(up_sum)
        down_sum[...] = jnp.zeros_like(down_sum)
        row_sums[...] = jnp.zeros_like(row_sums)
        arrive(downs, sems.at[1])

    low_now = low_rows[...]
    row = lax.broadcasted_iota(jnp.int32, (count, 1), 0)
    weight = jnp.concatenate(
        [jnp.where(row < patches, frame_weight[step * span + f], 0.0) for f in range(span)]
    )
    grad_final = spread[0:1] * weight
    xhat = hat3[...].reshape(flat).astype(f32)
    rstd = rstd3[...].reshape(flat[0], 128)[:, 0:1]
    row_sums[3] += fold(grad_final * xhat)
    row_sums[4] += fold(grad_final)
    grad_top = norm_back(grad_final, xhat, rstd, low_now[3:4])
    row_sums[2] += fold(grad_top)
    grad_b = grad_top.astype(bf16)

    for j in range(members):
        lanes = slice(j * width, (j + 1) * width)
        du = mm_nt(grad_b, downs[lanes]) * gp[j].reshape(flat).astype(f32)
        dus[:, lanes] = du.astype(bf16)

    @pl.when(step == 0)
    def _():
        arrive(ups, sems.at[0])

    grad_hidden = mm_nt(dus[...], ups[...])
    for i in range(2):
        own = pl.ds(pl.multiple_of((member[0] ^ i) * width, 128), width)
        up_sum[i] += mm_tn(hid2[...].reshape(flat), dus[:, own])
        down_sum[i] += mm_tn(act[i].reshape(flat), grad_b)
    xhat = hat2[...].reshape(flat).astype(f32)
    rstd = rstd2[...].reshape(flat[0], 128)[:, 0:1]
    row_sums[0] += fold(grad_hidden * xhat)
    row_sums[1] += fold(grad_hidden)
    dx2_ref[...] = (grad_top + norm_back(grad_hidden, xhat, rstd, low_now[0:1])).reshape(cut)

    @pl.when(step == pl.num_programs(0) - 1)
    def _():
        for i, ref in enumerate((own_ref, other_ref)):
            ref[0] = up_sum[i].astype(bf16)
            ref[1] = down_sum[i].astype(bf16)
        rows_ref[...] = jnp.zeros_like(rows_ref)
        for i in range(5):
            rows_ref[i : i + 1] = jnp.sum(row_sums[i], axis=0, keepdims=True)


def close_attention(
    grad_stream, grad_b, hidden, xhat, rstd, grads, merged, rows_now, picked, ones, joint,
    joint_sum, out_sum, row_sums,
):
    grad_hidden = mm_nt(grads, joint[...])
    hidden_t = mm_nt(picked, hidden).astype(bf16) + ones
    merged_t = mm_nt(picked, merged).astype(bf16) + ones
    joint_sum[...] += mm(hidden_t, grads)
    out_sum[...] += mm(merged_t, grad_b)
    xhat = xhat.astype(f32)
    row_sums[0] += fold(grad_hidden * xhat)
    row_sums[1] += fold(grad_hidden)
    return grad_stream + norm_back(grad_hidden, xhat, rstd[:, 0:1], rows_now[0:1])


def ones_row(picked):
    row = lax.broadcasted_iota(jnp.int32, (picked.shape[0], 1), 0)
    return jnp.where(row == picked.shape[0] - 16, 1.0, 0.0).astype(bf16)


def clear(*refs):
    for ref in refs:
        ref[...] = jnp.zeros_like(ref)


def finish_attention(tile_refs, at, rows_ref, joint_sum, out_sum, row_sums):
    share, width = tile_refs[0].shape[1:]
    rows_ref[...] = jnp.zeros_like(rows_ref)
    for n, tile_ref in enumerate(tile_refs):
        here = slice(n * share, (n + 1) * share)
        for i in range(3):
            tile_ref[at + i] = joint_sum[here, i * width : (i + 1) * width].astype(bf16)
        tile_ref[at + 3] = out_sum[here].astype(bf16)
    last = slice(2 * share, 2 * share + 1)
    for i in range(2):
        rows_ref[i : i + 1] = jnp.sum(row_sums[i], axis=0, keepdims=True)
    rows_ref[2:3] = joint_sum[last, :width]
    rows_ref[3:4] = joint_sum[last, 2 * width :]
    rows_ref[4:5] = out_sum[last]


def space_backward(
    slots, gathered, dx2, hid1, hat1, rstd1, q, k, v, o, rows, picked, extra_q, extra_k,
    g1_ref, own_ref, other_ref, rows_ref,
    joint, out, joint_sum, out_sum, row_sums, grads, outer, sems,
):
    step = pl.program_id(0)
    cut = hid1.shape
    span, count, width = cut
    flat = (span * count, width)

    @pl.when(step == 0)
    def _():
        fetch(slots, gathered, out, sems.at[1], lambda t: t + 8, False)
        fetch(slots, gathered, joint, sems.at[0], lambda t: t + 5, True)
        clear(joint_sum, out_sum, row_sums)
        arrive(out, sems.at[1])
        arrive(joint, sems.at[0])

    grad_b = dx2[...].reshape(flat).astype(bf16)
    outer[...] = mm_nt(grad_b, out[...]).astype(bf16)
    for f in range(span):
        here = slice(f * count, (f + 1) * count)

        def load(lanes):
            return q[f, :, lanes], k[f, :, lanes], v[f, :, lanes], outer[here, lanes]

        def store(lanes, *parts):
            for i, part in enumerate(parts):
                grads[here, i * width + lanes.start : i * width + lanes.stop] = part

        attend_back(load, store, extra_q, extra_k)
    picked_now = picked[...]
    g1_ref[...] = close_attention(
        dx2[...].reshape(flat), grad_b, hid1[...].reshape(flat), hat1[...].reshape(flat),
        rstd1[...].reshape(flat[0], 128), grads[...], o[...].reshape(flat), rows[...],
        picked_now, ones_row(picked_now), joint, joint_sum, out_sum, row_sums,
    ).astype(bf16).reshape(cut)

    @pl.when(step == pl.num_programs(0) - 1)
    def _():
        finish_attention((own_ref, other_ref), 0, rows_ref, joint_sum, out_sum, row_sums)


def time_backward(
    rest, slots, member, gathered, near, far, hid0, hat0, rstd0, q, k, v, o, pixels, rows, picked,
    extra_q, extra_k,
    own_ref, other_ref, rows_ref, pos_ref, frame_ref,
    joint, out, joint_sum, out_sum, embed_sum, row_sums, grads, outer, sems,
):
    step = pl.program_id(0)
    frames, span, width = hid0.shape

    @pl.when(step == 0)
    def _():
        fetch(slots, gathered, out, sems.at[1], lambda t: t + 4, False)
        fetch(slots, gathered, joint, sems.at[0], lambda t: t + 1, True)
        clear(joint_sum, out_sum, embed_sum, row_sums, frame_ref)
        arrive(out, sems.at[1])
        arrive(joint, sems.at[0])

    def work(groups):
        cut = (frames, groups * GROUP, width)
        flat = (frames * groups * GROUP, width)
        small = (frames, GROUP, PAIR)
        here = slice(0, groups * GROUP)
        first = member[0] % 2 == 0
        near_now, far_now = near[:, here], far[:, here]
        grad_b = jnp.concatenate(
            [jnp.where(first, near_now, far_now), jnp.where(first, far_now, near_now)]
        ).reshape(flat)
        outer[:, here] = mm_nt(grad_b, out[...]).astype(bf16).reshape(cut)
        for g in range(groups):
            part = slice(g * GROUP, (g + 1) * GROUP)

            def load(lanes):
                return tuple(
                    ref[:, part, lanes].reshape(frames * GROUP, PAIR)
                    for ref in (q, k, v, outer)
                )

            def store(lanes, *parts):
                for i, value in enumerate(parts):
                    span_now = slice(i * width + lanes.start, i * width + lanes.stop)
                    grads[:, part, span_now] = value.reshape(small)

            attend_back(load, store, extra_q, extra_k)
        picked_now = picked[...]
        grad = close_attention(
            grad_b.astype(f32), grad_b, hid0[:, here].reshape(flat),
            hat0[:, here].reshape(flat), rstd0[:, here].reshape(flat[0], 128),
            grads[:, here].reshape(flat[0], 3 * width), o[:, here].reshape(flat), rows[...],
            picked_now, ones_row(picked_now), joint, joint_sum, out_sum, row_sums,
        )
        pix_t = mm_nt(picked_now, pixels[:, here].reshape(flat)).astype(bf16)
        embed_sum[...] += mm(pix_t, grad.astype(bf16))
        cube = grad.reshape(cut)
        pos_ref[here] = jnp.sum(cube, axis=0)
        frame_ref[...] += jnp.sum(cube, axis=1)

    last = step == pl.num_programs(0) - 1
    if rest == 0:
        work(span // GROUP)
    else:
        odd = member[0] % 2 == 1
        pl.when(jnp.logical_not(last))(lambda: work(span // GROUP))
        pl.when(jnp.logical_and(last, jnp.logical_not(odd)))(lambda: work(rest))

        @pl.when(jnp.logical_and(last, odd))
        def _():
            pos_ref[...] = jnp.zeros_like(pos_ref)

    @pl.when(last)
    def _():
        finish_attention((own_ref, other_ref), 1, rows_ref, joint_sum, out_sum, row_sums)
        share = own_ref.shape[1]
        own_ref[0] = embed_sum[:share].astype(bf16)
        other_ref[0] = embed_sum[share : 2 * share].astype(bf16)


def pack(dests, core, *refs):
    count = (len(refs) - 3) // 3
    owns, others, sums = refs[:count], refs[count : 2 * count], refs[-1 - count : -1]
    keep_ref, send_ref, sems = refs[2 * count], refs[2 * count + 1], refs[-1]
    table_rows = sums[-1].shape[1]
    slots = (keep_ref.shape[1] - table_rows) // BR

    def route(source, chunk, place, sem):
        mine = chunk % 2 == core[0]

        @pl.when(mine)
        def _():
            pltpu.make_async_copy(source, keep_ref.at[chunk // 2, place], sem).start()

        @pl.when(jnp.logical_not(mine))
        def _():
            pltpu.make_async_copy(source, send_ref.at[chunk // 2, place], sem).start()

    first = 0
    for n, (own, other, source) in enumerate(zip(owns, others, sums)):
        table = n == count - 1

        def one(i, carry, own=own, other=other, source=source, first=first, n=n, table=table):
            source[i] = (own[i].astype(f32) + other[i].astype(f32)).astype(bf16)
            if table:
                route(source.at[i], i, pl.ds(slots * BR, table_rows), sems.at[n])
            else:
                dest = dests[first + i]
                row = pl.multiple_of((dest % slots) * BR, 16)
                route(source.at[i], dest // slots, pl.ds(row, BR), sems.at[n])
            return carry

        lax.fori_loop(0, source.shape[0], one, 0)
        first += source.shape[0]
    for n, source in enumerate(sums):
        pltpu.make_async_copy(source, source, sems.at[n]).wait()


def swap(value, axis, hop):
    size = lax.axis_size(axis)
    return lax.ppermute(value, axis, [(i, i ^ hop) for i in range(size)])


def halve(kept, sent, axis):
    size = lax.axis_size(axis)
    place = lax.axis_index(axis)
    bits = size.bit_length() - 1
    rows, width = kept.shape[1:]
    middle = (width // 256) * 128
    met = swap(sent, axis, 1)
    cut = (2,) * (bits - 1) + (rows, width)
    kept, met = kept.reshape(cut), met.reshape(cut)
    ascending = list(range(1, bits))
    parts = [
        [kept[..., :middle], met[..., :middle], ascending],
        [kept[..., middle:], met[..., middle:], ascending[::-1]],
    ]
    parts = [(left.astype(f32) + right.astype(f32), order) for left, right, order in parts]
    for stage in range(bits - 1):
        outgoing, staying = [], []
        for value, order in parts:
            alive = sorted(order[stage:], reverse=True)
            at = alive.index(order[stage])
            bit = (place >> order[stage]) & 1
            outgoing.append(lax.dynamic_index_in_dim(value, 1 - bit, at, False).astype(bf16))
            staying.append(lax.dynamic_index_in_dim(value, bit, at, False))
        arrived = [
            swap(value, axis, 1 << order[stage]) for value, (unused, order) in zip(outgoing, parts)
        ]
        parts = [
            (stay + come.astype(f32), order)
            for stay, come, (unused, order) in zip(staying, arrived, parts)
        ]
    return jnp.concatenate([parts[0][0], parts[1][0]], axis=-1)


def block_ranks(owners):
    total_blocks = owners.shape[0]
    same_owner = owners[:, None] == owners[None, :]
    earlier = jnp.arange(total_blocks)[None, :] < jnp.arange(total_blocks)[:, None]
    return jnp.sum((same_owner & earlier).astype(jnp.int32), axis=1)


def adamw(weight, gradient, moment_one, moment_two, weight_decay, rate):
    first_new = beta_one * moment_one + (1.0 - beta_one) * gradient
    second_new = beta_two * moment_two + (1.0 - beta_two) * gradient * gradient
    mean_hat = first_new / (1.0 - beta_one**STEP)
    var_hat = second_new / (1.0 - beta_two**STEP)
    updated = weight - rate * (mean_hat / (jnp.sqrt(var_hat) + adam_eps) + weight_decay * weight)
    return (updated, first_new, second_new)


def local(
    pixels,
    lengths,
    frame_mask,
    time_index,
    label_valid,
    targets,
    owners,
    slot_weight,
    slot_moment1,
    slot_moment2,
    tables,
    table_moment1,
    table_moment2,
    head_weight,
    head_moment1,
    head_moment2,
):
    dp_count = lax.axis_size("dp")
    mlp_count = lax.axis_size("mlp")
    member = lax.axis_index("mlp").astype(jnp.int32)
    width = slot_weight.shape[1]
    per_tile = width // BR
    slots = slot_weight.shape[0] // BR
    shared_blocks = 9 * per_tile
    frames, patches = pixels.shape[1], pixels.shape[2]
    padded = -(-patches // GROUP) * GROUP
    groups = padded // GROUP
    classes = head_weight.shape[1]
    class_pad = -(-classes // 128) * 128
    params = pltpu.CompilerParams(vmem_limit_bytes=VMEM_BYTES)
    any_spec = pl.BlockSpec(memory_space=pl.ANY)

    gathered = lax.all_gather(slot_weight.astype(bf16), ("dp", "mlp"), axis=0, tiled=True)
    gathered = gathered.reshape(-1, BR, width)
    slot_index = (owners * slots + block_ranks(owners)).astype(jnp.int32)

    pix = jnp.pad(pixels[0], ((0, 0), (0, padded - patches), (0, 0)))
    slot_pos = jnp.arange(frames)
    frame_live = slot_pos < lengths[0]
    key_ok = frame_live & (frame_mask[0] == 1)
    allowed = key_ok[None, :] | (slot_pos[:, None] == slot_pos[None, :])
    extra_lane = jnp.arange(HEAD_DIM)
    flat_id = jnp.arange(frames * GROUP)
    frame_id, patch_id = flat_id // GROUP, flat_id % GROUP
    lane_frame = jnp.clip(extra_lane - GROUP, 0, frames - 1)
    in_patch = (extra_lane < GROUP)[None, :]
    in_frame = ((extra_lane >= GROUP) & (extra_lane < GROUP + frames))[None, :]
    same_patch = patch_id[:, None] == extra_lane[None, :]
    same_frame = frame_id[:, None] == lane_frame[None, :]
    time_q = (in_patch & same_patch) | (in_frame & same_frame)
    time_k = (in_patch & ~same_patch) | (in_frame & ~allowed.T[frame_id][:, lane_frame])
    is_pad = (jnp.arange(padded) >= patches)[:, None]
    space_q = jnp.broadcast_to(extra_lane[None, :] == 0, (padded, HEAD_DIM))
    space_k = is_pad & (extra_lane[None, :] == 0)

    def widen(flags, value):
        block = jnp.where(flags, value, 0.0).astype(bf16)
        block = jnp.pad(block, ((0, 0), (0, PAIR - HEAD_DIM)))
        return jnp.concatenate([block, block])

    time_q, time_k = widen(time_q, 1.0), widen(time_k, masked)
    space_q, space_k = widen(space_q, 1.0), widen(space_k, masked)
    time_hot = (time_index[0][:, None] == jnp.arange(TROWS)[None, :]).astype(f32)
    trow = jnp.einsum("ft,td->fd", time_hot, tables[16 + patches :], precision=highest)
    pos = jnp.pad(tables[16 : 16 + patches] + tables[0], ((0, padded - patches), (0, 0)))
    frame_weight = jnp.where(
        frame_live, 1.0 / (lengths[0] * patches).astype(f32), 0.0
    ).astype(f32)
    valid_f = label_valid.astype(f32)
    label_total = lax.psum(jnp.sum(valid_f), "dp")
    pix, label_total = lax.optimization_barrier((pix, label_total))
    share = width // mlp_count
    half = member % 2
    pick_row = jnp.arange(2 * share)
    pick_member = jnp.where(pick_row < share, member, member ^ 1)
    pick_row = pick_row % share
    pick_feature = (pick_row // BR) * (BR * mlp_count) + pick_member * BR + pick_row % BR
    picked = (pick_feature[:, None] == jnp.arange(width)[None, :]).astype(bf16)
    picked = jnp.pad(picked, ((0, 16), (0, 0)))
    member_s = member[None]
    time_rows = jnp.pad(tables[1:6], ((0, 3), (0, 0)))
    space_rows = jnp.pad(tables[6:11], ((0, 3), (0, 0)))
    low_rows = jnp.pad(tables[11:16], ((0, 3), (0, 0)))

    cube32 = jax.ShapeDtypeStruct((frames, padded, width), f32)
    cube16 = jax.ShapeDtypeStruct((frames, padded, width), bf16)
    thin32 = jax.ShapeDtypeStruct((frames, padded, 128), f32)
    row32 = jax.ShapeDtypeStruct((8, width), f32)
    group_rows = GROUPS_AT_ONCE * GROUP
    frame_rows = FRAMES_AT_ONCE * padded
    group_spec = pl.BlockSpec((frames, group_rows, width), lambda g, *_: (0, g, 0))
    group_thin = pl.BlockSpec((frames, group_rows, 128), lambda g, *_: (0, g, 0))
    patch_spec = pl.BlockSpec((group_rows, width), lambda g, *_: (g, 0))
    frame_spec = pl.BlockSpec((FRAMES_AT_ONCE, padded, width), lambda f, *_: (f, 0, 0))
    frame_thin = pl.BlockSpec((FRAMES_AT_ONCE, padded, 128), lambda f, *_: (f, 0, 0))
    gp_spec = pl.BlockSpec(
        (mlp_count, FRAMES_AT_ONCE, padded, width), lambda f, *_: (0, f, 0, 0)
    )
    time_grid = (-(-groups // GROUPS_AT_ONCE),)
    half_frames = frames // 2
    space_grid = (half_frames // FRAMES_AT_ONCE,)
    half_blocks = groups // 2 // GROUPS_AT_ONCE
    rest = groups - 2 * half_blocks * GROUPS_AT_ONCE
    half_rows = (half_blocks * GROUPS_AT_ONCE + rest) * GROUP
    back_grid = (half_blocks + (1 if rest else 0),)

    def half_index(s, m):
        ending = jnp.where(m[0] % 2 == 0, 2 * half_blocks, 2 * half_blocks - 1)
        return jnp.where(s < half_blocks, (m[0] % 2) * half_blocks + s, ending)

    back_spec = pl.BlockSpec((frames, group_rows, width), lambda s, i, m: (0, half_index(s, m), 0))
    back_thin = pl.BlockSpec((frames, group_rows, 128), lambda s, i, m: (0, half_index(s, m), 0))
    near_spec = pl.BlockSpec((half_frames, group_rows, width), lambda s, *_: (0, s, 0))
    my_frame_spec = pl.BlockSpec(
        (FRAMES_AT_ONCE, padded, width),
        lambda f, s, w, m: ((m[0] % 2) * (half_frames // FRAMES_AT_ONCE) + f, 0, 0),
    )
    act_spec = pl.BlockSpec((2, FRAMES_AT_ONCE, padded, width), lambda f, *_: (0, f, 0, 0))
    half16 = jax.ShapeDtypeStruct((half_frames, padded, width), bf16)
    half32 = jax.ShapeDtypeStruct((half_frames, padded, width), f32)
    half_thin = jax.ShapeDtypeStruct((half_frames, padded, 128), f32)
    frame_weight = lax.dynamic_slice_in_dim(frame_weight, half * half_frames, half_frames)

    def whole(*shape):
        return pl.BlockSpec(shape, lambda i, *_: (0,) * len(shape))

    rows_spec = whole(8, width)
    time_extra = whole(2 * frames * GROUP, PAIR)
    space_extra = whole(2 * padded, PAIR)
    pick_spec = whole(2 * share + 16, width)

    def call(kernel, name, units, scalars, grid, ins, in_specs, outs, out_specs, scratch):
        return pl.pallas_call(
            kernel,
            grid_spec=pltpu.PrefetchScalarGridSpec(
                num_scalar_prefetch=len(scalars),
                grid=grid,
                in_specs=[any_spec] + in_specs,
                out_specs=out_specs,
                scratch_shapes=scratch,
            ),
            out_shape=outs,
            compiler_params=params,
            cost_estimate=pl.CostEstimate(
                flops=units * 2 * frames * padded * width * width,
                bytes_accessed=16 * width * width,
                transcendentals=0,
            ),
            name=name,
        )(*scalars, gathered, *ins)

    def tile_bufs(*shapes):
        return [pltpu.VMEM((rows * width, cols * width), bf16) for rows, cols in shapes]

    x1, hid0, hat0, rstd0, q_t, k_t, v_t, o_t = call(
        partial(time_forward, groups),
        "time_forward",
        14,
        [slot_index],
        time_grid,
        [pix, pos, trow, time_rows, time_q, time_k],
        [group_spec, patch_spec, whole(frames, width), rows_spec, time_extra, time_extra],
        [cube32, cube16, cube16, thin32] + [cube16] * 4,
        [group_spec] * 3 + [group_thin] + [group_spec] * 4,
        tile_bufs((1, 1), (1, 3), (1, 1))
        + [pltpu.VMEM((frames * group_rows, width), f32), pltpu.SemaphoreType.DMA((3,))],
    )
    (hid1, hat1, rstd1, q_s, k_s, v_s, o_s, hid2, hat2, rstd2, hat3, rstd3, gp, act, pool) = call(
        lambda s, fw, m, *refs: space_forward(s, fw, m, patches, *refs),
        "space_forward",
        15,
        [slot_index, frame_weight, member_s],
        space_grid,
        [x1, space_rows, low_rows, space_q, space_k],
        [my_frame_spec, rows_spec, rows_spec, space_extra, space_extra],
        [half16, half16, half_thin]
        + [half16] * 4
        + [half16, half16, half_thin, half16, half_thin]
        + [
            jax.ShapeDtypeStruct((mlp_count, half_frames, padded, width), bf16),
            jax.ShapeDtypeStruct((2, half_frames, padded, width), bf16),
            row32,
        ],
        [frame_spec, frame_spec, frame_thin]
        + [frame_spec] * 4
        + [frame_spec, frame_spec, frame_thin, frame_spec, frame_thin]
        + [gp_spec, act_spec, rows_spec],
        tile_bufs((1, 3), (1, 1), (1, mlp_count), (mlp_count, 1))
        + [pltpu.VMEM((frame_rows, mlp_count * width), bf16), pltpu.SemaphoreType.DMA((4,))],
    )

    head_b = jnp.pad(head_weight.astype(bf16), ((0, 0), (0, class_pad - classes)))
    valid_p = jnp.pad(valid_f, ((0, 0), (0, class_pad - classes)))
    targets_p = jnp.pad(targets, ((0, 0), (0, class_pad - classes)))
    pool_other = swap(pool, "mlp", 1)
    squares16 = jax.ShapeDtypeStruct((2, width, width), bf16)
    dx2, own_mlp, other_mlp, rows_low, small = call(
        lambda s, fw, m, *refs: mlp_backward(s, fw, m, patches, *refs),
        "mlp_backward",
        13,
        [slot_index, frame_weight, member_s],
        space_grid,
        [
            pool, pool_other, head_b, valid_p, targets_p, label_total[None],
            hid2, hat2, rstd2, hat3, rstd3, gp, act, low_rows,
        ],
        [
            rows_spec, rows_spec, whole(width, class_pad), whole(1, class_pad), whole(1, class_pad),
            pl.BlockSpec(memory_space=pltpu.SMEM),
            frame_spec, frame_spec, frame_thin, frame_spec, frame_thin, gp_spec, act_spec,
            rows_spec,
        ],
        [half32, squares16, squares16, row32, row32],
        [frame_spec, whole(2, width, width), whole(2, width, width), rows_spec, rows_spec],
        tile_bufs((1, mlp_count), (mlp_count, 1))
        + [
            pltpu.VMEM((frame_rows, mlp_count * width), bf16),
            pltpu.VMEM((8, width), f32),
            pltpu.VMEM((2, width, width), f32),
            pltpu.VMEM((2, width, width), f32),
            pltpu.VMEM((5, 8, width), f32),
            pltpu.SemaphoreType.DMA((2,)),
        ],
    )

    sums = [
        pltpu.VMEM((2 * share + 16, 3 * width), f32),
        pltpu.VMEM((2 * share + 16, width), f32),
    ]
    met_mlp = swap(other_mlp, "mlp", 1)
    g1, own_space, other_space, rows_space = call(
        space_backward,
        "space_backward",
        16,
        [slot_index],
        space_grid,
        [dx2, hid1, hat1, rstd1, q_s, k_s, v_s, o_s, space_rows, picked, space_q, space_k],
        [frame_spec] * 3
        + [frame_thin]
        + [frame_spec] * 4
        + [rows_spec, pick_spec, space_extra, space_extra],
        [half16] + [jax.ShapeDtypeStruct((4, share, width), bf16)] * 2 + [row32],
        [frame_spec] + [whole(4, share, width)] * 2 + [rows_spec],
        tile_bufs((1, 3), (1, 1))
        + sums
        + [
            pltpu.VMEM((2, 8, width), f32),
            pltpu.VMEM((frame_rows, 3 * width), bf16),
            pltpu.VMEM((frame_rows, width), bf16),
            pltpu.SemaphoreType.DMA((2,)),
        ],
    )


    def patches_of(which):
        main = half_blocks * group_rows
        here = lax.dynamic_slice_in_dim(g1, which * main, main, 1)
        return jnp.concatenate([here, g1[:, 2 * main :]], axis=1)

    far = swap(patches_of(1 - half), "mlp", 1)
    near = patches_of(half)
    near, met_mlp = lax.optimization_barrier((near, met_mlp))
    met_space = swap(other_space, "mlp", 1)
    own_time, other_time, rows_time, grad_pos, grad_frames = call(
        partial(time_backward, rest),
        "time_backward",
        18,
        [slot_index, member_s],
        back_grid,
        [near, far, hid0, hat0, rstd0, q_t, k_t, v_t, o_t, pix, time_rows, picked, time_q, time_k],
        [near_spec] * 2
        + [back_spec] * 2
        + [back_thin]
        + [back_spec] * 5
        + [rows_spec, pick_spec, time_extra, time_extra],
        [jax.ShapeDtypeStruct((5, share, width), bf16)] * 2
        + [
            row32,
            jax.ShapeDtypeStruct((half_rows, width), f32),
            jax.ShapeDtypeStruct((frames, width), f32),
        ],
        [whole(5, share, width)] * 2 + [rows_spec, patch_spec, whole(frames, width)],
        tile_bufs((1, 3), (1, 1))
        + sums
        + [
            pltpu.VMEM((2 * share + 16, width), f32),
            pltpu.VMEM((2, 8, width), f32),
            pltpu.VMEM((frames, group_rows, 3 * width), bf16),
            pltpu.VMEM((frames, group_rows, width), bf16),
            pltpu.SemaphoreType.DMA((2,)),
        ],
    )

    grad_time = jnp.einsum("ft,fd->td", time_hot, grad_frames, precision=highest)
    other_time, met_space = lax.optimization_barrier((other_time, met_space))
    met_time = swap(other_time, "mlp", 1)
    main = half_blocks * group_rows
    all_pos = jnp.concatenate(
        [jnp.where(half == i, grad_pos[:main], 0.0) for i in range(2)] + [grad_pos[main:]]
    )
    table_rows = tables.shape[0]
    table_part = jnp.concatenate(
        [
            jnp.sum(grad_frames, axis=0, keepdims=True),
            rows_time[:5],
            rows_space[:5],
            rows_low[:5],
            all_pos[:patches],
            grad_time,
        ]
    )
    rows_each = -(-table_rows // (dp_count * mlp_count))
    table_part = jnp.pad(
        table_part, ((0, rows_each * dp_count * mlp_count - table_rows), (0, 0))
    ).reshape(dp_count, mlp_count, rows_each, width)

    def table_of(which):
        rows_now = lax.dynamic_index_in_dim(table_part, which, 1, False).astype(bf16)
        return jnp.pad(rows_now, ((0, 0), (0, 16 - rows_each), (0, 0)))

    met_table = swap(table_of(member ^ 1), "mlp", 1)

    def blocks_of(*parts):
        return [part.reshape(-1, BR, width) for part in parts]

    sources = blocks_of(own_time, own_space, own_mlp) + [table_of(member)]
    sources = sources + blocks_of(met_time, met_space, met_mlp) + [met_table]
    shared_here = shared_blocks // mlp_count
    here_ids = jnp.arange(shared_here + 2 * per_tile)
    block_of = jnp.where(
        here_ids < shared_here,
        here_ids * mlp_count + member,
        here_ids - shared_here + shared_blocks + member * 2 * per_tile,
    )
    here_slots = slot_index[block_of]
    dests = (here_slots // (slots * mlp_count)) * slots + here_slots % slots
    place = lax.axis_index("dp").astype(jnp.int32)
    chunk = jax.ShapeDtypeStruct((dp_count // 2, slots * BR + 16, width), bf16)
    kept, sent = pl.pallas_call(
        pack,
        grid_spec=pltpu.PrefetchScalarGridSpec(
            num_scalar_prefetch=2,
            grid=(1,),
            in_specs=[pl.BlockSpec(memory_space=pltpu.VMEM)] * 8,
            out_specs=[any_spec] * 2,
            scratch_shapes=[pltpu.VMEM(part.shape, bf16) for part in sources[:4]]
            + [pltpu.SemaphoreType.DMA((4,))],
        ),
        out_shape=[chunk, chunk],
        compiler_params=params,
        name="pack",
    )(dests, (place % 2)[None], *sources)
    summed = halve(kept, sent, "dp")
    my_slots = (place * mlp_count + member) * slots + jnp.arange(slots)
    filled = jnp.any(slot_index[:, None] == my_slots[None, :], axis=0)
    filled = jnp.repeat(filled, BR)[:, None]
    own_grad = jnp.where(filled, summed[: slots * BR], 0.0)
    squares_own = jnp.sum(own_grad * own_grad)
    block = jnp.concatenate(
        [
            jnp.pad(summed[slots * BR : slots * BR + rows_each], ((0, 7 - rows_each), (0, 0))),
            jnp.broadcast_to(squares_own, (1, width)),
            small,
        ]
    )
    blocks = jnp.concatenate(
        [lax.all_gather(block[:8], "mlp", axis=0), block[None, 8:]], axis=0
    )
    blocks = lax.all_gather(blocks, "dp", axis=0)
    heads, blocks = blocks[:, mlp_count], blocks[:, :mlp_count]
    grad_head = jnp.einsum("cd,ck->dk", heads[:, 0], heads[:, 1, :classes], precision=highest)
    loss_sum = jnp.sum(heads[:, 2, 0])
    grad_tables = blocks[:, :, :rows_each].reshape(-1, width)[:table_rows]
    grad_norm = jnp.sqrt(
        jnp.sum(blocks[:, :, 7, 0])
        + jnp.sum(grad_tables * grad_tables)
        + jnp.sum(grad_head * grad_head)
    )
    factor = jnp.minimum(1.0, clip_max / (grad_norm + 1e-06))
    new_slots = adamw(
        slot_weight, own_grad * factor, slot_moment1, slot_moment2, decay_rate, learn_rate
    )
    new_tabs = adamw(tables, grad_tables * factor, table_moment1, table_moment2, 0.0, table_rate)
    new_heads = adamw(
        head_weight, grad_head * factor, head_moment1, head_moment2, decay_rate, learn_rate
    )
    return (
        loss_sum,
        label_total,
        grad_norm,
        new_slots[0],
        new_slots[1],
        new_slots[2],
        new_tabs[0],
        new_tabs[1],
        new_tabs[2],
        new_heads[0],
        new_heads[1],
        new_heads[2],
    )


def solution(mesh):
    return jax.shard_map(
        local,
        mesh=mesh,
        in_specs=(
            P("dp", None, None, None),
            P("dp"),
            P("dp", None),
            P("dp", None),
            P("dp", None),
            P("dp", None),
            P(),
            P(("dp", "mlp"), None),
            P(("dp", "mlp"), None),
            P(("dp", "mlp"), None),
            P(),
            P(),
            P(),
            P(),
            P(),
            P(),
        ),
        out_specs=(
            P(),
            P(),
            P(),
            P(("dp", "mlp"), None),
            P(("dp", "mlp"), None),
            P(("dp", "mlp"), None),
            P(),
            P(),
            P(),
            P(),
            P(),
            P(),
        ),
        check_vma=False,
    )
```

```python
from functools import partial

import jax
import jax.numpy as jnp
from jax import lax
from jax.experimental import pallas as pl
from jax.experimental.pallas import tpu as pltpu
from jax.sharding import PartitionSpec as P

HEADS = 12
HEAD_DIM = 64
TROWS = 8
BR = 48
STEP = 10
GROUP = 16
PAIR = 2 * HEAD_DIM
GROUPS_AT_ONCE = 2
FRAMES_AT_ONCE = 2
VMEM_BYTES = 58 * 2**20

ln_eps = 1e-06
beta_one = 0.9
beta_two = 0.999
learn_rate = 0.05
table_rate = 0.4
decay_rate = 0.05
adam_eps = 1e-08
clip_max = 0.001
highest = lax.Precision.HIGHEST
f32 = jnp.float32
bf16 = jnp.bfloat16
gelu_a = 0.7978845608028654
gelu_b = 0.044715
masked = -1e30


def mm(left, right):
    return jnp.dot(left, right, preferred_element_type=f32)


def mm_nt(left, right):
    return lax.dot_general(left, right, (((1,), (1,)), ((), ())), preferred_element_type=f32)


def mm_tn(left, right):
    return lax.dot_general(left, right, (((0,), (0,)), ((), ())), preferred_element_type=f32)


def normed(values):
    centred = values - jnp.mean(values, axis=-1, keepdims=True)
    rstd = lax.rsqrt(jnp.mean(centred * centred, axis=-1, keepdims=True) + ln_eps)
    return centred * rstd, rstd


def norm_back(grad, xhat, rstd, gain):
    scaled = grad * gain
    return rstd * (
        scaled
        - jnp.mean(scaled, axis=-1, keepdims=True)
        - xhat * jnp.mean(scaled * xhat, axis=-1, keepdims=True)
    )


def fold(values):
    return jnp.sum(values.reshape(-1, 8, values.shape[-1]), axis=0)


def low_lanes():
    lane = lax.broadcasted_iota(jnp.int32, (1, PAIR), 1)
    low = jnp.where(lane < HEAD_DIM, 1.0, 0.0)
    return low.astype(bf16), (1.0 - low).astype(bf16)


def pick_half(stacked):
    rows = stacked.shape[0] // 2
    lane = lax.broadcasted_iota(jnp.int32, (rows, PAIR), 1)
    return jnp.where(lane < HEAD_DIM, stacked[:rows], stacked[rows:])


def fetch(slots_ref, source, target, sem, first, across):
    width = source.shape[2]
    per_tile = width // BR

    def one(i, carry):
        tile, row = i // per_tile, pl.multiple_of((i % per_tile) * BR, 16)
        place = pl.ds(row, BR)
        if across:
            into = target.at[place, pl.ds(pl.multiple_of(tile * width, width), width)]
        else:
            into = target.at[pl.ds(pl.multiple_of(tile * width, 16) + row, BR)]
        block = first(tile) * per_tile + i % per_tile
        pltpu.make_async_copy(source.at[slots_ref[block]], into, sem).start()
        return carry

    count = target.shape[0] * target.shape[1] // (width * width)
    lax.fori_loop(0, count * per_tile, one, 0)


def arrive(target, sem):
    pltpu.make_async_copy(target, target, sem).wait()


def jobs_of(count):
    pairs = [slice(p * PAIR, (p + 1) * PAIR) for p in range(HEADS // 2)]
    return [(i, lanes) for i in range(count) for lanes in pairs]


def in_flight(jobs, begin, finish):
    waiting = None
    for job in jobs:
        started = begin(*job)
        if waiting is not None:
            finish(*waiting)
        waiting = job + started
    finish(*waiting)


def attend(count, load, store, extra_q, extra_k):
    low, high = low_lanes()

    def begin(i, lanes):
        queries, keys, values = load(i, lanes)
        both = jnp.concatenate([queries * low, queries * high], axis=0)
        scores = mm_nt(
            jnp.concatenate([both, extra_q[...]], axis=1),
            jnp.concatenate([keys, extra_k[: keys.shape[0]]], axis=1),
        )
        return values, scores

    def finish(i, lanes, values, scores):
        top = jnp.max(scores, axis=-1, keepdims=True)
        weights = jnp.exp(scores - top).astype(bf16)
        summed = mm(weights, jnp.concatenate([values, jnp.ones_like(values)], axis=1))
        merged = pick_half(summed[:, :PAIR]) / pick_half(summed[:, PAIR:])
        store(i, lanes, merged.astype(bf16))

    in_flight(jobs_of(count), begin, finish)


def attend_back(count, load, store, extra_q, extra_k):
    low, high = low_lanes()

    def begin(i, lanes):
        queries, keys, values, grads = load(i, lanes)
        both_k = jnp.concatenate([keys * low, keys * high], axis=0)
        both_v = jnp.concatenate([values * low, values * high], axis=0)
        scores = mm_nt(
            jnp.concatenate([both_k, extra_k[...]], axis=1),
            jnp.concatenate([queries, extra_q[: queries.shape[0]]], axis=1),
        )
        return queries, both_k, grads, scores, mm_nt(both_v, grads)

    def finish(i, lanes, queries, both_k, grads, scores, back):
        rows = queries.shape[0]
        soft, inner = [], []
        for half in (slice(0, rows), slice(rows, 2 * rows)):
            part = scores[half]
            weights = jnp.exp(part - jnp.max(part, axis=0, keepdims=True))
            weights = weights * (1.0 / jnp.sum(weights, axis=0, keepdims=True))
            delta = back[half] - jnp.sum(weights * back[half], axis=0, keepdims=True)
            soft.append(weights.astype(bf16))
            inner.append((weights * delta).astype(bf16))
        soft = jnp.concatenate(soft, axis=0)
        inner = jnp.concatenate(inner, axis=0)
        store(
            i,
            lanes,
            (mm_tn(inner, both_k) * HEAD_DIM ** (-0.5)).astype(bf16),
            pick_half(mm(inner, queries)).astype(bf16),
            pick_half(mm(soft, grads)).astype(bf16),
        )

    in_flight(jobs_of(count), begin, finish)


def project(hidden, rows, tiles):
    width = hidden.shape[1]
    joint = mm(hidden, tiles[...])
    queries = (joint[:, :width] + rows[2:3]).astype(bf16) * jnp.asarray(HEAD_DIM ** (-0.5), bf16)
    keys = joint[:, width : 2 * width].astype(bf16)
    values = (joint[:, 2 * width :] + rows[3:4]).astype(bf16)
    return queries, keys, values


def keep_norm(stream, rows, at, hid_ref, hat_ref, rstd_ref, here, cut):
    xhat, rstd = normed(stream)
    hat_ref[here] = xhat.astype(bf16).reshape(cut)
    rstd_ref[here] = jnp.broadcast_to(rstd, (rstd.shape[0], 128)).reshape(cut[:-1] + (128,))
    hidden = (xhat * rows[at : at + 1] + rows[at + 1 : at + 2]).astype(bf16)
    if hid_ref is not None:
        hid_ref[here] = hidden.reshape(cut)
    return xhat, hidden


def by_groups(block, total, work):
    step = pl.program_id(0)
    full, rest = total // block, total % block
    if rest == 0:
        work(block)
    else:
        pl.when(step < full)(lambda: work(block))
        pl.when(step == full)(lambda: work(rest))


def time_forward(
    total, slots, gathered, pixels, pos, trow, rows, extra_q, extra_k,
    x1_ref, hid_ref, hat_ref, rstd_ref, q_ref, k_ref, v_ref, o_ref,
    embed, joint, out, base, sems,
):
    frames, span, width = x1_ref.shape

    @pl.when(pl.program_id(0) == 0)
    def _():
        fetch(slots, gathered, embed, sems.at[0], lambda t: t, False)
        fetch(slots, gathered, joint, sems.at[1], lambda t: t + 1, True)
        fetch(slots, gathered, out, sems.at[2], lambda t: t + 4, False)
        arrive(embed, sems.at[0])

    def first(target, sem):
        pl.when(pl.program_id(0) == 0)(lambda: arrive(target, sem))

    def work(count):
        cut = (frames, count * GROUP, width)
        flat = (frames * count * GROUP, width)
        here = slice(0, count * GROUP)
        every = (slice(None), here)
        offset = (pos[here][None] + trow[...][:, None]).reshape(flat)
        stream = mm(pixels[:, here].reshape(flat), embed[...]) + offset
        base[: flat[0]] = stream
        rows_now = rows[...]
        unused, hidden = keep_norm(stream, rows_now, 0, hid_ref, hat_ref, rstd_ref, every, cut)
        first(joint, sems.at[1])
        queries, keys, values = project(hidden, rows_now, joint)
        q_ref[:, here] = queries.reshape(cut)
        k_ref[:, here] = keys.reshape(cut)
        v_ref[:, here] = values.reshape(cut)

        def load(g, lanes):
            part = slice(g * GROUP, (g + 1) * GROUP)
            return tuple(
                ref[:, part, lanes].reshape(frames * GROUP, PAIR) for ref in (q_ref, k_ref, v_ref)
            )

        def store(g, lanes, merged):
            part = slice(g * GROUP, (g + 1) * GROUP)
            o_ref[:, part, lanes] = merged.reshape(frames, GROUP, PAIR)

        attend(count, load, store, extra_q, extra_k)
        first(out, sems.at[2])
        merged = o_ref[:, here].reshape(flat)
        stream = base[: flat[0]] + mm(merged, out[...]) + rows_now[4:5]
        x1_ref[:, here] = stream.reshape(cut)

    by_groups(span // GROUP, total, work)


def space_forward(
    slots, frame_weight, member, patches, gathered, x1, rows, low_rows, extra_q, extra_k,
    hid1_ref, hat1_ref, rstd1_ref, q_ref, k_ref, v_ref, o_ref,
    hid2_ref, hat2_ref, rstd2_ref, hat3_ref, rstd3_ref, gp_ref, act_ref, pool_ref,
    joint, out, ups, downs, acts, sems,
):
    step = pl.program_id(0)
    members = gp_ref.shape[0]
    cut = x1.shape
    span, count, width = cut
    flat = (span * count, width)
    every = (slice(None),)

    @pl.when(step == 0)
    def _():
        fetch(slots, gathered, joint, sems.at[0], lambda t: t + 5, True)
        fetch(slots, gathered, out, sems.at[1], lambda t: t + 8, False)
        fetch(slots, gathered, ups, sems.at[2], lambda t: 2 * t + 9, True)
        fetch(slots, gathered, downs, sems.at[3], lambda t: 2 * t + 10, False)
        pool_ref[...] = jnp.zeros_like(pool_ref)
        arrive(joint, sems.at[0])

    rows_now = rows[...]
    unused, hidden = keep_norm(
        x1[...].reshape(flat), rows_now, 0, hid1_ref, hat1_ref, rstd1_ref, every, cut
    )
    queries, keys, values = project(hidden, rows_now, joint)
    q_ref[...] = queries.reshape(cut)
    k_ref[...] = keys.reshape(cut)
    v_ref[...] = values.reshape(cut)

    def load(f, lanes):
        return q_ref[f, :, lanes], k_ref[f, :, lanes], v_ref[f, :, lanes]

    def store(f, lanes, merged):
        o_ref[f, :, lanes] = merged

    attend(span, load, store, extra_q, extra_k)
    pl.when(step == 0)(lambda: arrive(out, sems.at[1]))
    merged = o_ref[...].reshape(flat)
    stream = x1[...].reshape(flat) + mm(merged, out[...]) + rows_now[4:5]
    low_now = low_rows[...]
    unused, hidden = keep_norm(stream, low_now, 0, hid2_ref, hat2_ref, rstd2_ref, every, cut)

    @pl.when(step == 0)
    def _():
        arrive(ups, sems.at[2])
        arrive(downs, sems.at[3])

    def begin(j, lanes):
        return (mm(hidden, ups[:, lanes]),)

    lowered = []

    def finish(j, lanes, upper):
        cubic = gelu_a * gelu_b * (upper * upper)
        gate = 0.5 + 0.5 * jnp.tanh(upper * (gelu_a + cubic))
        active = upper * gate
        slope = gate + active * (1.0 - gate) * (2.0 * gelu_a + 6.0 * cubic)
        gp_ref[j] = slope.astype(bf16).reshape(cut)
        acts[:, lanes] = active.astype(bf16)
        lowered.append(mm(acts[:, lanes], downs[lanes]))

    in_flight([(j, slice(j * width, (j + 1) * width)) for j in range(members)], begin, finish)
    for part in lowered:
        stream = stream + part
    for i in range(2):
        own = pl.ds(pl.multiple_of((member[0] ^ i) * width, 128), width)
        act_ref[i] = acts[:, own].reshape(cut)
    stream = stream + low_now[2:3]
    xhat, rstd = normed(stream)
    hat3_ref[...] = xhat.astype(bf16).reshape(cut)
    rstd3_ref[...] = jnp.broadcast_to(rstd, (flat[0], 128)).reshape(span, count, 128)
    final = xhat * low_now[3:4] + low_now[4:5]
    row = lax.broadcasted_iota(jnp.int32, (count, 1), 0)
    for f in range(span):
        part = jnp.where(row < patches, final[f * count : (f + 1) * count], 0.0)
        pool_ref[...] += fold(part) * frame_weight[step * span + f]


def mlp_backward(
    slots, frame_weight, member, core, patches, gathered, pool, pool_other, head, valid, targets, total,
    hid2, hat2, rstd2, hat3, rstd3, gp, act, low_rows,
    dx2_ref, keep_ref, send_ref, rows_ref, small_ref,
    ups, downs, dus, spread, up_sum, down_sum, row_sums, sems,
):
    step = pl.program_id(0)
    members = gp.shape[0]
    cut = hid2.shape
    span, count, width = cut
    flat = (span * count, width)

    @pl.when(step == 0)
    def _():
        fetch(slots, gathered, downs, sems.at[1], lambda t: 2 * t + 10, False)
        fetch(slots, gathered, ups, sems.at[0], lambda t: 2 * t + 9, True)
        pooled = jnp.sum(pool[...] + pool_other[...], axis=0, keepdims=True).astype(bf16)
        pooled8 = jnp.broadcast_to(pooled, (8, width))
        logits = mm(pooled8, head[...])
        valid_f = valid[...]
        target = targets[...]
        soft = jnp.maximum(logits, 0.0) + jnp.log(1.0 + jnp.exp(-jnp.abs(logits)))
        loss = jnp.sum(valid_f * (soft - target * logits), axis=1, keepdims=True)
        sig = 1.0 / (1.0 + jnp.exp(-logits))
        grad = (valid_f * (sig - target) / jnp.maximum(total[0], 1.0)).astype(bf16)
        spread[...] = mm_nt(grad, head[...])
        small_ref[...] = jnp.zeros_like(small_ref)
        small_ref[0:1, :] = pooled.astype(f32)
        small_ref[1:2, 0 : grad.shape[1]] = grad[0:1].astype(f32)
        small_ref[2:3, 0:128] = jnp.broadcast_to(loss[0:1], (1, 128))
        up_sum[...] = jnp.zeros_like(up_sum)
        down_sum[...] = jnp.zeros_like(down_sum)
        row_sums[...] = jnp.zeros_like(row_sums)
        arrive(downs, sems.at[1])

    low_now = low_rows[...]
    row = lax.broadcasted_iota(jnp.int32, (count, 1), 0)
    weight = jnp.concatenate(
        [jnp.where(row < patches, frame_weight[step * span + f], 0.0) for f in range(span)]
    )
    grad_final = spread[0:1] * weight
    xhat = hat3[...].reshape(flat).astype(f32)
    rstd = rstd3[...].reshape(flat[0], 128)[:, 0:1]
    row_sums[3] += fold(grad_final * xhat)
    row_sums[4] += fold(grad_final)
    grad_top = norm_back(grad_final, xhat, rstd, low_now[3:4])
    row_sums[2] += fold(grad_top)
    grad_b = grad_top.astype(bf16)

    for j in range(members):
        lanes = slice(j * width, (j + 1) * width)
        du = mm_nt(grad_b, downs[lanes]) * gp[j].reshape(flat).astype(f32)
        dus[:, lanes] = du.astype(bf16)

    @pl.when(step == 0)
    def _():
        arrive(ups, sems.at[0])

    grad_hidden = mm_nt(dus[...], ups[...])
    for i in range(2):
        own = pl.ds(pl.multiple_of((member[0] ^ i) * width, 128), width)
        up_sum[i] += mm_tn(hid2[...].reshape(flat), dus[:, own])
        down_sum[i] += mm_tn(act[i].reshape(flat), grad_b)
    xhat = hat2[...].reshape(flat).astype(f32)
    rstd = rstd2[...].reshape(flat[0], 128)[:, 0:1]
    row_sums[0] += fold(grad_hidden * xhat)
    row_sums[1] += fold(grad_hidden)
    dx2_ref[...] = (grad_top + norm_back(grad_hidden, xhat, rstd, low_now[0:1])).reshape(cut)

    @pl.when(step == pl.num_programs(0) - 1)
    def _():
        for ref, half in zip((keep_ref, send_ref), column_halves(core[0], width)):
            for i in range(2):
                ref[i, 0] = up_sum[i, :, half].astype(bf16)
                ref[i, 1] = down_sum[i, :, half].astype(bf16)
        rows_ref[...] = jnp.zeros_like(rows_ref)
        for i in range(5):
            rows_ref[i : i + 1] = jnp.sum(row_sums[i], axis=0, keepdims=True)


def close_attention(
    grad_stream, grad_b, hidden, xhat, rstd, grads, merged, rows_now, picked, ones, joint,
    joint_sum, out_sum, row_sums,
):
    grad_hidden = mm_nt(grads, joint[...])
    hidden_t = mm_nt(picked, hidden).astype(bf16) + ones
    merged_t = mm_nt(picked, merged).astype(bf16) + ones
    joint_sum[...] += mm(hidden_t, grads)
    out_sum[...] += mm(merged_t, grad_b)
    xhat = xhat.astype(f32)
    row_sums[0] += fold(grad_hidden * xhat)
    row_sums[1] += fold(grad_hidden)
    return grad_stream + norm_back(grad_hidden, xhat, rstd[:, 0:1], rows_now[0:1])


def ones_row(picked):
    row = lax.broadcasted_iota(jnp.int32, (picked.shape[0], 1), 0)
    return jnp.where(row == picked.shape[0] - 16, 1.0, 0.0).astype(bf16)


def column_halves(core, width):
    middle = width // 2
    keep = pl.ds(pl.multiple_of(core * middle, 128), middle)
    send = pl.ds(pl.multiple_of((1 - core) * middle, 128), middle)
    return keep, send


def clear(*refs):
    for ref in refs:
        ref[...] = jnp.zeros_like(ref)


def finish_attention(core, tile_refs, at, rows_ref, joint_sum, out_sum, row_sums):
    share = tile_refs[0].shape[2]
    width = out_sum.shape[1]
    rows_ref[...] = jnp.zeros_like(rows_ref)
    for tile_ref, half in zip(tile_refs, column_halves(core, width)):
        for n in range(2):
            here = slice(n * share, (n + 1) * share)
            for i in range(3):
                start = pl.multiple_of(i * width + half.start, 128)
                columns = pl.ds(start, half.size)
                tile_ref[n, at + i] = joint_sum[here, columns].astype(bf16)
            tile_ref[n, at + 3] = out_sum[here, half].astype(bf16)
    last = slice(2 * share, 2 * share + 1)
    for i in range(2):
        rows_ref[i : i + 1] = jnp.sum(row_sums[i], axis=0, keepdims=True)
    rows_ref[2:3] = joint_sum[last, :width]
    rows_ref[3:4] = joint_sum[last, 2 * width :]
    rows_ref[4:5] = out_sum[last]


def space_backward(
    slots, core, gathered, dx2, hid1, hat1, rstd1, q, k, v, o, rows, picked, extra_q, extra_k,
    g1_ref, keep_ref, send_ref, rows_ref,
    joint, out, joint_sum, out_sum, row_sums, grads, outer, sems,
):
    step = pl.program_id(0)
    cut = hid1.shape
    span, count, width = cut
    flat = (span * count, width)

    @pl.when(step == 0)
    def _():
        fetch(slots, gathered, out, sems.at[1], lambda t: t + 8, False)
        fetch(slots, gathered, joint, sems.at[0], lambda t: t + 5, True)
        clear(joint_sum, out_sum, row_sums)
        arrive(out, sems.at[1])

    grad_b = dx2[...].reshape(flat).astype(bf16)
    outer[...] = mm_nt(grad_b, out[...]).astype(bf16)

    def load(f, lanes):
        here = slice(f * count, (f + 1) * count)
        return q[f, :, lanes], k[f, :, lanes], v[f, :, lanes], outer[here, lanes]

    def store(f, lanes, *parts):
        here = slice(f * count, (f + 1) * count)
        for i, part in enumerate(parts):
            grads[here, i * width + lanes.start : i * width + lanes.stop] = part

    attend_back(span, load, store, extra_q, extra_k)
    pl.when(step == 0)(lambda: arrive(joint, sems.at[0]))
    picked_now = picked[...]
    g1_ref[...] = close_attention(
        dx2[...].reshape(flat), grad_b, hid1[...].reshape(flat), hat1[...].reshape(flat),
        rstd1[...].reshape(flat[0], 128), grads[...], o[...].reshape(flat), rows[...],
        picked_now, ones_row(picked_now), joint, joint_sum, out_sum, row_sums,
    ).astype(bf16).reshape(cut)

    @pl.when(step == pl.num_programs(0) - 1)
    def _():
        finish_attention(
            core[0], (keep_ref, send_ref), 0, rows_ref, joint_sum, out_sum, row_sums
        )


def time_backward(
    rest, slots, member, core, gathered, near, far, hid0, hat0, rstd0, q, k, v, o, pixels, rows, picked,
    extra_q, extra_k,
    keep_ref, send_ref, rows_ref, pos_ref, frame_ref,
    joint, out, joint_sum, out_sum, embed_sum, row_sums, grads, outer, sems,
):
    step = pl.program_id(0)
    frames, span, width = hid0.shape

    @pl.when(step == 0)
    def _():
        fetch(slots, gathered, out, sems.at[1], lambda t: t + 4, False)
        fetch(slots, gathered, joint, sems.at[0], lambda t: t + 1, True)
        clear(joint_sum, out_sum, embed_sum, row_sums, frame_ref)
        arrive(out, sems.at[1])

    def work(groups):
        cut = (frames, groups * GROUP, width)
        flat = (frames * groups * GROUP, width)
        small = (frames, GROUP, PAIR)
        here = slice(0, groups * GROUP)
        first = member[0] % 2 == 0
        near_now, far_now = near[:, here], far[:, here]
        grad_b = jnp.concatenate(
            [jnp.where(first, near_now, far_now), jnp.where(first, far_now, near_now)]
        ).reshape(flat)
        outer[:, here] = mm_nt(grad_b, out[...]).astype(bf16).reshape(cut)

        def load(g, lanes):
            part = slice(g * GROUP, (g + 1) * GROUP)
            return tuple(
                ref[:, part, lanes].reshape(frames * GROUP, PAIR) for ref in (q, k, v, outer)
            )

        def store(g, lanes, *parts):
            part = slice(g * GROUP, (g + 1) * GROUP)
            for i, value in enumerate(parts):
                span_now = slice(i * width + lanes.start, i * width + lanes.stop)
                grads[:, part, span_now] = value.reshape(small)

        attend_back(groups, load, store, extra_q, extra_k)
        pl.when(step == 0)(lambda: arrive(joint, sems.at[0]))
        picked_now = picked[...]
        grad = close_attention(
            grad_b.astype(f32), grad_b, hid0[:, here].reshape(flat),
            hat0[:, here].reshape(flat), rstd0[:, here].reshape(flat[0], 128),
            grads[:, here].reshape(flat[0], 3 * width), o[:, here].reshape(flat), rows[...],
            picked_now, ones_row(picked_now), joint, joint_sum, out_sum, row_sums,
        )
        pix_t = mm_nt(picked_now, pixels[:, here].reshape(flat)).astype(bf16)
        embed_sum[...] += mm(pix_t, grad.astype(bf16))
        cube = grad.reshape(cut)
        pos_ref[here] = jnp.sum(cube, axis=0)
        frame_ref[...] += jnp.sum(cube, axis=1)

    last = step == pl.num_programs(0) - 1
    if rest == 0:
        work(span // GROUP)
    else:
        odd = member[0] % 2 == 1
        pl.when(jnp.logical_not(last))(lambda: work(span // GROUP))
        pl.when(jnp.logical_and(last, jnp.logical_not(odd)))(lambda: work(rest))

        @pl.when(jnp.logical_and(last, odd))
        def _():
            pos_ref[...] = jnp.zeros_like(pos_ref)

    @pl.when(last)
    def _():
        finish_attention(
            core[0], (keep_ref, send_ref), 1, rows_ref, joint_sum, out_sum, row_sums
        )
        share = keep_ref.shape[2]
        for ref, half in zip((keep_ref, send_ref), column_halves(core[0], width)):
            for n in range(2):
                ref[n, 0] = embed_sum[n * share : (n + 1) * share, half].astype(bf16)


def pack(bits, dests, place, *refs):
    count = (len(refs) - 5) // 4
    keeps, mets, fars = (refs[i * count : (i + 1) * count] for i in range(3))
    (stay_a, go_a, stay_b, go_b), sems = refs[3 * count : 3 * count + 4], refs[-1]
    sums = refs[-1 - count : -1]
    table_rows = sums[-1].shape[1]
    slots = (stay_a.shape[1] - table_rows) // BR
    top = bits - 1
    rest = 2 ** (bits - 2) - 1

    def route(source, chunk, rows, sem):
        differs = chunk ^ place[0]
        in_b = chunk % 2 == 1
        index_a, index_b = chunk >> 2, (chunk >> 1) & rest
        moves_a, moves_b = (differs >> 1) % 2 == 1, (differs >> top) % 2 == 1
        for flag, target, index in (
            (~in_b & ~moves_a, stay_a, index_a),
            (~in_b & moves_a, go_a, index_a),
            (in_b & ~moves_b, stay_b, index_b),
            (in_b & moves_b, go_b, index_b),
        ):

            @pl.when(flag)
            def _(target=target, index=index):
                pltpu.make_async_copy(source, target.at[index, rows], sem).start()

    first = 0
    for n, (keep, met, far, source) in enumerate(zip(keeps, mets, fars, sums)):
        table = n == count - 1

        def one(i, carry, keep=keep, met=met, far=far, source=source, first=first, n=n, table=table):
            total = keep[i].astype(f32) + met[i].astype(f32) + far[i].astype(f32)
            source[i] = total.astype(bf16)
            if table:
                route(source.at[i], i, pl.ds(slots * BR, table_rows), sems.at[n])
            else:
                dest = dests[first + i]
                row = pl.multiple_of((dest % slots) * BR, 16)
                route(source.at[i], dest // slots, pl.ds(row, BR), sems.at[n])
            return carry

        lax.fori_loop(0, source.shape[0], one, 0)
        first += source.shape[0]
    for n, source in enumerate(sums):
        pltpu.make_async_copy(source, source, sems.at[n]).wait()


def swap(value, axis, hop):
    size = lax.axis_size(axis)
    return lax.ppermute(value, axis, [(i, i ^ hop) for i in range(size)])


def added(*parts):
    total = parts[0].astype(f32)
    for part in parts[1:]:
        total = total + part.astype(f32)
    return total


def halve(stay_a, go_a, stay_b, go_b, axis):
    bits = lax.axis_size(axis).bit_length() - 1
    place = lax.axis_index(axis)
    orders = [list(range(1, bits)), list(range(bits - 1, 0, -1))]
    shape = (2,) * (bits - 2) + stay_a.shape[1:]
    going, staying = [go_a, go_b], [stay_a, stay_b]
    for stage in range(bits - 1):
        met = [swap(value, axis, 1 << order[stage]) for value, order in zip(going, orders)]
        values = [added(stay, come) for stay, come in zip(staying, met)]
        if stage == bits - 2:
            return values
        going, staying = [], []
        for value, order in zip(values, orders):
            alive = sorted(order[stage + 1 :], reverse=True)
            value = value.reshape(shape[stage:])
            at = alive.index(order[stage + 1])
            bit = (place >> order[stage + 1]) & 1
            going.append(lax.dynamic_index_in_dim(value, 1 - bit, at, False).astype(bf16))
            staying.append(lax.dynamic_index_in_dim(value, bit, at, False))


def spread_four(value, axis):
    size = lax.axis_size(axis)
    place = lax.axis_index(axis)
    value = value[None]
    hop = 1
    while hop < size:
        come = swap(value, axis, hop)
        low = (place & hop) == 0
        value = jnp.concatenate(
            [jnp.where(low, value, come), jnp.where(low, come, value)], axis=0
        )
        hop *= 2
    return value


def block_ranks(owners):
    total_blocks = owners.shape[0]
    same_owner = owners[:, None] == owners[None, :]
    earlier = jnp.arange(total_blocks)[None, :] < jnp.arange(total_blocks)[:, None]
    return jnp.sum((same_owner & earlier).astype(jnp.int32), axis=1)


def adamw(weight, gradient, moment_one, moment_two, weight_decay, rate):
    first_new = beta_one * moment_one + (1.0 - beta_one) * gradient
    second_new = beta_two * moment_two + (1.0 - beta_two) * gradient * gradient
    mean_hat = first_new / (1.0 - beta_one**STEP)
    var_hat = second_new / (1.0 - beta_two**STEP)
    updated = weight - rate * (mean_hat / (jnp.sqrt(var_hat) + adam_eps) + weight_decay * weight)
    return (updated, first_new, second_new)


def local(
    pixels,
    lengths,
    frame_mask,
    time_index,
    label_valid,
    targets,
    owners,
    slot_weight,
    slot_moment1,
    slot_moment2,
    tables,
    table_moment1,
    table_moment2,
    head_weight,
    head_moment1,
    head_moment2,
):
    dp_count = lax.axis_size("dp")
    mlp_count = lax.axis_size("mlp")
    member = lax.axis_index("mlp").astype(jnp.int32)
    width = slot_weight.shape[1]
    per_tile = width // BR
    slots = slot_weight.shape[0] // BR
    shared_blocks = 9 * per_tile
    frames, patches = pixels.shape[1], pixels.shape[2]
    padded = -(-patches // GROUP) * GROUP
    groups = padded // GROUP
    classes = head_weight.shape[1]
    class_pad = -(-classes // 128) * 128
    params = pltpu.CompilerParams(vmem_limit_bytes=VMEM_BYTES)
    any_spec = pl.BlockSpec(memory_space=pl.ANY)

    gathered = lax.all_gather(slot_weight.astype(bf16), ("dp", "mlp"), axis=0, tiled=True)
    gathered = gathered.reshape(-1, BR, width)
    slot_index = (owners * slots + block_ranks(owners)).astype(jnp.int32)

    pix = jnp.pad(pixels[0], ((0, 0), (0, padded - patches), (0, 0)))
    slot_pos = jnp.arange(frames)
    frame_live = slot_pos < lengths[0]
    key_ok = frame_live & (frame_mask[0] == 1)
    allowed = key_ok[None, :] | (slot_pos[:, None] == slot_pos[None, :])
    extra_lane = jnp.arange(HEAD_DIM)
    flat_id = jnp.arange(frames * GROUP)
    frame_id, patch_id = flat_id // GROUP, flat_id % GROUP
    lane_frame = jnp.clip(extra_lane - GROUP, 0, frames - 1)
    in_patch = (extra_lane < GROUP)[None, :]
    in_frame = ((extra_lane >= GROUP) & (extra_lane < GROUP + frames))[None, :]
    same_patch = patch_id[:, None] == extra_lane[None, :]
    same_frame = frame_id[:, None] == lane_frame[None, :]
    time_q = (in_patch & same_patch) | (in_frame & same_frame)
    time_k = (in_patch & ~same_patch) | (in_frame & ~allowed.T[frame_id][:, lane_frame])
    is_pad = (jnp.arange(padded) >= patches)[:, None]
    space_q = jnp.broadcast_to(extra_lane[None, :] == 0, (padded, HEAD_DIM))
    space_k = is_pad & (extra_lane[None, :] == 0)

    def widen(flags, value):
        block = jnp.where(flags, value, 0.0).astype(bf16)
        block = jnp.pad(block, ((0, 0), (0, PAIR - HEAD_DIM)))
        return jnp.concatenate([block, block])

    time_q, time_k = widen(time_q, 1.0), widen(time_k, masked)
    space_q, space_k = widen(space_q, 1.0), widen(space_k, masked)
    time_hot = (time_index[0][:, None] == jnp.arange(TROWS)[None, :]).astype(f32)
    trow = jnp.einsum("ft,td->fd", time_hot, tables[16 + patches :], precision=highest)
    pos = jnp.pad(tables[16 : 16 + patches] + tables[0], ((0, padded - patches), (0, 0)))
    frame_weight = jnp.where(
        frame_live, 1.0 / (lengths[0] * patches).astype(f32), 0.0
    ).astype(f32)
    valid_f = label_valid.astype(f32)
    label_total = lax.psum(jnp.sum(valid_f), "dp")
    pix, label_total = lax.optimization_barrier((pix, label_total))
    share = width // mlp_count
    half = member % 2
    place = lax.axis_index("dp").astype(jnp.int32)
    core_s = (place % 2)[None]
    pick_row = jnp.arange(2 * share)
    pick_member = jnp.where(pick_row < share, member, member ^ 1)
    pick_row = pick_row % share
    pick_feature = (pick_row // BR) * (BR * mlp_count) + pick_member * BR + pick_row % BR
    picked = (pick_feature[:, None] == jnp.arange(width)[None, :]).astype(bf16)
    picked = jnp.pad(picked, ((0, 16), (0, 0)))
    member_s = member[None]
    time_rows = jnp.pad(tables[1:6], ((0, 3), (0, 0)))
    space_rows = jnp.pad(tables[6:11], ((0, 3), (0, 0)))
    low_rows = jnp.pad(tables[11:16], ((0, 3), (0, 0)))

    cube32 = jax.ShapeDtypeStruct((frames, padded, width), f32)
    cube16 = jax.ShapeDtypeStruct((frames, padded, width), bf16)
    thin32 = jax.ShapeDtypeStruct((frames, padded, 128), f32)
    row32 = jax.ShapeDtypeStruct((8, width), f32)
    group_rows = GROUPS_AT_ONCE * GROUP
    frame_rows = FRAMES_AT_ONCE * padded
    group_spec = pl.BlockSpec((frames, group_rows, width), lambda g, *_: (0, g, 0))
    group_thin = pl.BlockSpec((frames, group_rows, 128), lambda g, *_: (0, g, 0))
    patch_spec = pl.BlockSpec((group_rows, width), lambda g, *_: (g, 0))
    frame_spec = pl.BlockSpec((FRAMES_AT_ONCE, padded, width), lambda f, *_: (f, 0, 0))
    frame_thin = pl.BlockSpec((FRAMES_AT_ONCE, padded, 128), lambda f, *_: (f, 0, 0))
    gp_spec = pl.BlockSpec(
        (mlp_count, FRAMES_AT_ONCE, padded, width), lambda f, *_: (0, f, 0, 0)
    )
    time_grid = (-(-groups // GROUPS_AT_ONCE),)
    half_frames = frames // 2
    space_grid = (half_frames // FRAMES_AT_ONCE,)
    half_blocks = groups // 2 // GROUPS_AT_ONCE
    rest = groups - 2 * half_blocks * GROUPS_AT_ONCE
    half_rows = (half_blocks * GROUPS_AT_ONCE + rest) * GROUP
    back_grid = (half_blocks + (1 if rest else 0),)

    def half_index(s, m):
        ending = jnp.where(m[0] % 2 == 0, 2 * half_blocks, 2 * half_blocks - 1)
        return jnp.where(s < half_blocks, (m[0] % 2) * half_blocks + s, ending)

    back_spec = pl.BlockSpec((frames, group_rows, width), lambda s, i, m, c: (0, half_index(s, m), 0))
    back_thin = pl.BlockSpec((frames, group_rows, 128), lambda s, i, m, c: (0, half_index(s, m), 0))
    near_spec = pl.BlockSpec((half_frames, group_rows, width), lambda s, *_: (0, s, 0))
    my_frame_spec = pl.BlockSpec(
        (FRAMES_AT_ONCE, padded, width),
        lambda f, s, w, m: ((m[0] % 2) * (half_frames // FRAMES_AT_ONCE) + f, 0, 0),
    )
    act_spec = pl.BlockSpec((2, FRAMES_AT_ONCE, padded, width), lambda f, *_: (0, f, 0, 0))
    half16 = jax.ShapeDtypeStruct((half_frames, padded, width), bf16)
    half32 = jax.ShapeDtypeStruct((half_frames, padded, width), f32)
    half_thin = jax.ShapeDtypeStruct((half_frames, padded, 128), f32)
    frame_weight = lax.dynamic_slice_in_dim(frame_weight, half * half_frames, half_frames)

    def whole(*shape):
        return pl.BlockSpec(shape, lambda i, *_: (0,) * len(shape))

    rows_spec = whole(8, width)
    time_extra = whole(2 * frames * GROUP, PAIR)
    space_extra = whole(2 * padded, PAIR)
    pick_spec = whole(2 * share + 16, width)

    def call(kernel, name, units, scalars, grid, ins, in_specs, outs, out_specs, scratch):
        return pl.pallas_call(
            kernel,
            grid_spec=pltpu.PrefetchScalarGridSpec(
                num_scalar_prefetch=len(scalars),
                grid=grid,
                in_specs=[any_spec] + in_specs,
                out_specs=out_specs,
                scratch_shapes=scratch,
            ),
            out_shape=outs,
            compiler_params=params,
            cost_estimate=pl.CostEstimate(
                flops=units * 2 * frames * padded * width * width,
                bytes_accessed=16 * width * width,
                transcendentals=0,
            ),
            name=name,
        )(*scalars, gathered, *ins)

    def tile_bufs(*shapes):
        return [pltpu.VMEM((rows * width, cols * width), bf16) for rows, cols in shapes]

    x1, hid0, hat0, rstd0, q_t, k_t, v_t, o_t = call(
        partial(time_forward, groups),
        "time_forward",
        14,
        [slot_index],
        time_grid,
        [pix, pos, trow, time_rows, time_q, time_k],
        [group_spec, patch_spec, whole(frames, width), rows_spec, time_extra, time_extra],
        [cube32, cube16, cube16, thin32] + [cube16] * 4,
        [group_spec] * 3 + [group_thin] + [group_spec] * 4,
        tile_bufs((1, 1), (1, 3), (1, 1))
        + [pltpu.VMEM((frames * group_rows, width), f32), pltpu.SemaphoreType.DMA((3,))],
    )
    (hid1, hat1, rstd1, q_s, k_s, v_s, o_s, hid2, hat2, rstd2, hat3, rstd3, gp, act, pool) = call(
        lambda s, fw, m, *refs: space_forward(s, fw, m, patches, *refs),
        "space_forward",
        15,
        [slot_index, frame_weight, member_s],
        space_grid,
        [x1, space_rows, low_rows, space_q, space_k],
        [my_frame_spec, rows_spec, rows_spec, space_extra, space_extra],
        [half16, half16, half_thin]
        + [half16] * 4
        + [half16, half16, half_thin, half16, half_thin]
        + [
            jax.ShapeDtypeStruct((mlp_count, half_frames, padded, width), bf16),
            jax.ShapeDtypeStruct((2, half_frames, padded, width), bf16),
            row32,
        ],
        [frame_spec, frame_spec, frame_thin]
        + [frame_spec] * 4
        + [frame_spec, frame_spec, frame_thin, frame_spec, frame_thin]
        + [gp_spec, act_spec, rows_spec],
        tile_bufs((1, 3), (1, 1), (1, mlp_count), (mlp_count, 1))
        + [pltpu.VMEM((frame_rows, mlp_count * width), bf16), pltpu.SemaphoreType.DMA((4,))],
    )

    head_b = jnp.pad(head_weight.astype(bf16), ((0, 0), (0, class_pad - classes)))
    valid_p = jnp.pad(valid_f, ((0, 0), (0, class_pad - classes)))
    targets_p = jnp.pad(targets, ((0, 0), (0, class_pad - classes)))
    pool_other = swap(pool, "mlp", 1)
    middle = width // 2
    squares16 = jax.ShapeDtypeStruct((2, 2, width, middle), bf16)
    dx2, keep_mlp, send_mlp, rows_low, small = call(
        lambda s, fw, m, c, *refs: mlp_backward(s, fw, m, c, patches, *refs),
        "mlp_backward",
        13,
        [slot_index, frame_weight, member_s, core_s],
        space_grid,
        [
            pool, pool_other, head_b, valid_p, targets_p, label_total[None],
            hid2, hat2, rstd2, hat3, rstd3, gp, act, low_rows,
        ],
        [
            rows_spec, rows_spec, whole(width, class_pad), whole(1, class_pad), whole(1, class_pad),
            pl.BlockSpec(memory_space=pltpu.SMEM),
            frame_spec, frame_spec, frame_thin, frame_spec, frame_thin, gp_spec, act_spec,
            rows_spec,
        ],
        [half32, squares16, squares16, row32, row32],
        [frame_spec] + [whole(2, 2, width, middle)] * 2 + [rows_spec, rows_spec],
        tile_bufs((1, mlp_count), (mlp_count, 1))
        + [
            pltpu.VMEM((frame_rows, mlp_count * width), bf16),
            pltpu.VMEM((8, width), f32),
            pltpu.VMEM((2, width, width), f32),
            pltpu.VMEM((2, width, width), f32),
            pltpu.VMEM((5, 8, width), f32),
            pltpu.SemaphoreType.DMA((2,)),
        ],
    )

    sums = [
        pltpu.VMEM((2 * share + 16, 3 * width), f32),
        pltpu.VMEM((2 * share + 16, width), f32),
    ]
    met_mlp = swap(send_mlp, "dp", 1)
    g1, keep_space, send_space, rows_space = call(
        space_backward,
        "space_backward",
        16,
        [slot_index, core_s],
        space_grid,
        [dx2, hid1, hat1, rstd1, q_s, k_s, v_s, o_s, space_rows, picked, space_q, space_k],
        [frame_spec] * 3
        + [frame_thin]
        + [frame_spec] * 4
        + [rows_spec, pick_spec, space_extra, space_extra],
        [half16] + [jax.ShapeDtypeStruct((2, 4, share, middle), bf16)] * 2 + [row32],
        [frame_spec] + [whole(2, 4, share, middle)] * 2 + [rows_spec],
        tile_bufs((1, 3), (1, 1))
        + sums
        + [
            pltpu.VMEM((2, 8, width), f32),
            pltpu.VMEM((frame_rows, 3 * width), bf16),
            pltpu.VMEM((frame_rows, width), bf16),
            pltpu.SemaphoreType.DMA((2,)),
        ],
    )


    def patches_of(which):
        main = half_blocks * group_rows
        here = lax.dynamic_slice_in_dim(g1, which * main, main, 1)
        return jnp.concatenate([here, g1[:, 2 * main :]], axis=1)

    far = swap(patches_of(1 - half), "mlp", 1)
    near = patches_of(half)
    met_space = swap(send_space, "dp", 1)
    chip_mlp = added(keep_mlp[1], met_mlp[1]).astype(bf16)
    chip_space = added(keep_space[1], met_space[1]).astype(bf16)
    far, chip_mlp, chip_space = lax.optimization_barrier((far, chip_mlp, chip_space))
    far_mlp = swap(chip_mlp, "mlp", 1)
    far_space = swap(chip_space, "mlp", 1)
    keep_time, send_time, rows_time, grad_pos, grad_frames = call(
        partial(time_backward, rest),
        "time_backward",
        18,
        [slot_index, member_s, core_s],
        back_grid,
        [near, far, hid0, hat0, rstd0, q_t, k_t, v_t, o_t, pix, time_rows, picked, time_q, time_k],
        [near_spec] * 2
        + [back_spec] * 2
        + [back_thin]
        + [back_spec] * 5
        + [rows_spec, pick_spec, time_extra, time_extra],
        [jax.ShapeDtypeStruct((2, 5, share, middle), bf16)] * 2
        + [
            row32,
            jax.ShapeDtypeStruct((half_rows, width), f32),
            jax.ShapeDtypeStruct((frames, width), f32),
        ],
        [whole(2, 5, share, middle)] * 2 + [rows_spec, patch_spec, whole(frames, width)],
        tile_bufs((1, 3), (1, 1))
        + sums
        + [
            pltpu.VMEM((2 * share + 16, width), f32),
            pltpu.VMEM((2, 8, width), f32),
            pltpu.VMEM((frames, group_rows, 3 * width), bf16),
            pltpu.VMEM((frames, group_rows, width), bf16),
            pltpu.SemaphoreType.DMA((2,)),
        ],
    )

    grad_time = jnp.einsum("ft,fd->td", time_hot, grad_frames, precision=highest)
    send_time, far_mlp, far_space = lax.optimization_barrier((send_time, far_mlp, far_space))
    met_time = swap(send_time, "dp", 1)
    chip_time = added(keep_time[1], met_time[1]).astype(bf16)
    far_time = swap(chip_time, "mlp", 1)
    main = half_blocks * group_rows
    all_pos = jnp.concatenate(
        [jnp.where(half == i, grad_pos[:main], 0.0) for i in range(2)] + [grad_pos[main:]]
    )
    table_rows = tables.shape[0]
    table_part = jnp.concatenate(
        [
            jnp.sum(grad_frames, axis=0, keepdims=True),
            rows_time[:5],
            rows_space[:5],
            rows_low[:5],
            all_pos[:patches],
            grad_time,
        ]
    )
    rows_each = -(-table_rows // (dp_count * mlp_count))
    table_part = jnp.pad(
        table_part, ((0, rows_each * dp_count * mlp_count - table_rows), (0, 0))
    ).reshape(dp_count, mlp_count, rows_each, width)

    def table_of(which):
        rows_now = lax.dynamic_index_in_dim(table_part, which, 1, False).astype(bf16)
        return jnp.pad(rows_now, ((0, 0), (0, 16 - rows_each), (0, 0)))

    table_pair = jnp.stack([table_of(member), table_of(member ^ 1)])
    columns = jnp.stack([table_pair[..., :middle], table_pair[..., middle:]])
    keep_table = lax.dynamic_index_in_dim(columns, place % 2, 0, False)
    met_table = swap(lax.dynamic_index_in_dim(columns, 1 - place % 2, 0, False), "dp", 1)
    far_table = swap(added(keep_table[1], met_table[1]).astype(bf16), "mlp", 1)

    def blocks_of(*parts):
        return [part.reshape(-1, BR, middle) for part in parts]

    sources = (
        blocks_of(keep_time[0], keep_space[0], keep_mlp[0])
        + [keep_table[0]]
        + blocks_of(met_time[0], met_space[0], met_mlp[0])
        + [met_table[0]]
        + blocks_of(far_time, far_space, far_mlp)
        + [far_table]
    )
    shared_here = shared_blocks // mlp_count
    here_ids = jnp.arange(shared_here + 2 * per_tile)
    block_of = jnp.where(
        here_ids < shared_here,
        here_ids * mlp_count + member,
        here_ids - shared_here + shared_blocks + member * 2 * per_tile,
    )
    here_slots = slot_index[block_of]
    dests = (here_slots // (slots * mlp_count)) * slots + here_slots % slots
    bits = dp_count.bit_length() - 1
    chunk = jax.ShapeDtypeStruct((dp_count // 4, slots * BR + 16, middle), bf16)
    packed = pl.pallas_call(
        partial(pack, bits),
        grid_spec=pltpu.PrefetchScalarGridSpec(
            num_scalar_prefetch=2,
            grid=(1,),
            in_specs=[pl.BlockSpec(memory_space=pltpu.VMEM)] * 12,
            out_specs=[any_spec] * 4,
            scratch_shapes=[pltpu.VMEM(part.shape, bf16) for part in sources[:4]]
            + [pltpu.SemaphoreType.DMA((4,))],
        ),
        out_shape=[chunk] * 4,
        compiler_params=params,
        name="pack",
    )(dests, place[None], *sources)
    sum_a, sum_b = (value.reshape(value.shape[-2:]) for value in halve(*packed, "dp"))
    even = place % 2 == 0
    mine = jnp.where(even, sum_a, sum_b)
    met = swap(jnp.where(even, sum_b, sum_a), "dp", 1)
    summed = jnp.concatenate([jnp.where(even, mine, met), jnp.where(even, met, mine)], axis=1)
    my_slots = (place * mlp_count + member) * slots + jnp.arange(slots)
    filled = jnp.any(slot_index[:, None] == my_slots[None, :], axis=0)
    filled = jnp.repeat(filled, BR)[:, None]
    own_grad = jnp.where(filled, summed[: slots * BR], 0.0)
    squares_own = jnp.sum(own_grad * own_grad)
    block = jnp.concatenate(
        [
            jnp.pad(summed[slots * BR : slots * BR + rows_each], ((0, 7 - rows_each), (0, 0))),
            jnp.broadcast_to(squares_own, (1, width)),
            small,
        ]
    )
    blocks = jnp.concatenate(
        [spread_four(block[:8], "mlp"), block[None, 8:]], axis=0
    )
    blocks = lax.all_gather(blocks, "dp", axis=0)
    heads, blocks = blocks[:, mlp_count], blocks[:, :mlp_count]
    grad_head = jnp.einsum("cd,ck->dk", heads[:, 0], heads[:, 1, :classes], precision=highest)
    loss_sum = jnp.sum(heads[:, 2, 0])
    grad_tables = blocks[:, :, :rows_each].reshape(-1, width)[:table_rows]
    grad_norm = jnp.sqrt(
        jnp.sum(blocks[:, :, 7, 0])
        + jnp.sum(grad_tables * grad_tables)
        + jnp.sum(grad_head * grad_head)
    )
    factor = jnp.minimum(1.0, clip_max / (grad_norm + 1e-06))
    new_slots = adamw(
        slot_weight, own_grad * factor, slot_moment1, slot_moment2, decay_rate, learn_rate
    )
    new_tabs = adamw(tables, grad_tables * factor, table_moment1, table_moment2, 0.0, table_rate)
    new_heads = adamw(
        head_weight, grad_head * factor, head_moment1, head_moment2, decay_rate, learn_rate
    )
    return (
        loss_sum,
        label_total,
        grad_norm,
        new_slots[0],
        new_slots[1],
        new_slots[2],
        new_tabs[0],
        new_tabs[1],
        new_tabs[2],
        new_heads[0],
        new_heads[1],
        new_heads[2],
    )


def solution(mesh):
    return jax.shard_map(
        local,
        mesh=mesh,
        in_specs=(
            P("dp", None, None, None),
            P("dp"),
            P("dp", None),
            P("dp", None),
            P("dp", None),
            P("dp", None),
            P(),
            P(("dp", "mlp"), None),
            P(("dp", "mlp"), None),
            P(("dp", "mlp"), None),
            P(),
            P(),
            P(),
            P(),
            P(),
            P(),
        ),
        out_specs=(
            P(),
            P(),
            P(),
            P(("dp", "mlp"), None),
            P(("dp", "mlp"), None),
            P(("dp", "mlp"), None),
            P(),
            P(),
            P(),
            P(),
            P(),
            P(),
        ),
        check_vma=False,
    )
```

```python
from functools import partial

import jax
import jax.numpy as jnp
from jax import lax
from jax.experimental import pallas as pl
from jax.experimental.pallas import tpu as pltpu
from jax.sharding import PartitionSpec as P

HEADS = 12
HEAD_DIM = 64
TROWS = 8
BR = 48
STEP = 10
GROUP = 16
PAIR = 2 * HEAD_DIM
GROUPS_AT_ONCE = 2
FRAMES_AT_ONCE = 2
VMEM_BYTES = 58 * 2**20

ln_eps = 1e-06
beta_one = 0.9
beta_two = 0.999
learn_rate = 0.05
table_rate = 0.4
decay_rate = 0.05
adam_eps = 1e-08
clip_max = 0.001
highest = lax.Precision.HIGHEST
f32 = jnp.float32
bf16 = jnp.bfloat16
gelu_a = 0.7978845608028654
gelu_b = 0.044715
masked = -1e30


def mm(left, right):
    return jnp.dot(left, right, preferred_element_type=f32)


def mm_nt(left, right):
    return lax.dot_general(left, right, (((1,), (1,)), ((), ())), preferred_element_type=f32)


def mm_tn(left, right):
    return lax.dot_general(left, right, (((0,), (0,)), ((), ())), preferred_element_type=f32)


def normed(values):
    centred = values - jnp.mean(values, axis=-1, keepdims=True)
    rstd = lax.rsqrt(jnp.mean(centred * centred, axis=-1, keepdims=True) + ln_eps)
    return centred * rstd, rstd


def norm_back(grad, xhat, rstd, gain):
    scaled = grad * gain
    return rstd * (
        scaled
        - jnp.mean(scaled, axis=-1, keepdims=True)
        - xhat * jnp.mean(scaled * xhat, axis=-1, keepdims=True)
    )


def fold(values):
    return jnp.sum(values.reshape(-1, 8, values.shape[-1]), axis=0)


def low_lanes():
    lane = lax.broadcasted_iota(jnp.int32, (1, PAIR), 1)
    low = jnp.where(lane < HEAD_DIM, 1.0, 0.0)
    return low.astype(bf16), (1.0 - low).astype(bf16)


def pick_half(stacked):
    rows = stacked.shape[0] // 2
    lane = lax.broadcasted_iota(jnp.int32, (rows, PAIR), 1)
    return jnp.where(lane < HEAD_DIM, stacked[:rows], stacked[rows:])


def fetch(slots_ref, source, target, sem, first, across):
    width = source.shape[2]
    per_tile = width // BR

    def one(i, carry):
        tile, row = i // per_tile, pl.multiple_of((i % per_tile) * BR, 16)
        place = pl.ds(row, BR)
        if across:
            into = target.at[place, pl.ds(pl.multiple_of(tile * width, width), width)]
        else:
            into = target.at[pl.ds(pl.multiple_of(tile * width, 16) + row, BR)]
        block = first(tile) * per_tile + i % per_tile
        pltpu.make_async_copy(source.at[slots_ref[block]], into, sem).start()
        return carry

    count = target.shape[0] * target.shape[1] // (width * width)
    lax.fori_loop(0, count * per_tile, one, 0)


def arrive(target, sem):
    pltpu.make_async_copy(target, target, sem).wait()


def jobs_of(count):
    pairs = [slice(p * PAIR, (p + 1) * PAIR) for p in range(HEADS // 2)]
    return [(i, lanes) for i in range(count) for lanes in pairs]


def each_row(count, begin, finish):
    def one(i, carry):
        in_flight([(i, lanes) for unused, lanes in jobs_of(1)], begin, finish)
        return carry

    lax.fori_loop(0, count, one, 0)


def in_flight(jobs, begin, finish):
    waiting = None
    for job in jobs:
        started = begin(*job)
        if waiting is not None:
            finish(*waiting)
        waiting = job + started
    finish(*waiting)


def attend(count, load, store, extra_q, extra_k):
    low, high = low_lanes()

    def begin(i, lanes):
        queries, keys, values = load(i, lanes)
        both = jnp.concatenate([queries * low, queries * high], axis=0)
        scores = mm_nt(
            jnp.concatenate([both, extra_q[...]], axis=1),
            jnp.concatenate([keys, extra_k[: keys.shape[0]]], axis=1),
        )
        return values, scores

    def finish(i, lanes, values, scores):
        top = jnp.max(scores, axis=-1, keepdims=True)
        weights = jnp.exp(scores - top).astype(bf16)
        summed = mm(weights, jnp.concatenate([values, jnp.ones_like(values)], axis=1))
        merged = pick_half(summed[:, :PAIR]) / pick_half(summed[:, PAIR:])
        store(i, lanes, merged.astype(bf16))

    in_flight(jobs_of(count), begin, finish)


def attend_back(count, load, store, extra_q, extra_k, looped=False):
    low, high = low_lanes()

    def begin(i, lanes):
        queries, keys, values, grads = load(i, lanes)
        both_k = jnp.concatenate([keys * low, keys * high], axis=0)
        both_v = jnp.concatenate([values * low, values * high], axis=0)
        scores = mm_nt(
            jnp.concatenate([both_k, extra_k[...]], axis=1),
            jnp.concatenate([queries, extra_q[: queries.shape[0]]], axis=1),
        )
        return queries, both_k, grads, scores, mm_nt(both_v, grads)

    def finish(i, lanes, queries, both_k, grads, scores, back):
        rows = queries.shape[0]
        soft, inner = [], []
        for half in (slice(0, rows), slice(rows, 2 * rows)):
            part = scores[half]
            weights = jnp.exp(part - jnp.max(part, axis=0, keepdims=True))
            weights = weights * (1.0 / jnp.sum(weights, axis=0, keepdims=True))
            delta = back[half] - jnp.sum(weights * back[half], axis=0, keepdims=True)
            soft.append(weights.astype(bf16))
            inner.append((weights * delta).astype(bf16))
        soft = jnp.concatenate(soft, axis=0)
        inner = jnp.concatenate(inner, axis=0)
        store(
            i,
            lanes,
            (mm_tn(inner, both_k) * HEAD_DIM ** (-0.5)).astype(bf16),
            pick_half(mm(inner, queries)).astype(bf16),
            pick_half(mm(soft, grads)).astype(bf16),
        )

    if looped:
        each_row(count, begin, finish)
    else:
        in_flight(jobs_of(count), begin, finish)


def project(hidden, rows, tiles):
    width = hidden.shape[1]
    joint = mm(hidden, tiles[...])
    queries = (joint[:, :width] + rows[2:3]).astype(bf16) * jnp.asarray(HEAD_DIM ** (-0.5), bf16)
    keys = joint[:, width : 2 * width].astype(bf16)
    values = (joint[:, 2 * width :] + rows[3:4]).astype(bf16)
    return queries, keys, values


def keep_norm(stream, rows, at, hid_ref, hat_ref, rstd_ref, here, cut):
    xhat, rstd = normed(stream)
    hat_ref[here] = xhat.astype(bf16).reshape(cut)
    rstd_ref[here] = jnp.broadcast_to(rstd, (rstd.shape[0], 128)).reshape(cut[:-1] + (128,))
    hidden = (xhat * rows[at : at + 1] + rows[at + 1 : at + 2]).astype(bf16)
    if hid_ref is not None:
        hid_ref[here] = hidden.reshape(cut)
    return xhat, hidden


def by_groups(block, total, work):
    step = pl.program_id(0)
    full, rest = total // block, total % block
    if rest == 0:
        work(block)
    else:
        pl.when(step < full)(lambda: work(block))
        pl.when(step == full)(lambda: work(rest))


def time_forward(
    total, slots, gathered, pixels, pos, trow, rows, extra_q, extra_k,
    x1_ref, hid_ref, hat_ref, rstd_ref, q_ref, k_ref, v_ref, o_ref,
    embed, joint, out, base, sems,
):
    frames, span, width = x1_ref.shape

    @pl.when(pl.program_id(0) == 0)
    def _():
        fetch(slots, gathered, embed, sems.at[0], lambda t: t, False)
        fetch(slots, gathered, joint, sems.at[1], lambda t: t + 1, True)
        fetch(slots, gathered, out, sems.at[2], lambda t: t + 4, False)
        arrive(embed, sems.at[0])

    def first(target, sem):
        pl.when(pl.program_id(0) == 0)(lambda: arrive(target, sem))

    def work(count):
        cut = (frames, count * GROUP, width)
        flat = (frames * count * GROUP, width)
        here = slice(0, count * GROUP)
        every = (slice(None), here)
        offset = (pos[here][None] + trow[...][:, None]).reshape(flat)
        stream = mm(pixels[:, here].reshape(flat), embed[...]) + offset
        base[: flat[0]] = stream
        rows_now = rows[...]
        unused, hidden = keep_norm(stream, rows_now, 0, hid_ref, hat_ref, rstd_ref, every, cut)
        first(joint, sems.at[1])
        queries, keys, values = project(hidden, rows_now, joint)
        q_ref[:, here] = queries.reshape(cut)
        k_ref[:, here] = keys.reshape(cut)
        v_ref[:, here] = values.reshape(cut)

        def load(g, lanes):
            part = slice(g * GROUP, (g + 1) * GROUP)
            return tuple(
                ref[:, part, lanes].reshape(frames * GROUP, PAIR) for ref in (q_ref, k_ref, v_ref)
            )

        def store(g, lanes, merged):
            part = slice(g * GROUP, (g + 1) * GROUP)
            o_ref[:, part, lanes] = merged.reshape(frames, GROUP, PAIR)

        attend(count, load, store, extra_q, extra_k)
        first(out, sems.at[2])
        merged = o_ref[:, here].reshape(flat)
        stream = base[: flat[0]] + mm(merged, out[...]) + rows_now[4:5]
        x1_ref[:, here] = stream.reshape(cut)

    by_groups(span // GROUP, total, work)


def space_forward(
    slots, frame_weight, member, patches, gathered, x1, rows, low_rows, extra_q, extra_k,
    hid1_ref, hat1_ref, rstd1_ref, q_ref, k_ref, v_ref, o_ref,
    hid2_ref, hat2_ref, rstd2_ref, hat3_ref, rstd3_ref, gp_ref, act_ref, pool_ref,
    joint, out, ups, downs, acts, sems,
):
    step = pl.program_id(0)
    members = gp_ref.shape[0]
    cut = x1.shape
    span, count, width = cut
    flat = (span * count, width)
    every = (slice(None),)

    @pl.when(step == 0)
    def _():
        fetch(slots, gathered, joint, sems.at[0], lambda t: t + 5, True)
        fetch(slots, gathered, out, sems.at[1], lambda t: t + 8, False)
        fetch(slots, gathered, ups, sems.at[2], lambda t: 2 * t + 9, True)
        fetch(slots, gathered, downs, sems.at[3], lambda t: 2 * t + 10, False)
        pool_ref[...] = jnp.zeros_like(pool_ref)
        arrive(joint, sems.at[0])

    rows_now = rows[...]
    unused, hidden = keep_norm(
        x1[...].reshape(flat), rows_now, 0, hid1_ref, hat1_ref, rstd1_ref, every, cut
    )
    queries, keys, values = project(hidden, rows_now, joint)
    q_ref[...] = queries.reshape(cut)
    k_ref[...] = keys.reshape(cut)
    v_ref[...] = values.reshape(cut)

    def load(f, lanes):
        return q_ref[f, :, lanes], k_ref[f, :, lanes], v_ref[f, :, lanes]

    def store(f, lanes, merged):
        o_ref[f, :, lanes] = merged

    attend(span, load, store, extra_q, extra_k)
    pl.when(step == 0)(lambda: arrive(out, sems.at[1]))
    merged = o_ref[...].reshape(flat)
    stream = x1[...].reshape(flat) + mm(merged, out[...]) + rows_now[4:5]
    low_now = low_rows[...]
    unused, hidden = keep_norm(stream, low_now, 0, hid2_ref, hat2_ref, rstd2_ref, every, cut)

    @pl.when(step == 0)
    def _():
        arrive(ups, sems.at[2])
        arrive(downs, sems.at[3])

    def begin(j, lanes):
        return (mm(hidden, ups[:, lanes]),)

    lowered = []

    def finish(j, lanes, upper):
        cubic = gelu_a * gelu_b * (upper * upper)
        gate = 0.5 + 0.5 * jnp.tanh(upper * (gelu_a + cubic))
        active = upper * gate
        slope = gate + active * (1.0 - gate) * (2.0 * gelu_a + 6.0 * cubic)
        gp_ref[j] = slope.astype(bf16).reshape(cut)
        acts[:, lanes] = active.astype(bf16)
        lowered.append(mm(acts[:, lanes], downs[lanes]))

    in_flight([(j, slice(j * width, (j + 1) * width)) for j in range(members)], begin, finish)
    for part in lowered:
        stream = stream + part
    for i in range(2):
        own = pl.ds(pl.multiple_of((member[0] ^ i) * width, 128), width)
        act_ref[i] = acts[:, own].reshape(cut)
    stream = stream + low_now[2:3]
    xhat, rstd = normed(stream)
    hat3_ref[...] = xhat.astype(bf16).reshape(cut)
    rstd3_ref[...] = jnp.broadcast_to(rstd, (flat[0], 128)).reshape(span, count, 128)
    final = xhat * low_now[3:4] + low_now[4:5]
    row = lax.broadcasted_iota(jnp.int32, (count, 1), 0)
    for f in range(span):
        part = jnp.where(row < patches, final[f * count : (f + 1) * count], 0.0)
        pool_ref[...] += fold(part) * frame_weight[step * span + f]


def mlp_backward(
    slots, frame_weight, member, patches, gathered, pool, pool_other, head, valid, targets, total,
    hat2, rstd2, hat3, rstd3, gp, low_rows,
    dx2_ref, g3_ref, du_ref, rows_ref, small_ref,
    ups, downs, dus, spread, row_sums, sems,
):
    step = pl.program_id(0)
    members = gp.shape[0]
    cut = hat2.shape
    span, count, width = cut
    flat = (span * count, width)

    @pl.when(step == 0)
    def _():
        fetch(slots, gathered, downs, sems.at[1], lambda t: 2 * t + 10, False)
        fetch(slots, gathered, ups, sems.at[0], lambda t: 2 * t + 9, True)
        pooled = jnp.sum(pool[...] + pool_other[...], axis=0, keepdims=True).astype(bf16)
        pooled8 = jnp.broadcast_to(pooled, (8, width))
        logits = mm(pooled8, head[...])
        valid_f = valid[...]
        target = targets[...]
        soft = jnp.maximum(logits, 0.0) + jnp.log(1.0 + jnp.exp(-jnp.abs(logits)))
        loss = jnp.sum(valid_f * (soft - target * logits), axis=1, keepdims=True)
        sig = 1.0 / (1.0 + jnp.exp(-logits))
        grad = (valid_f * (sig - target) / jnp.maximum(total[0], 1.0)).astype(bf16)
        spread[...] = mm_nt(grad, head[...])
        small_ref[...] = jnp.zeros_like(small_ref)
        small_ref[0:1, :] = pooled.astype(f32)
        small_ref[1:2, 0 : grad.shape[1]] = grad[0:1].astype(f32)
        small_ref[2:3, 0:128] = jnp.broadcast_to(loss[0:1], (1, 128))
        row_sums[...] = jnp.zeros_like(row_sums)
        arrive(downs, sems.at[1])

    low_now = low_rows[...]
    row = lax.broadcasted_iota(jnp.int32, (count, 1), 0)
    weight = jnp.concatenate(
        [jnp.where(row < patches, frame_weight[step * span + f], 0.0) for f in range(span)]
    )
    grad_final = spread[0:1] * weight
    xhat = hat3[...].reshape(flat).astype(f32)
    rstd = rstd3[...].reshape(flat[0], 128)[:, 0:1]
    row_sums[3] += fold(grad_final * xhat)
    row_sums[4] += fold(grad_final)
    grad_top = norm_back(grad_final, xhat, rstd, low_now[3:4])
    row_sums[2] += fold(grad_top)
    grad_b = grad_top.astype(bf16)
    g3_ref[...] = grad_b.reshape(cut)

    for j in range(members):
        lanes = slice(j * width, (j + 1) * width)
        du = mm_nt(grad_b, downs[lanes]) * gp[j].reshape(flat).astype(f32)
        dus[:, lanes] = du.astype(bf16)

    @pl.when(step == 0)
    def _():
        arrive(ups, sems.at[0])

    grad_hidden = mm_nt(dus[...], ups[...])
    for i in range(2):
        own = pl.ds(pl.multiple_of((member[0] ^ i) * width, 128), width)
        du_ref[i] = dus[:, own].reshape(cut)
    xhat = hat2[...].reshape(flat).astype(f32)
    rstd = rstd2[...].reshape(flat[0], 128)[:, 0:1]
    row_sums[0] += fold(grad_hidden * xhat)
    row_sums[1] += fold(grad_hidden)
    dx2_ref[...] = (grad_top + norm_back(grad_hidden, xhat, rstd, low_now[0:1])).reshape(cut)

    @pl.when(step == pl.num_programs(0) - 1)
    def _():
        rows_ref[...] = jnp.zeros_like(rows_ref)
        for i in range(5):
            rows_ref[i : i + 1] = jnp.sum(row_sums[i], axis=0, keepdims=True)


def mlp_weights(core, hid2, g3, du, act, keep_ref, send_ref, sums):
    rows, width = hid2.shape[0] * hid2.shape[1], hid2.shape[2]
    sums[0] = mm_tn(hid2[...].reshape(rows, width), du[0].reshape(rows, width))
    sums[1] = mm_tn(act[0].reshape(rows, width), g3[...].reshape(rows, width))
    for ref, half in zip((keep_ref, send_ref), column_halves(core[0], width)):
        for n in range(2):
            ref[0, n] = sums[n, :, half].astype(bf16)


def space_weights(core, picked, hid1, o, grads, keep_ref, send_ref, rows_ref, left, sums):
    step = pl.program_id(0)
    rows, width = hid1.shape[0] * hid1.shape[1], hid1.shape[2]
    share = keep_ref.shape[2]

    def select(source):
        chosen = mm_nt(picked[...], source[...].reshape(rows, width)).astype(bf16)
        left[...] = chosen + ones_row(picked)

    pl.when(step == 0)(lambda: select(hid1))
    pl.when(step == pl.num_programs(0) - 1)(lambda: select(o))
    sums[...] = mm(left[...], grads[...].reshape(rows, width))
    for ref, half in zip((keep_ref, send_ref), column_halves(core[0], width)):
        for n in range(2):
            ref[n, 0] = sums[n * share : (n + 1) * share, half].astype(bf16)
    rows_ref[0] = sums[2 * share : 2 * share + 8]


def close_attention(
    grad_stream, grad_b, hidden, xhat, rstd, grads, merged, rows_now, picked, ones, joint,
    joint_sum, out_sum, row_sums,
):
    grad_hidden = mm_nt(grads, joint[...])
    hidden_t = mm_nt(picked, hidden).astype(bf16) + ones
    merged_t = mm_nt(picked, merged).astype(bf16) + ones
    joint_sum[...] += mm(hidden_t, grads)
    out_sum[...] += mm(merged_t, grad_b)
    xhat = xhat.astype(f32)
    row_sums[0] += fold(grad_hidden * xhat)
    row_sums[1] += fold(grad_hidden)
    return grad_stream + norm_back(grad_hidden, xhat, rstd[:, 0:1], rows_now[0:1])


def ones_row(picked):
    row = lax.broadcasted_iota(jnp.int32, (picked.shape[0], 1), 0)
    return jnp.where(row == picked.shape[0] - 16, 1.0, 0.0).astype(bf16)


def column_halves(core, width):
    middle = width // 2
    keep = pl.ds(pl.multiple_of(core * middle, 128), middle)
    send = pl.ds(pl.multiple_of((1 - core) * middle, 128), middle)
    return keep, send


def clear(*refs):
    for ref in refs:
        ref[...] = jnp.zeros_like(ref)


def finish_attention(core, tile_refs, at, rows_ref, joint_sum, out_sum, row_sums):
    share = tile_refs[0].shape[2]
    width = out_sum.shape[1]
    rows_ref[...] = jnp.zeros_like(rows_ref)
    for tile_ref, half in zip(tile_refs, column_halves(core, width)):
        for n in range(2):
            here = slice(n * share, (n + 1) * share)
            for i in range(3):
                start = pl.multiple_of(i * width + half.start, 128)
                columns = pl.ds(start, half.size)
                tile_ref[n, at + i] = joint_sum[here, columns].astype(bf16)
            tile_ref[n, at + 3] = out_sum[here, half].astype(bf16)
    last = slice(2 * share, 2 * share + 1)
    for i in range(2):
        rows_ref[i : i + 1] = jnp.sum(row_sums[i], axis=0, keepdims=True)
    rows_ref[2:3] = joint_sum[last, :width]
    rows_ref[3:4] = joint_sum[last, 2 * width :]
    rows_ref[4:5] = out_sum[last]


def space_backward(
    slots, gathered, dx2, hat1, rstd1, q, k, v, rows, extra_q, extra_k,
    g1_ref, grads_ref, rows_ref, joint, out, row_sums, outer, sems,
):
    step = pl.program_id(0)
    cut = hat1.shape
    span, count, width = cut
    flat = (span * count, width)

    @pl.when(step == 0)
    def _():
        fetch(slots, gathered, out, sems.at[1], lambda t: t + 8, False)
        fetch(slots, gathered, joint, sems.at[0], lambda t: t + 5, True)
        clear(row_sums)
        arrive(out, sems.at[1])

    grad_b = dx2[...].reshape(flat).astype(bf16)
    grads_ref[:, :, 3 * width :] = grad_b.reshape(cut)
    outer[...] = mm_nt(grad_b, out[...]).astype(bf16)

    def load(f, lanes):
        here = pl.ds(pl.multiple_of(f * count, 16), count)
        return q[f, :, lanes], k[f, :, lanes], v[f, :, lanes], outer[here, lanes]

    def store(f, lanes, *parts):
        for i, part in enumerate(parts):
            grads_ref[f, :, i * width + lanes.start : i * width + lanes.stop] = part

    attend_back(span, load, store, extra_q, extra_k, looped=True)
    pl.when(step == 0)(lambda: arrive(joint, sems.at[0]))
    grads = grads_ref[:, :, : 3 * width].reshape(flat[0], 3 * width)
    grad_hidden = mm_nt(grads, joint[...])
    xhat = hat1[...].reshape(flat).astype(f32)
    rstd = rstd1[...].reshape(flat[0], 128)[:, 0:1]
    row_sums[0] += fold(grad_hidden * xhat)
    row_sums[1] += fold(grad_hidden)
    grad_stream = dx2[...].reshape(flat) + norm_back(grad_hidden, xhat, rstd, rows[0:1])
    g1_ref[...] = grad_stream.astype(bf16).reshape(cut)

    @pl.when(step == pl.num_programs(0) - 1)
    def _():
        rows_ref[...] = jnp.zeros_like(rows_ref)
        for i in range(2):
            rows_ref[i : i + 1] = jnp.sum(row_sums[i], axis=0, keepdims=True)


def time_backward(
    rest, slots, member, core, gathered, near, far, hid0, hat0, rstd0, q, k, v, o, pixels, rows, picked,
    extra_q, extra_k,
    keep_ref, send_ref, rows_ref, pos_ref, frame_ref,
    joint, out, joint_sum, out_sum, embed_sum, row_sums, grads, outer, sems,
):
    step = pl.program_id(0)
    frames, span, width = hid0.shape

    @pl.when(step == 0)
    def _():
        fetch(slots, gathered, out, sems.at[1], lambda t: t + 4, False)
        fetch(slots, gathered, joint, sems.at[0], lambda t: t + 1, True)
        clear(joint_sum, out_sum, embed_sum, row_sums, frame_ref)
        arrive(out, sems.at[1])

    def work(groups):
        cut = (frames, groups * GROUP, width)
        flat = (frames * groups * GROUP, width)
        small = (frames, GROUP, PAIR)
        here = slice(0, groups * GROUP)
        first = member[0] % 2 == 0
        near_now, far_now = near[:, here], far[:, here]
        grad_b = jnp.concatenate(
            [jnp.where(first, near_now, far_now), jnp.where(first, far_now, near_now)]
        ).reshape(flat)
        outer[:, here] = mm_nt(grad_b, out[...]).astype(bf16).reshape(cut)

        def load(g, lanes):
            part = slice(g * GROUP, (g + 1) * GROUP)
            return tuple(
                ref[:, part, lanes].reshape(frames * GROUP, PAIR) for ref in (q, k, v, outer)
            )

        def store(g, lanes, *parts):
            part = slice(g * GROUP, (g + 1) * GROUP)
            for i, value in enumerate(parts):
                span_now = slice(i * width + lanes.start, i * width + lanes.stop)
                grads[:, part, span_now] = value.reshape(small)

        attend_back(groups, load, store, extra_q, extra_k)
        pl.when(step == 0)(lambda: arrive(joint, sems.at[0]))
        picked_now = picked[...]
        grad = close_attention(
            grad_b.astype(f32), grad_b, hid0[:, here].reshape(flat),
            hat0[:, here].reshape(flat), rstd0[:, here].reshape(flat[0], 128),
            grads[:, here].reshape(flat[0], 3 * width), o[:, here].reshape(flat), rows[...],
            picked_now, ones_row(picked_now), joint, joint_sum, out_sum, row_sums,
        )
        pix_t = mm_nt(picked_now, pixels[:, here].reshape(flat)).astype(bf16)
        embed_sum[...] += mm(pix_t, grad.astype(bf16))
        cube = grad.reshape(cut)
        pos_ref[here] = jnp.sum(cube, axis=0)
        frame_ref[...] += jnp.sum(cube, axis=1)

    last = step == pl.num_programs(0) - 1
    if rest == 0:
        work(span // GROUP)
    else:
        odd = member[0] % 2 == 1
        pl.when(jnp.logical_not(last))(lambda: work(span // GROUP))
        pl.when(jnp.logical_and(last, jnp.logical_not(odd)))(lambda: work(rest))

        @pl.when(jnp.logical_and(last, odd))
        def _():
            pos_ref[...] = jnp.zeros_like(pos_ref)

    @pl.when(last)
    def _():
        finish_attention(
            core[0], (keep_ref, send_ref), 1, rows_ref, joint_sum, out_sum, row_sums
        )
        share = keep_ref.shape[2]
        for ref, half in zip((keep_ref, send_ref), column_halves(core[0], width)):
            for n in range(2):
                ref[n, 0] = embed_sum[n * share : (n + 1) * share, half].astype(bf16)


def pack(bits, dests, place, *refs):
    count = (len(refs) - 5) // 4
    keeps, mets, fars = (refs[i * count : (i + 1) * count] for i in range(3))
    (stay_a, go_a, stay_b, go_b), sems = refs[3 * count : 3 * count + 4], refs[-1]
    sums = refs[-1 - count : -1]
    table_rows = sums[-1].shape[1]
    slots = (stay_a.shape[1] - table_rows) // BR
    top = bits - 1
    rest = 2 ** (bits - 2) - 1

    def route(source, chunk, rows, sem):
        differs = chunk ^ place[0]
        in_b = chunk % 2 == 1
        index_a, index_b = chunk >> 2, (chunk >> 1) & rest
        moves_a, moves_b = (differs >> 1) % 2 == 1, (differs >> top) % 2 == 1
        for flag, target, index in (
            (~in_b & ~moves_a, stay_a, index_a),
            (~in_b & moves_a, go_a, index_a),
            (in_b & ~moves_b, stay_b, index_b),
            (in_b & moves_b, go_b, index_b),
        ):

            @pl.when(flag)
            def _(target=target, index=index):
                pltpu.make_async_copy(source, target.at[index, rows], sem).start()

    first = 0
    for n, (keep, met, far, source) in enumerate(zip(keeps, mets, fars, sums)):
        table = n == count - 1

        def one(i, carry, keep=keep, met=met, far=far, source=source, first=first, n=n, table=table):
            total = keep[0, i].astype(f32) + met[0, i].astype(f32) + far[i].astype(f32)
            source[i] = total.astype(bf16)
            if table:
                route(source.at[i], i, pl.ds(slots * BR, table_rows), sems.at[n])
            else:
                dest = dests[first + i]
                row = pl.multiple_of((dest % slots) * BR, 16)
                route(source.at[i], dest // slots, pl.ds(row, BR), sems.at[n])
            return carry

        lax.fori_loop(0, source.shape[0], one, 0)
        first += source.shape[0]
    for n, source in enumerate(sums):
        pltpu.make_async_copy(source, source, sems.at[n]).wait()


def swap(value, axis, hop):
    size = lax.axis_size(axis)
    return lax.ppermute(value, axis, [(i, i ^ hop) for i in range(size)])


def added(*parts):
    total = parts[0].astype(f32)
    for part in parts[1:]:
        total = total + part.astype(f32)
    return total


def halve(stay_a, go_a, stay_b, go_b, axis):
    bits = lax.axis_size(axis).bit_length() - 1
    place = lax.axis_index(axis)
    orders = [list(range(1, bits)), list(range(bits - 1, 0, -1))]
    shape = (2,) * (bits - 2) + stay_a.shape[1:]
    going, staying = [go_a, go_b], [stay_a, stay_b]
    for stage in range(bits - 1):
        met = [swap(value, axis, 1 << order[stage]) for value, order in zip(going, orders)]
        values = [added(stay, come) for stay, come in zip(staying, met)]
        if stage == bits - 2:
            return values
        going, staying = [], []
        for value, order in zip(values, orders):
            alive = sorted(order[stage + 1 :], reverse=True)
            value = value.reshape(shape[stage:])
            at = alive.index(order[stage + 1])
            bit = (place >> order[stage + 1]) & 1
            going.append(lax.dynamic_index_in_dim(value, 1 - bit, at, False).astype(bf16))
            staying.append(lax.dynamic_index_in_dim(value, bit, at, False))


def spread_four(value, axis):
    size = lax.axis_size(axis)
    place = lax.axis_index(axis)
    value = value[None]
    hop = 1
    while hop < size:
        come = swap(value, axis, hop)
        low = (place & hop) == 0
        value = jnp.concatenate(
            [jnp.where(low, value, come), jnp.where(low, come, value)], axis=0
        )
        hop *= 2
    return value


def block_ranks(owners):
    total_blocks = owners.shape[0]
    same_owner = owners[:, None] == owners[None, :]
    earlier = jnp.arange(total_blocks)[None, :] < jnp.arange(total_blocks)[:, None]
    return jnp.sum((same_owner & earlier).astype(jnp.int32), axis=1)


def adamw(weight, gradient, moment_one, moment_two, weight_decay, rate):
    first_new = beta_one * moment_one + (1.0 - beta_one) * gradient
    second_new = beta_two * moment_two + (1.0 - beta_two) * gradient * gradient
    mean_hat = first_new / (1.0 - beta_one**STEP)
    var_hat = second_new / (1.0 - beta_two**STEP)
    updated = weight - rate * (mean_hat / (jnp.sqrt(var_hat) + adam_eps) + weight_decay * weight)
    return (updated, first_new, second_new)


def local(
    pixels,
    lengths,
    frame_mask,
    time_index,
    label_valid,
    targets,
    owners,
    slot_weight,
    slot_moment1,
    slot_moment2,
    tables,
    table_moment1,
    table_moment2,
    head_weight,
    head_moment1,
    head_moment2,
):
    dp_count = lax.axis_size("dp")
    mlp_count = lax.axis_size("mlp")
    member = lax.axis_index("mlp").astype(jnp.int32)
    width = slot_weight.shape[1]
    per_tile = width // BR
    slots = slot_weight.shape[0] // BR
    shared_blocks = 9 * per_tile
    frames, patches = pixels.shape[1], pixels.shape[2]
    padded = -(-patches // GROUP) * GROUP
    groups = padded // GROUP
    classes = head_weight.shape[1]
    class_pad = -(-classes // 128) * 128
    params = pltpu.CompilerParams(vmem_limit_bytes=VMEM_BYTES)
    any_spec = pl.BlockSpec(memory_space=pl.ANY)

    gathered = lax.all_gather(slot_weight.astype(bf16), ("dp", "mlp"), axis=0, tiled=True)
    gathered = gathered.reshape(-1, BR, width)
    slot_index = (owners * slots + block_ranks(owners)).astype(jnp.int32)

    pix = jnp.pad(pixels[0], ((0, 0), (0, padded - patches), (0, 0)))
    slot_pos = jnp.arange(frames)
    frame_live = slot_pos < lengths[0]
    key_ok = frame_live & (frame_mask[0] == 1)
    allowed = key_ok[None, :] | (slot_pos[:, None] == slot_pos[None, :])
    extra_lane = jnp.arange(HEAD_DIM)
    flat_id = jnp.arange(frames * GROUP)
    frame_id, patch_id = flat_id // GROUP, flat_id % GROUP
    lane_frame = jnp.clip(extra_lane - GROUP, 0, frames - 1)
    in_patch = (extra_lane < GROUP)[None, :]
    in_frame = ((extra_lane >= GROUP) & (extra_lane < GROUP + frames))[None, :]
    same_patch = patch_id[:, None] == extra_lane[None, :]
    same_frame = frame_id[:, None] == lane_frame[None, :]
    time_q = (in_patch & same_patch) | (in_frame & same_frame)
    time_k = (in_patch & ~same_patch) | (in_frame & ~allowed.T[frame_id][:, lane_frame])
    is_pad = (jnp.arange(padded) >= patches)[:, None]
    space_q = jnp.broadcast_to(extra_lane[None, :] == 0, (padded, HEAD_DIM))
    space_k = is_pad & (extra_lane[None, :] == 0)

    def widen(flags, value):
        block = jnp.where(flags, value, 0.0).astype(bf16)
        block = jnp.pad(block, ((0, 0), (0, PAIR - HEAD_DIM)))
        return jnp.concatenate([block, block])

    time_q, time_k = widen(time_q, 1.0), widen(time_k, masked)
    space_q, space_k = widen(space_q, 1.0), widen(space_k, masked)
    time_hot = (time_index[0][:, None] == jnp.arange(TROWS)[None, :]).astype(f32)
    trow = jnp.einsum("ft,td->fd", time_hot, tables[16 + patches :], precision=highest)
    pos = jnp.pad(tables[16 : 16 + patches] + tables[0], ((0, padded - patches), (0, 0)))
    frame_weight = jnp.where(
        frame_live, 1.0 / (lengths[0] * patches).astype(f32), 0.0
    ).astype(f32)
    valid_f = label_valid.astype(f32)
    label_total = lax.psum(jnp.sum(valid_f), "dp")
    head_b = jnp.pad(head_weight.astype(bf16), ((0, 0), (0, class_pad - classes)))
    valid_p = jnp.pad(valid_f, ((0, 0), (0, class_pad - classes)))
    targets_p = jnp.pad(targets, ((0, 0), (0, class_pad - classes)))
    share = width // mlp_count
    half = member % 2
    place = lax.axis_index("dp").astype(jnp.int32)
    core_s = (place % 2)[None]
    pick_row = jnp.arange(2 * share)
    pick_member = jnp.where(pick_row < share, member, member ^ 1)
    pick_row = pick_row % share
    pick_feature = (pick_row // BR) * (BR * mlp_count) + pick_member * BR + pick_row % BR
    picked = (pick_feature[:, None] == jnp.arange(width)[None, :]).astype(bf16)
    picked = jnp.pad(picked, ((0, 16), (0, 0)))
    member_s = member[None]
    time_rows = jnp.pad(tables[1:6], ((0, 3), (0, 0)))
    space_rows = jnp.pad(tables[6:11], ((0, 3), (0, 0)))
    low_rows = jnp.pad(tables[11:16], ((0, 3), (0, 0)))

    shared_here = shared_blocks // mlp_count
    here_ids = jnp.arange(shared_here + 2 * per_tile)
    block_of = jnp.where(
        here_ids < shared_here,
        here_ids * mlp_count + member,
        here_ids - shared_here + shared_blocks + member * 2 * per_tile,
    )
    here_slots = slot_index[block_of]
    dests = (here_slots // (slots * mlp_count)) * slots + here_slots % slots
    pix, label_total, head_b, valid_p, targets_p, picked, dests = lax.optimization_barrier(
        (pix, label_total, head_b, valid_p, targets_p, picked, dests)
    )
    cube32 = jax.ShapeDtypeStruct((frames, padded, width), f32)
    cube16 = jax.ShapeDtypeStruct((frames, padded, width), bf16)
    thin32 = jax.ShapeDtypeStruct((frames, padded, 128), f32)
    row32 = jax.ShapeDtypeStruct((8, width), f32)
    group_rows = GROUPS_AT_ONCE * GROUP
    frame_rows = FRAMES_AT_ONCE * padded
    group_spec = pl.BlockSpec((frames, group_rows, width), lambda g, *_: (0, g, 0))
    group_thin = pl.BlockSpec((frames, group_rows, 128), lambda g, *_: (0, g, 0))
    patch_spec = pl.BlockSpec((group_rows, width), lambda g, *_: (g, 0))
    frame_spec = pl.BlockSpec((FRAMES_AT_ONCE, padded, width), lambda f, *_: (f, 0, 0))
    frame_thin = pl.BlockSpec((FRAMES_AT_ONCE, padded, 128), lambda f, *_: (f, 0, 0))
    gp_spec = pl.BlockSpec(
        (mlp_count, FRAMES_AT_ONCE, padded, width), lambda f, *_: (0, f, 0, 0)
    )
    time_grid = (-(-groups // GROUPS_AT_ONCE),)
    half_frames = frames // 2
    space_grid = (half_frames // FRAMES_AT_ONCE,)
    half_blocks = groups // 2 // GROUPS_AT_ONCE
    rest = groups - 2 * half_blocks * GROUPS_AT_ONCE
    half_rows = (half_blocks * GROUPS_AT_ONCE + rest) * GROUP
    back_grid = (half_blocks + (1 if rest else 0),)

    def half_index(s, m):
        ending = jnp.where(m[0] % 2 == 0, 2 * half_blocks, 2 * half_blocks - 1)
        return jnp.where(s < half_blocks, (m[0] % 2) * half_blocks + s, ending)

    back_spec = pl.BlockSpec((frames, group_rows, width), lambda s, i, m, c: (0, half_index(s, m), 0))
    back_thin = pl.BlockSpec((frames, group_rows, 128), lambda s, i, m, c: (0, half_index(s, m), 0))
    near_spec = pl.BlockSpec((half_frames, group_rows, width), lambda s, *_: (0, s, 0))
    my_frame_spec = pl.BlockSpec(
        (FRAMES_AT_ONCE, padded, width),
        lambda f, s, w, m: ((m[0] % 2) * (half_frames // FRAMES_AT_ONCE) + f, 0, 0),
    )
    act_spec = pl.BlockSpec((2, FRAMES_AT_ONCE, padded, width), lambda f, *_: (0, f, 0, 0))
    half16 = jax.ShapeDtypeStruct((half_frames, padded, width), bf16)
    half32 = jax.ShapeDtypeStruct((half_frames, padded, width), f32)
    half_thin = jax.ShapeDtypeStruct((half_frames, padded, 128), f32)
    frame_weight = lax.dynamic_slice_in_dim(frame_weight, half * half_frames, half_frames)

    def whole(*shape):
        return pl.BlockSpec(shape, lambda i, *_: (0,) * len(shape))

    rows_spec = whole(8, width)
    time_extra = whole(2 * frames * GROUP, PAIR)
    space_extra = whole(2 * padded, PAIR)
    pick_spec = whole(2 * share + 16, width)

    def call(
        kernel, name, units, scalars, grid, ins, in_specs, outs, out_specs, scratch, tiles=True
    ):
        return pl.pallas_call(
            kernel,
            grid_spec=pltpu.PrefetchScalarGridSpec(
                num_scalar_prefetch=len(scalars),
                grid=grid,
                in_specs=([any_spec] if tiles else []) + in_specs,
                out_specs=out_specs,
                scratch_shapes=scratch,
            ),
            out_shape=outs,
            compiler_params=params,
            cost_estimate=pl.CostEstimate(
                flops=units * 2 * frames * padded * width * width,
                bytes_accessed=16 * width * width,
                transcendentals=0,
            ),
            name=name,
        )(*scalars, *([gathered] if tiles else []), *ins)

    def tile_bufs(*shapes):
        return [pltpu.VMEM((rows * width, cols * width), bf16) for rows, cols in shapes]

    x1, hid0, hat0, rstd0, q_t, k_t, v_t, o_t = call(
        partial(time_forward, groups),
        "time_forward",
        14,
        [slot_index],
        time_grid,
        [pix, pos, trow, time_rows, time_q, time_k],
        [group_spec, patch_spec, whole(frames, width), rows_spec, time_extra, time_extra],
        [cube32, cube16, cube16, thin32] + [cube16] * 4,
        [group_spec] * 3 + [group_thin] + [group_spec] * 4,
        tile_bufs((1, 1), (1, 3), (1, 1))
        + [pltpu.VMEM((frames * group_rows, width), f32), pltpu.SemaphoreType.DMA((3,))],
    )
    (hid1, hat1, rstd1, q_s, k_s, v_s, o_s, hid2, hat2, rstd2, hat3, rstd3, gp, act, pool) = call(
        lambda s, fw, m, *refs: space_forward(s, fw, m, patches, *refs),
        "space_forward",
        15,
        [slot_index, frame_weight, member_s],
        space_grid,
        [x1, space_rows, low_rows, space_q, space_k],
        [my_frame_spec, rows_spec, rows_spec, space_extra, space_extra],
        [half16, half16, half_thin]
        + [half16] * 4
        + [half16, half16, half_thin, half16, half_thin]
        + [
            jax.ShapeDtypeStruct((mlp_count, half_frames, padded, width), bf16),
            jax.ShapeDtypeStruct((2, half_frames, padded, width), bf16),
            row32,
        ],
        [frame_spec, frame_spec, frame_thin]
        + [frame_spec] * 4
        + [frame_spec, frame_spec, frame_thin, frame_spec, frame_thin]
        + [gp_spec, act_spec, rows_spec],
        tile_bufs((1, 3), (1, 1), (1, mlp_count), (mlp_count, 1))
        + [pltpu.VMEM((frame_rows, mlp_count * width), bf16), pltpu.SemaphoreType.DMA((4,))],
    )

    pool_other = swap(pool, "mlp", 1)
    middle = width // 2
    squares16 = jax.ShapeDtypeStruct((2, 2, width, middle), bf16)
    pair16 = jax.ShapeDtypeStruct((2, half_frames, padded, width), bf16)
    dx2, g3, du, rows_low, small = call(
        lambda s, fw, m, *refs: mlp_backward(s, fw, m, patches, *refs),
        "mlp_backward",
        9,
        [slot_index, frame_weight, member_s],
        space_grid,
        [
            pool, pool_other, head_b, valid_p, targets_p, label_total[None],
            hat2, rstd2, hat3, rstd3, gp, low_rows,
        ],
        [
            rows_spec, rows_spec, whole(width, class_pad), whole(1, class_pad), whole(1, class_pad),
            pl.BlockSpec(memory_space=pltpu.SMEM),
            frame_spec, frame_thin, frame_spec, frame_thin, gp_spec, rows_spec,
        ],
        [half32, half16, pair16, row32, row32],
        [frame_spec, frame_spec, act_spec, rows_spec, rows_spec],
        tile_bufs((1, mlp_count), (mlp_count, 1))
        + [
            pltpu.VMEM((frame_rows, mlp_count * width), bf16),
            pltpu.VMEM((8, width), f32),
            pltpu.VMEM((5, 8, width), f32),
            pltpu.SemaphoreType.DMA((2,)),
        ],
    )

    grads_spec = pl.BlockSpec((FRAMES_AT_ONCE, padded, 4 * width), lambda f, *_: (f, 0, 0))
    g1, grads_space, norm_space = call(
        space_backward,
        "space_backward",
        11,
        [slot_index],
        space_grid,
        [dx2, hat1, rstd1, q_s, k_s, v_s, space_rows, space_q, space_k],
        [frame_spec] * 2 + [frame_thin] + [frame_spec] * 3 + [rows_spec, space_extra, space_extra],
        [half16, jax.ShapeDtypeStruct((half_frames, padded, 4 * width), bf16), row32],
        [frame_spec, grads_spec, rows_spec],
        tile_bufs((1, 3), (1, 1))
        + [
            pltpu.VMEM((2, 8, width), f32),
            pltpu.VMEM((frame_rows, width), bf16),
            pltpu.SemaphoreType.DMA((2,)),
        ],
    )

    def patches_of(grad, which):
        main = half_blocks * group_rows
        here = lax.dynamic_slice_in_dim(grad, which * main, main, 1)
        return jnp.concatenate([here, grad[:, 2 * main :]], axis=1)

    leaving, near, late_hid1, late_hid2 = lax.optimization_barrier(
        (patches_of(g1, 1 - half), patches_of(g1, half), hid1, hid2)
    )
    far = swap(leaving, "mlp", 1)
    clip_spec = whole(half_frames, padded, width)
    one_spec = pl.BlockSpec((1, half_frames, padded, width), lambda i, c: (i, 0, 0, 0))
    square_spec = pl.BlockSpec((1, 2, width, middle), lambda i, c: (i, 0, 0, 0))
    keep_mlp, send_mlp = call(
        mlp_weights,
        "mlp_weights",
        2,
        [core_s],
        (2,),
        [late_hid2, g3, du, act],
        [clip_spec, clip_spec, one_spec, one_spec],
        [squares16] * 2,
        [square_spec] * 2,
        [pltpu.VMEM((2, width, width), f32)],
        tiles=False,
    )
    met_mlp = swap(send_mlp, "dp", 1)
    keep_space, send_space, sums_space = call(
        space_weights,
        "space_weights",
        2,
        [core_s],
        (4,),
        [picked, late_hid1, o_s, grads_space],
        [
            pick_spec, clip_spec, clip_spec,
            pl.BlockSpec((half_frames, padded, width), lambda i, c: (0, 0, i)),
        ],
        [jax.ShapeDtypeStruct((2, 4, share, middle), bf16)] * 2
        + [jax.ShapeDtypeStruct((4, 8, width), f32)],
        [pl.BlockSpec((2, 1, share, middle), lambda i, c: (0, i, 0, 0))] * 2
        + [pl.BlockSpec((1, 8, width), lambda i, c: (i, 0, 0))],
        [pltpu.VMEM((2 * share + 16, half_frames * padded), bf16),
         pltpu.VMEM((2 * share + 16, width), f32)],
        tiles=False,
    )
    far, keep_space, send_space = lax.optimization_barrier((far, keep_space, send_space))
    met_space = swap(send_space, "dp", 1)
    chip_mlp = added(keep_mlp[1], met_mlp[1]).astype(bf16)
    chip_space = added(keep_space[1], met_space[1]).astype(bf16)
    far, chip_mlp, chip_space = lax.optimization_barrier((far, chip_mlp, chip_space))
    far_mlp = swap(chip_mlp, "mlp", 1)
    far_space = swap(chip_space, "mlp", 1)
    keep_time, send_time, rows_time, grad_pos, grad_frames = call(
        partial(time_backward, rest),
        "time_backward",
        18,
        [slot_index, member_s, core_s],
        back_grid,
        [near, far, hid0, hat0, rstd0, q_t, k_t, v_t, o_t, pix, time_rows, picked, time_q, time_k],
        [near_spec] * 2
        + [back_spec] * 2
        + [back_thin]
        + [back_spec] * 5
        + [rows_spec, pick_spec, time_extra, time_extra],
        [jax.ShapeDtypeStruct((2, 5, share, middle), bf16)] * 2
        + [
            row32,
            jax.ShapeDtypeStruct((half_rows, width), f32),
            jax.ShapeDtypeStruct((frames, width), f32),
        ],
        [whole(2, 5, share, middle)] * 2 + [rows_spec, patch_spec, whole(frames, width)],
        tile_bufs((1, 3), (1, 1))
        + [
            pltpu.VMEM((2 * share + 16, 3 * width), f32),
            pltpu.VMEM((2 * share + 16, width), f32),
        ]
        + [
            pltpu.VMEM((2 * share + 16, width), f32),
            pltpu.VMEM((2, 8, width), f32),
            pltpu.VMEM((frames, group_rows, 3 * width), bf16),
            pltpu.VMEM((frames, group_rows, width), bf16),
            pltpu.SemaphoreType.DMA((2,)),
        ],
    )

    grad_time = jnp.einsum("ft,fd->td", time_hot, grad_frames, precision=highest)
    send_time, far_mlp, far_space = lax.optimization_barrier((send_time, far_mlp, far_space))
    met_time = swap(send_time, "dp", 1)
    chip_time = added(keep_time[1], met_time[1]).astype(bf16)
    far_time = swap(chip_time, "mlp", 1)
    main = half_blocks * group_rows
    all_pos = jnp.concatenate(
        [jnp.where(half == i, grad_pos[:main], 0.0) for i in range(2)] + [grad_pos[main:]]
    )
    table_rows = tables.shape[0]
    table_part = jnp.concatenate(
        [
            jnp.sum(grad_frames, axis=0, keepdims=True),
            rows_time[:5],
            norm_space[:2],
            sums_space[0, :1],
            sums_space[2, :1],
            sums_space[3, :1],
            rows_low[:5],
            all_pos[:patches],
            grad_time,
        ]
    )
    rows_each = -(-table_rows // (dp_count * mlp_count))
    table_part = jnp.pad(
        table_part, ((0, rows_each * dp_count * mlp_count - table_rows), (0, 0))
    ).reshape(dp_count, mlp_count, rows_each, width)

    def table_of(which):
        rows_now = lax.dynamic_index_in_dim(table_part, which, 1, False).astype(bf16)
        return jnp.pad(rows_now, ((0, 0), (0, 16 - rows_each), (0, 0)))

    table_pair = jnp.stack([table_of(member), table_of(member ^ 1)])
    columns = jnp.stack([table_pair[..., :middle], table_pair[..., middle:]])
    keep_table = lax.dynamic_index_in_dim(columns, place % 2, 0, False)
    met_table = swap(lax.dynamic_index_in_dim(columns, 1 - place % 2, 0, False), "dp", 1)
    far_table = swap(added(keep_table[1], met_table[1]).astype(bf16), "mlp", 1)

    def blocks_of(*parts):
        return [part.reshape(part.shape[0], -1, BR, middle) for part in parts]

    sources = (
        blocks_of(keep_time, keep_space, keep_mlp)
        + [keep_table]
        + blocks_of(met_time, met_space, met_mlp)
        + [met_table]
        + [part.reshape(-1, BR, middle) for part in (far_time, far_space, far_mlp)]
        + [far_table]
    )
    bits = dp_count.bit_length() - 1
    chunk = jax.ShapeDtypeStruct((dp_count // 4, slots * BR + 16, middle), bf16)
    packed = pl.pallas_call(
        partial(pack, bits),
        grid_spec=pltpu.PrefetchScalarGridSpec(
            num_scalar_prefetch=2,
            grid=(1,),
            in_specs=[
                pl.BlockSpec((1,) + part.shape[1:], lambda i, *_: (0, 0, 0, 0))
                if part.ndim == 4
                else whole(*part.shape)
                for part in sources
            ],
            out_specs=[any_spec] * 4,
            scratch_shapes=[pltpu.VMEM(part.shape, bf16) for part in sources[8:]]
            + [pltpu.SemaphoreType.DMA((4,))],
        ),
        out_shape=[chunk] * 4,
        compiler_params=params,
        name="pack",
    )(dests, place[None], *sources)
    sum_a, sum_b = (value.reshape(value.shape[-2:]) for value in halve(*packed, "dp"))
    even = place % 2 == 0
    mine = jnp.where(even, sum_a, sum_b)
    met = swap(jnp.where(even, sum_b, sum_a), "dp", 1)
    summed = jnp.concatenate([jnp.where(even, mine, met), jnp.where(even, met, mine)], axis=1)
    my_slots = (place * mlp_count + member) * slots + jnp.arange(slots)
    filled = jnp.any(slot_index[:, None] == my_slots[None, :], axis=0)
    filled = jnp.repeat(filled, BR)[:, None]
    own_grad = jnp.where(filled, summed[: slots * BR], 0.0)
    squares_own = jnp.sum(own_grad * own_grad)
    block = jnp.concatenate(
        [
            jnp.pad(summed[slots * BR : slots * BR + rows_each], ((0, 7 - rows_each), (0, 0))),
            jnp.broadcast_to(squares_own, (1, width)),
            small,
        ]
    )
    blocks = jnp.concatenate(
        [spread_four(block[:8], "mlp"), block[None, 8:]], axis=0
    )
    blocks = lax.all_gather(blocks, "dp", axis=0)
    heads, blocks = blocks[:, mlp_count], blocks[:, :mlp_count]
    grad_head = jnp.einsum("cd,ck->dk", heads[:, 0], heads[:, 1, :classes], precision=highest)
    loss_sum = jnp.sum(heads[:, 2, 0])
    grad_tables = blocks[:, :, :rows_each].reshape(-1, width)[:table_rows]
    grad_norm = jnp.sqrt(
        jnp.sum(blocks[:, :, 7, 0])
        + jnp.sum(grad_tables * grad_tables)
        + jnp.sum(grad_head * grad_head)
    )
    factor = jnp.minimum(1.0, clip_max / (grad_norm + 1e-06))
    new_slots = adamw(
        slot_weight, own_grad * factor, slot_moment1, slot_moment2, decay_rate, learn_rate
    )
    new_tabs = adamw(tables, grad_tables * factor, table_moment1, table_moment2, 0.0, table_rate)
    new_heads = adamw(
        head_weight, grad_head * factor, head_moment1, head_moment2, decay_rate, learn_rate
    )
    return (
        loss_sum,
        label_total,
        grad_norm,
        new_slots[0],
        new_slots[1],
        new_slots[2],
        new_tabs[0],
        new_tabs[1],
        new_tabs[2],
        new_heads[0],
        new_heads[1],
        new_heads[2],
    )


def solution(mesh):
    return jax.shard_map(
        local,
        mesh=mesh,
        in_specs=(
            P("dp", None, None, None),
            P("dp"),
            P("dp", None),
            P("dp", None),
            P("dp", None),
            P("dp", None),
            P(),
            P(("dp", "mlp"), None),
            P(("dp", "mlp"), None),
            P(("dp", "mlp"), None),
            P(),
            P(),
            P(),
            P(),
            P(),
            P(),
        ),
        out_specs=(
            P(),
            P(),
            P(),
            P(("dp", "mlp"), None),
            P(("dp", "mlp"), None),
            P(("dp", "mlp"), None),
            P(),
            P(),
            P(),
            P(),
            P(),
            P(),
        ),
        check_vma=False,
    )
```

```python
from functools import partial

import jax
import jax.numpy as jnp
from jax import lax
from jax.experimental import pallas as pl
from jax.experimental.pallas import tpu as pltpu
from jax.sharding import PartitionSpec as P

HEADS = 12
HEAD_DIM = 64
TROWS = 8
BR = 48
STEP = 10
GROUP = 16
PAIR = 2 * HEAD_DIM
GROUPS_AT_ONCE = 2
FRAMES_AT_ONCE = 2
VMEM_BYTES = 58 * 2**20

ln_eps = 1e-06
beta_one = 0.9
beta_two = 0.999
learn_rate = 0.05
table_rate = 0.4
decay_rate = 0.05
adam_eps = 1e-08
clip_max = 0.001
highest = lax.Precision.HIGHEST
f32 = jnp.float32
bf16 = jnp.bfloat16
gelu_a = 0.7978845608028654
gelu_b = 0.044715
masked = -1e30


def mm(left, right):
    return jnp.dot(left, right, preferred_element_type=f32)


def mm_nt(left, right):
    return lax.dot_general(left, right, (((1,), (1,)), ((), ())), preferred_element_type=f32)


def mm_tn(left, right):
    return lax.dot_general(left, right, (((0,), (0,)), ((), ())), preferred_element_type=f32)


def normed(values):
    centred = values - jnp.mean(values, axis=-1, keepdims=True)
    rstd = lax.rsqrt(jnp.mean(centred * centred, axis=-1, keepdims=True) + ln_eps)
    return centred * rstd, rstd


def norm_back(grad, xhat, rstd, gain):
    scaled = grad * gain
    return rstd * (
        scaled
        - jnp.mean(scaled, axis=-1, keepdims=True)
        - xhat * jnp.mean(scaled * xhat, axis=-1, keepdims=True)
    )


def fold(values):
    return jnp.sum(values.reshape(-1, 8, values.shape[-1]), axis=0)


def low_lanes():
    lane = lax.broadcasted_iota(jnp.int32, (1, PAIR), 1)
    low = jnp.where(lane < HEAD_DIM, 1.0, 0.0)
    return low.astype(bf16), (1.0 - low).astype(bf16)


def pick_half(stacked):
    rows = stacked.shape[0] // 2
    lane = lax.broadcasted_iota(jnp.int32, (rows, PAIR), 1)
    return jnp.where(lane < HEAD_DIM, stacked[:rows], stacked[rows:])


def fetch(slots_ref, source, target, sem, first, across):
    width = source.shape[2]
    per_tile = width // BR

    def one(i, carry):
        tile, row = i // per_tile, pl.multiple_of((i % per_tile) * BR, 16)
        place = pl.ds(row, BR)
        if across:
            into = target.at[place, pl.ds(pl.multiple_of(tile * width, width), width)]
        else:
            into = target.at[pl.ds(pl.multiple_of(tile * width, 16) + row, BR)]
        block = first(tile) * per_tile + i % per_tile
        pltpu.make_async_copy(source.at[slots_ref[block]], into, sem).start()
        return carry

    count = target.shape[0] * target.shape[1] // (width * width)
    lax.fori_loop(0, count * per_tile, one, 0)


def arrive(target, sem):
    pltpu.make_async_copy(target, target, sem).wait()


def jobs_of(count):
    pairs = [slice(p * PAIR, (p + 1) * PAIR) for p in range(HEADS // 2)]
    return [(i, lanes) for i in range(count) for lanes in pairs]


def each_row(count, begin, finish):
    def one(i, carry):
        in_flight([(i, lanes) for unused, lanes in jobs_of(1)], begin, finish)
        return carry

    lax.fori_loop(0, count, one, 0)


def in_flight(jobs, begin, finish):
    waiting = None
    for job in jobs:
        started = begin(*job)
        if waiting is not None:
            finish(*waiting)
        waiting = job + started
    finish(*waiting)


def attend(count, load, store, extra_q, extra_k):
    low, high = low_lanes()

    def begin(i, lanes):
        queries, keys, values = load(i, lanes)
        both = jnp.concatenate([queries * low, queries * high], axis=0)
        scores = mm_nt(
            jnp.concatenate([both, extra_q[...]], axis=1),
            jnp.concatenate([keys, extra_k[: keys.shape[0]]], axis=1),
        )
        return values, scores

    def finish(i, lanes, values, scores):
        top = jnp.max(scores, axis=-1, keepdims=True)
        weights = jnp.exp(scores - top).astype(bf16)
        summed = mm(weights, jnp.concatenate([values, jnp.ones_like(values)], axis=1))
        merged = pick_half(summed[:, :PAIR]) / pick_half(summed[:, PAIR:])
        store(i, lanes, merged.astype(bf16))

    in_flight(jobs_of(count), begin, finish)


def attend_back(count, load, store, extra_q, extra_k, looped=False):
    low, high = low_lanes()

    def begin(i, lanes):
        queries, keys, values, grads = load(i, lanes)
        both_k = jnp.concatenate([keys * low, keys * high], axis=0)
        both_v = jnp.concatenate([values * low, values * high], axis=0)
        scores = mm_nt(
            jnp.concatenate([both_k, extra_k[...]], axis=1),
            jnp.concatenate([queries, extra_q[: queries.shape[0]]], axis=1),
        )
        return queries, both_k, grads, scores, mm_nt(both_v, grads)

    def finish(i, lanes, queries, both_k, grads, scores, back):
        rows = queries.shape[0]
        soft, inner = [], []
        for half in (slice(0, rows), slice(rows, 2 * rows)):
            part = scores[half]
            weights = jnp.exp(part - jnp.max(part, axis=0, keepdims=True))
            weights = weights * (1.0 / jnp.sum(weights, axis=0, keepdims=True))
            delta = back[half] - jnp.sum(weights * back[half], axis=0, keepdims=True)
            soft.append(weights.astype(bf16))
            inner.append((weights * delta).astype(bf16))
        soft = jnp.concatenate(soft, axis=0)
        inner = jnp.concatenate(inner, axis=0)
        store(
            i,
            lanes,
            (mm_tn(inner, both_k) * HEAD_DIM ** (-0.5)).astype(bf16),
            pick_half(mm(inner, queries)).astype(bf16),
            pick_half(mm(soft, grads)).astype(bf16),
        )

    if looped:
        each_row(count, begin, finish)
    else:
        in_flight(jobs_of(count), begin, finish)


def project(hidden, rows, tiles):
    width = hidden.shape[1]
    joint = mm(hidden, tiles[...])
    queries = (joint[:, :width] + rows[2:3]).astype(bf16) * jnp.asarray(HEAD_DIM ** (-0.5), bf16)
    keys = joint[:, width : 2 * width].astype(bf16)
    values = (joint[:, 2 * width :] + rows[3:4]).astype(bf16)
    return queries, keys, values


def keep_norm(stream, rows, at, hid_ref, hat_ref, rstd_ref, here, cut):
    xhat, rstd = normed(stream)
    hat_ref[here] = xhat.astype(bf16).reshape(cut)
    rstd_ref[here] = jnp.broadcast_to(rstd, (rstd.shape[0], 128)).reshape(cut[:-1] + (128,))
    hidden = (xhat * rows[at : at + 1] + rows[at + 1 : at + 2]).astype(bf16)
    if hid_ref is not None:
        hid_ref[here] = hidden.reshape(cut)
    return xhat, hidden


def by_groups(block, total, work):
    step = pl.program_id(0)
    full, rest = total // block, total % block
    if rest == 0:
        work(block)
    else:
        pl.when(step < full)(lambda: work(block))
        pl.when(step == full)(lambda: work(rest))


def time_forward(
    total, slots, member, gathered, pixels, pos, trow, rows, extra_q, extra_k,
    x1_ref, hid_ref, hat_ref, rstd_ref, q_ref, k_ref, v_ref, o_ref,
    embed, joint, out, base, sems,
):
    frames, span, width = hid_ref.shape

    @pl.when(pl.program_id(0) == 0)
    def _():
        fetch(slots, gathered, embed, sems.at[0], lambda t: t, False)
        fetch(slots, gathered, joint, sems.at[1], lambda t: t + 1, True)
        fetch(slots, gathered, out, sems.at[2], lambda t: t + 4, False)
        arrive(embed, sems.at[0])

    def first(target, sem):
        pl.when(pl.program_id(0) == 0)(lambda: arrive(target, sem))

    def work(count):
        cut = (frames, count * GROUP, width)
        flat = (frames * count * GROUP, width)
        here = slice(0, count * GROUP)
        every = (slice(None), here)
        offset = (pos[here][None] + trow[...][:, None]).reshape(flat)
        stream = mm(pixels[:, here].reshape(flat), embed[...]) + offset
        base[: flat[0]] = stream
        rows_now = rows[...]
        unused, hidden = keep_norm(stream, rows_now, 0, hid_ref, hat_ref, rstd_ref, every, cut)
        first(joint, sems.at[1])
        queries, keys, values = project(hidden, rows_now, joint)
        q_ref[:, here] = queries.reshape(cut)
        k_ref[:, here] = keys.reshape(cut)
        v_ref[:, here] = values.reshape(cut)

        def load(g, lanes):
            part = slice(g * GROUP, (g + 1) * GROUP)
            return tuple(
                ref[:, part, lanes].reshape(frames * GROUP, PAIR) for ref in (q_ref, k_ref, v_ref)
            )

        def store(g, lanes, merged):
            part = slice(g * GROUP, (g + 1) * GROUP)
            o_ref[:, part, lanes] = merged.reshape(frames, GROUP, PAIR)

        attend(count, load, store, extra_q, extra_k)
        first(out, sems.at[2])
        near, some = frames // 2, flat[0] // 2
        late = member[0] % 2
        merged = o_ref[pl.ds(late * near, near), here].reshape(some, width)
        stream = base[pl.ds(pl.multiple_of(late * some, 16), some)] + mm(merged, out[...])
        x1_ref[:, here] = (stream + rows_now[4:5]).reshape(near, count * GROUP, width)

    by_groups(span // GROUP, total, work)


def space_forward(
    slots, frame_weight, member, patches, gathered, x1, rows, low_rows, extra_q, extra_k,
    hid1_ref, hat1_ref, rstd1_ref, q_ref, k_ref, v_ref, o_ref,
    hid2_ref, hat2_ref, rstd2_ref, hat3_ref, rstd3_ref, gp_ref, act_ref, pool_ref,
    joint, out, ups, downs, acts, sems,
):
    step = pl.program_id(0)
    members = gp_ref.shape[0]
    cut = x1.shape
    span, count, width = cut
    flat = (span * count, width)
    every = (slice(None),)

    @pl.when(step == 0)
    def _():
        fetch(slots, gathered, joint, sems.at[0], lambda t: t + 5, True)
        fetch(slots, gathered, out, sems.at[1], lambda t: t + 8, False)
        fetch(slots, gathered, ups, sems.at[2], lambda t: 2 * t + 9, True)
        fetch(slots, gathered, downs, sems.at[3], lambda t: 2 * t + 10, False)
        pool_ref[...] = jnp.zeros_like(pool_ref)
        arrive(joint, sems.at[0])

    rows_now = rows[...]
    unused, hidden = keep_norm(
        x1[...].reshape(flat), rows_now, 0, hid1_ref, hat1_ref, rstd1_ref, every, cut
    )
    queries, keys, values = project(hidden, rows_now, joint)
    q_ref[...] = queries.reshape(cut)
    k_ref[...] = keys.reshape(cut)
    v_ref[...] = values.reshape(cut)

    def load(f, lanes):
        return q_ref[f, :, lanes], k_ref[f, :, lanes], v_ref[f, :, lanes]

    def store(f, lanes, merged):
        o_ref[f, :, lanes] = merged

    attend(span, load, store, extra_q, extra_k)
    pl.when(step == 0)(lambda: arrive(out, sems.at[1]))
    merged = o_ref[...].reshape(flat)
    stream = x1[...].reshape(flat) + mm(merged, out[...]) + rows_now[4:5]
    low_now = low_rows[...]
    unused, hidden = keep_norm(stream, low_now, 0, hid2_ref, hat2_ref, rstd2_ref, every, cut)

    @pl.when(step == 0)
    def _():
        arrive(ups, sems.at[2])
        arrive(downs, sems.at[3])

    def begin(j, lanes):
        return (mm(hidden, ups[:, lanes]),)

    lowered = []

    def finish(j, lanes, upper):
        cubic = gelu_a * gelu_b * (upper * upper)
        gate = 0.5 + 0.5 * jnp.tanh(upper * (gelu_a + cubic))
        active = upper * gate
        slope = gate + active * (1.0 - gate) * (2.0 * gelu_a + 6.0 * cubic)
        gp_ref[j] = slope.astype(bf16).reshape(cut)
        acts[:, lanes] = active.astype(bf16)
        lowered.append(mm(acts[:, lanes], downs[lanes]))

    in_flight([(j, slice(j * width, (j + 1) * width)) for j in range(members)], begin, finish)
    for part in lowered:
        stream = stream + part
    for i in range(2):
        own = pl.ds(pl.multiple_of((member[0] ^ i) * width, 128), width)
        act_ref[i] = acts[:, own].reshape(cut)
    stream = stream + low_now[2:3]
    xhat, rstd = normed(stream)
    hat3_ref[...] = xhat.astype(bf16).reshape(cut)
    rstd3_ref[...] = jnp.broadcast_to(rstd, (flat[0], 128)).reshape(span, count, 128)
    final = xhat * low_now[3:4] + low_now[4:5]
    row = lax.broadcasted_iota(jnp.int32, (count, 1), 0)
    for f in range(span):
        part = jnp.where(row < patches, final[f * count : (f + 1) * count], 0.0)
        pool_ref[...] += fold(part) * frame_weight[step * span + f]


def mlp_backward(
    slots, frame_weight, member, patches, gathered, pool, pool_other, head, valid, targets, total,
    hat2, rstd2, hat3, rstd3, gp, low_rows,
    dx2_ref, g3_ref, du_ref, rows_ref, small_ref,
    ups, downs, dus, spread, row_sums, sems,
):
    step = pl.program_id(0)
    members = gp.shape[0]
    cut = hat2.shape
    span, count, width = cut
    flat = (span * count, width)

    @pl.when(step == 0)
    def _():
        fetch(slots, gathered, downs, sems.at[1], lambda t: 2 * t + 10, False)
        fetch(slots, gathered, ups, sems.at[0], lambda t: 2 * t + 9, True)
        pooled = jnp.sum(pool[...] + pool_other[...], axis=0, keepdims=True).astype(bf16)
        pooled8 = jnp.broadcast_to(pooled, (8, width))
        logits = mm(pooled8, head[...])
        valid_f = valid[...]
        target = targets[...]
        soft = jnp.maximum(logits, 0.0) + jnp.log(1.0 + jnp.exp(-jnp.abs(logits)))
        loss = jnp.sum(valid_f * (soft - target * logits), axis=1, keepdims=True)
        sig = 1.0 / (1.0 + jnp.exp(-logits))
        grad = (valid_f * (sig - target) / jnp.maximum(total[0], 1.0)).astype(bf16)
        spread[...] = mm_nt(grad, head[...])
        small_ref[...] = jnp.zeros_like(small_ref)
        small_ref[0:1, :] = pooled.astype(f32)
        small_ref[1:2, 0 : grad.shape[1]] = grad[0:1].astype(f32)
        small_ref[2:3, 0:128] = jnp.broadcast_to(loss[0:1], (1, 128))
        row_sums[...] = jnp.zeros_like(row_sums)
        arrive(downs, sems.at[1])

    low_now = low_rows[...]
    row = lax.broadcasted_iota(jnp.int32, (count, 1), 0)
    weight = jnp.concatenate(
        [jnp.where(row < patches, frame_weight[step * span + f], 0.0) for f in range(span)]
    )
    grad_final = spread[0:1] * weight
    xhat = hat3[...].reshape(flat).astype(f32)
    rstd = rstd3[...].reshape(flat[0], 128)[:, 0:1]
    row_sums[3] += fold(grad_final * xhat)
    row_sums[4] += fold(grad_final)
    grad_top = norm_back(grad_final, xhat, rstd, low_now[3:4])
    row_sums[2] += fold(grad_top)
    grad_b = grad_top.astype(bf16)
    g3_ref[...] = grad_b.reshape(cut)

    for j in range(members):
        lanes = slice(j * width, (j + 1) * width)
        du = mm_nt(grad_b, downs[lanes]) * gp[j].reshape(flat).astype(f32)
        dus[:, lanes] = du.astype(bf16)

    @pl.when(step == 0)
    def _():
        arrive(ups, sems.at[0])

    grad_hidden = mm_nt(dus[...], ups[...])
    for i in range(2):
        own = pl.ds(pl.multiple_of((member[0] ^ i) * width, 128), width)
        du_ref[i] = dus[:, own].reshape(cut)
    xhat = hat2[...].reshape(flat).astype(f32)
    rstd = rstd2[...].reshape(flat[0], 128)[:, 0:1]
    row_sums[0] += fold(grad_hidden * xhat)
    row_sums[1] += fold(grad_hidden)
    dx2_ref[...] = (grad_top + norm_back(grad_hidden, xhat, rstd, low_now[0:1])).reshape(cut)

    @pl.when(step == pl.num_programs(0) - 1)
    def _():
        rows_ref[...] = jnp.zeros_like(rows_ref)
        for i in range(5):
            rows_ref[i : i + 1] = jnp.sum(row_sums[i], axis=0, keepdims=True)


def mlp_weights(core, hid2, g3, du, act, keep_ref, send_ref, sums):
    rows, width = hid2.shape[0] * hid2.shape[1], hid2.shape[2]
    sums[0] = mm_tn(hid2[...].reshape(rows, width), du[0].reshape(rows, width))
    sums[1] = mm_tn(act[0].reshape(rows, width), g3[...].reshape(rows, width))
    for ref, half in zip((keep_ref, send_ref), column_halves(core[0], width)):
        for n in range(2):
            ref[0, n] = sums[n, :, half].astype(bf16)


def space_weights(core, picked, hid1, o, grads, keep_ref, send_ref, rows_ref, left, sums):
    step = pl.program_id(0)
    rows, width = hid1.shape[0] * hid1.shape[1], hid1.shape[2]
    share = keep_ref.shape[2]

    def select(source):
        chosen = mm_nt(picked[...], source[...].reshape(rows, width)).astype(bf16)
        left[...] = chosen + ones_row(picked)

    pl.when(step == 0)(lambda: select(hid1))
    pl.when(step == pl.num_programs(0) - 1)(lambda: select(o))
    sums[...] = mm(left[...], grads[...].reshape(rows, width))
    for ref, half in zip((keep_ref, send_ref), column_halves(core[0], width)):
        for n in range(2):
            ref[n, 0] = sums[n * share : (n + 1) * share, half].astype(bf16)
    rows_ref[0] = sums[2 * share : 2 * share + 8]


def close_attention(
    grad_stream, grad_b, hidden, xhat, rstd, grads, merged, rows_now, picked, ones, joint,
    joint_sum, out_sum, row_sums,
):
    grad_hidden = mm_nt(grads, joint[...])
    hidden_t = mm_nt(picked, hidden).astype(bf16) + ones
    merged_t = mm_nt(picked, merged).astype(bf16) + ones
    joint_sum[...] += mm(hidden_t, grads)
    out_sum[...] += mm(merged_t, grad_b)
    xhat = xhat.astype(f32)
    row_sums[0] += fold(grad_hidden * xhat)
    row_sums[1] += fold(grad_hidden)
    return grad_stream + norm_back(grad_hidden, xhat, rstd[:, 0:1], rows_now[0:1])


def ones_row(picked):
    row = lax.broadcasted_iota(jnp.int32, (picked.shape[0], 1), 0)
    return jnp.where(row == picked.shape[0] - 16, 1.0, 0.0).astype(bf16)


def column_halves(core, width):
    middle = width // 2
    keep = pl.ds(pl.multiple_of(core * middle, 128), middle)
    send = pl.ds(pl.multiple_of((1 - core) * middle, 128), middle)
    return keep, send


def clear(*refs):
    for ref in refs:
        ref[...] = jnp.zeros_like(ref)


def finish_attention(core, tile_refs, at, rows_ref, joint_sum, out_sum, row_sums):
    share = tile_refs[0].shape[2]
    width = out_sum.shape[1]
    rows_ref[...] = jnp.zeros_like(rows_ref)
    for tile_ref, half in zip(tile_refs, column_halves(core, width)):
        for n in range(2):
            here = slice(n * share, (n + 1) * share)
            for i in range(3):
                start = pl.multiple_of(i * width + half.start, 128)
                columns = pl.ds(start, half.size)
                tile_ref[n, at + i] = joint_sum[here, columns].astype(bf16)
            tile_ref[n, at + 3] = out_sum[here, half].astype(bf16)
    last = slice(2 * share, 2 * share + 1)
    for i in range(2):
        rows_ref[i : i + 1] = jnp.sum(row_sums[i], axis=0, keepdims=True)
    rows_ref[2:3] = joint_sum[last, :width]
    rows_ref[3:4] = joint_sum[last, 2 * width :]
    rows_ref[4:5] = out_sum[last]


def space_backward(
    slots, gathered, dx2, hat1, rstd1, q, k, v, rows, extra_q, extra_k,
    g1_ref, grads_ref, rows_ref, joint, out, row_sums, outer, sems,
):
    step = pl.program_id(0)
    cut = hat1.shape
    span, count, width = cut
    flat = (span * count, width)

    @pl.when(step == 0)
    def _():
        fetch(slots, gathered, out, sems.at[1], lambda t: t + 8, False)
        fetch(slots, gathered, joint, sems.at[0], lambda t: t + 5, True)
        clear(row_sums)
        arrive(out, sems.at[1])

    grad_b = dx2[...].reshape(flat).astype(bf16)
    grads_ref[:, :, 3 * width :] = grad_b.reshape(cut)
    outer[...] = mm_nt(grad_b, out[...]).astype(bf16)

    def load(f, lanes):
        here = pl.ds(pl.multiple_of(f * count, 16), count)
        return q[f, :, lanes], k[f, :, lanes], v[f, :, lanes], outer[here, lanes]

    def store(f, lanes, *parts):
        for i, part in enumerate(parts):
            grads_ref[f, :, i * width + lanes.start : i * width + lanes.stop] = part

    attend_back(span, load, store, extra_q, extra_k, looped=True)
    pl.when(step == 0)(lambda: arrive(joint, sems.at[0]))
    grads = grads_ref[:, :, : 3 * width].reshape(flat[0], 3 * width)
    grad_hidden = mm_nt(grads, joint[...])
    xhat = hat1[...].reshape(flat).astype(f32)
    rstd = rstd1[...].reshape(flat[0], 128)[:, 0:1]
    row_sums[0] += fold(grad_hidden * xhat)
    row_sums[1] += fold(grad_hidden)
    grad_stream = dx2[...].reshape(flat) + norm_back(grad_hidden, xhat, rstd, rows[0:1])
    g1_ref[...] = grad_stream.astype(bf16).reshape(cut)

    @pl.when(step == pl.num_programs(0) - 1)
    def _():
        rows_ref[...] = jnp.zeros_like(rows_ref)
        for i in range(2):
            rows_ref[i : i + 1] = jnp.sum(row_sums[i], axis=0, keepdims=True)


def time_backward(
    rest, slots, member, core, gathered, near, far, hid0, hat0, rstd0, q, k, v, o, pixels, rows, picked,
    extra_q, extra_k,
    keep_ref, send_ref, rows_ref, pos_ref, frame_ref,
    joint, out, joint_sum, out_sum, embed_sum, row_sums, grads, outer, sems,
):
    step = pl.program_id(0)
    frames, span, width = hid0.shape

    @pl.when(step == 0)
    def _():
        fetch(slots, gathered, out, sems.at[1], lambda t: t + 4, False)
        fetch(slots, gathered, joint, sems.at[0], lambda t: t + 1, True)
        clear(joint_sum, out_sum, embed_sum, row_sums, frame_ref)
        arrive(out, sems.at[1])

    def work(groups):
        cut = (frames, groups * GROUP, width)
        flat = (frames * groups * GROUP, width)
        small = (frames, GROUP, PAIR)
        here = slice(0, groups * GROUP)
        first = member[0] % 2 == 0
        near_now, far_now = near[:, here], far[:, here]
        grad_b = jnp.concatenate(
            [jnp.where(first, near_now, far_now), jnp.where(first, far_now, near_now)]
        ).reshape(flat)
        outer[:, here] = mm_nt(grad_b, out[...]).astype(bf16).reshape(cut)

        def load(g, lanes):
            part = slice(g * GROUP, (g + 1) * GROUP)
            return tuple(
                ref[:, part, lanes].reshape(frames * GROUP, PAIR) for ref in (q, k, v, outer)
            )

        def store(g, lanes, *parts):
            part = slice(g * GROUP, (g + 1) * GROUP)
            for i, value in enumerate(parts):
                span_now = slice(i * width + lanes.start, i * width + lanes.stop)
                grads[:, part, span_now] = value.reshape(small)

        attend_back(groups, load, store, extra_q, extra_k)
        pl.when(step == 0)(lambda: arrive(joint, sems.at[0]))
        picked_now = picked[...]
        grad = close_attention(
            grad_b.astype(f32), grad_b, hid0[:, here].reshape(flat),
            hat0[:, here].reshape(flat), rstd0[:, here].reshape(flat[0], 128),
            grads[:, here].reshape(flat[0], 3 * width), o[:, here].reshape(flat), rows[...],
            picked_now, ones_row(picked_now), joint, joint_sum, out_sum, row_sums,
        )
        pix_t = mm_nt(picked_now, pixels[:, here].reshape(flat)).astype(bf16)
        embed_sum[...] += mm(pix_t, grad.astype(bf16))
        cube = grad.reshape(cut)
        pos_ref[here] = jnp.sum(cube, axis=0)
        frame_ref[...] += jnp.sum(cube, axis=1)

    last = step == pl.num_programs(0) - 1
    if rest == 0:
        work(span // GROUP)
    else:
        odd = member[0] % 2 == 1
        pl.when(jnp.logical_not(last))(lambda: work(span // GROUP))
        pl.when(jnp.logical_and(last, jnp.logical_not(odd)))(lambda: work(rest))

        @pl.when(jnp.logical_and(last, odd))
        def _():
            pos_ref[...] = jnp.zeros_like(pos_ref)

    @pl.when(last)
    def _():
        finish_attention(
            core[0], (keep_ref, send_ref), 1, rows_ref, joint_sum, out_sum, row_sums
        )
        share = keep_ref.shape[2]
        for ref, half in zip((keep_ref, send_ref), column_halves(core[0], width)):
            for n in range(2):
                ref[n, 0] = embed_sum[n * share : (n + 1) * share, half].astype(bf16)


def pack(bits, dests, place, *refs):
    count = (len(refs) - 5) // 4
    keeps, mets, fars = (refs[i * count : (i + 1) * count] for i in range(3))
    (stay_a, go_a, stay_b, go_b), sems = refs[3 * count : 3 * count + 4], refs[-1]
    sums = refs[-1 - count : -1]
    table_rows = sums[-1].shape[1]
    slots = (stay_a.shape[1] - table_rows) // BR
    top = bits - 1
    rest = 2 ** (bits - 2) - 1

    def route(source, chunk, rows, sem):
        differs = chunk ^ place[0]
        in_b = chunk % 2 == 1
        index_a, index_b = chunk >> 2, (chunk >> 1) & rest
        moves_a, moves_b = (differs >> 1) % 2 == 1, (differs >> top) % 2 == 1
        for flag, target, index in (
            (~in_b & ~moves_a, stay_a, index_a),
            (~in_b & moves_a, go_a, index_a),
            (in_b & ~moves_b, stay_b, index_b),
            (in_b & moves_b, go_b, index_b),
        ):

            @pl.when(flag)
            def _(target=target, index=index):
                pltpu.make_async_copy(source, target.at[index, rows], sem).start()

    first = 0
    for n, (keep, met, far, source) in enumerate(zip(keeps, mets, fars, sums)):
        table = n == count - 1

        def one(i, carry, keep=keep, met=met, far=far, source=source, first=first, n=n, table=table):
            total = keep[0, i].astype(f32) + met[0, i].astype(f32) + far[i].astype(f32)
            source[i] = total.astype(bf16)
            if table:
                route(source.at[i], i, pl.ds(slots * BR, table_rows), sems.at[n])
            else:
                dest = dests[first + i]
                row = pl.multiple_of((dest % slots) * BR, 16)
                route(source.at[i], dest // slots, pl.ds(row, BR), sems.at[n])
            return carry

        lax.fori_loop(0, source.shape[0], one, 0)
        first += source.shape[0]
    for n, source in enumerate(sums):
        pltpu.make_async_copy(source, source, sems.at[n]).wait()


def swap(value, axis, hop):
    size = lax.axis_size(axis)
    return lax.ppermute(value, axis, [(i, i ^ hop) for i in range(size)])


def added(*parts):
    total = parts[0].astype(f32)
    for part in parts[1:]:
        total = total + part.astype(f32)
    return total


def halve(stay_a, go_a, stay_b, go_b, axis):
    bits = lax.axis_size(axis).bit_length() - 1
    place = lax.axis_index(axis)
    orders = [list(range(1, bits)), list(range(bits - 1, 0, -1))]
    shape = (2,) * (bits - 2) + stay_a.shape[1:]
    going, staying = [go_a, go_b], [stay_a, stay_b]
    for stage in range(bits - 1):
        met = [swap(value, axis, 1 << order[stage]) for value, order in zip(going, orders)]
        values = [added(stay, come) for stay, come in zip(staying, met)]
        if stage == bits - 2:
            return values
        going, staying = [], []
        for value, order in zip(values, orders):
            alive = sorted(order[stage + 1 :], reverse=True)
            value = value.reshape(shape[stage:])
            at = alive.index(order[stage + 1])
            bit = (place >> order[stage + 1]) & 1
            going.append(lax.dynamic_index_in_dim(value, 1 - bit, at, False).astype(bf16))
            staying.append(lax.dynamic_index_in_dim(value, bit, at, False))


def spread_four(value, axis):
    size = lax.axis_size(axis)
    place = lax.axis_index(axis)
    value = value[None]
    hop = 1
    while hop < size:
        come = swap(value, axis, hop)
        low = (place & hop) == 0
        value = jnp.concatenate(
            [jnp.where(low, value, come), jnp.where(low, come, value)], axis=0
        )
        hop *= 2
    return value


def block_ranks(owners):
    total_blocks = owners.shape[0]
    same_owner = owners[:, None] == owners[None, :]
    earlier = jnp.arange(total_blocks)[None, :] < jnp.arange(total_blocks)[:, None]
    return jnp.sum((same_owner & earlier).astype(jnp.int32), axis=1)


def adamw(weight, gradient, moment_one, moment_two, weight_decay, rate):
    first_new = beta_one * moment_one + (1.0 - beta_one) * gradient
    second_new = beta_two * moment_two + (1.0 - beta_two) * gradient * gradient
    mean_hat = first_new / (1.0 - beta_one**STEP)
    var_hat = second_new / (1.0 - beta_two**STEP)
    updated = weight - rate * (mean_hat / (jnp.sqrt(var_hat) + adam_eps) + weight_decay * weight)
    return (updated, first_new, second_new)


def local(
    pixels,
    lengths,
    frame_mask,
    time_index,
    label_valid,
    targets,
    owners,
    slot_weight,
    slot_moment1,
    slot_moment2,
    tables,
    table_moment1,
    table_moment2,
    head_weight,
    head_moment1,
    head_moment2,
):
    dp_count = lax.axis_size("dp")
    mlp_count = lax.axis_size("mlp")
    member = lax.axis_index("mlp").astype(jnp.int32)
    width = slot_weight.shape[1]
    per_tile = width // BR
    slots = slot_weight.shape[0] // BR
    shared_blocks = 9 * per_tile
    frames, patches = pixels.shape[1], pixels.shape[2]
    padded = -(-patches // GROUP) * GROUP
    groups = padded // GROUP
    classes = head_weight.shape[1]
    class_pad = -(-classes // 128) * 128
    params = pltpu.CompilerParams(vmem_limit_bytes=VMEM_BYTES)
    any_spec = pl.BlockSpec(memory_space=pl.ANY)

    gathered = lax.all_gather(slot_weight.astype(bf16), ("dp", "mlp"), axis=0, tiled=True)
    gathered = gathered.reshape(-1, BR, width)
    slot_index = (owners * slots + block_ranks(owners)).astype(jnp.int32)

    pix = jnp.pad(pixels[0], ((0, 0), (0, padded - patches), (0, 0)))
    slot_pos = jnp.arange(frames)
    frame_live = slot_pos < lengths[0]
    key_ok = frame_live & (frame_mask[0] == 1)
    allowed = key_ok[None, :] | (slot_pos[:, None] == slot_pos[None, :])
    extra_lane = jnp.arange(HEAD_DIM)
    flat_id = jnp.arange(frames * GROUP)
    frame_id, patch_id = flat_id // GROUP, flat_id % GROUP
    lane_frame = jnp.clip(extra_lane - GROUP, 0, frames - 1)
    in_patch = (extra_lane < GROUP)[None, :]
    in_frame = ((extra_lane >= GROUP) & (extra_lane < GROUP + frames))[None, :]
    same_patch = patch_id[:, None] == extra_lane[None, :]
    same_frame = frame_id[:, None] == lane_frame[None, :]
    time_q = (in_patch & same_patch) | (in_frame & same_frame)
    time_k = (in_patch & ~same_patch) | (in_frame & ~allowed.T[frame_id][:, lane_frame])
    is_pad = (jnp.arange(padded) >= patches)[:, None]
    space_q = jnp.broadcast_to(extra_lane[None, :] == 0, (padded, HEAD_DIM))
    space_k = is_pad & (extra_lane[None, :] == 0)

    def widen(flags, value):
        block = jnp.where(flags, value, 0.0).astype(bf16)
        block = jnp.pad(block, ((0, 0), (0, PAIR - HEAD_DIM)))
        return jnp.concatenate([block, block])

    time_q, time_k = widen(time_q, 1.0), widen(time_k, masked)
    space_q, space_k = widen(space_q, 1.0), widen(space_k, masked)
    time_hot = (time_index[0][:, None] == jnp.arange(TROWS)[None, :]).astype(f32)
    trow = jnp.einsum("ft,td->fd", time_hot, tables[16 + patches :], precision=highest)
    pos = jnp.pad(tables[16 : 16 + patches] + tables[0], ((0, padded - patches), (0, 0)))
    frame_weight = jnp.where(
        frame_live, 1.0 / (lengths[0] * patches).astype(f32), 0.0
    ).astype(f32)
    valid_f = label_valid.astype(f32)
    label_total = lax.psum(jnp.sum(valid_f), "dp")
    head_b = jnp.pad(head_weight.astype(bf16), ((0, 0), (0, class_pad - classes)))
    valid_p = jnp.pad(valid_f, ((0, 0), (0, class_pad - classes)))
    targets_p = jnp.pad(targets, ((0, 0), (0, class_pad - classes)))
    share = width // mlp_count
    half = member % 2
    place = lax.axis_index("dp").astype(jnp.int32)
    core_s = (place % 2)[None]
    pick_row = jnp.arange(2 * share)
    pick_member = jnp.where(pick_row < share, member, member ^ 1)
    pick_row = pick_row % share
    pick_feature = (pick_row // BR) * (BR * mlp_count) + pick_member * BR + pick_row % BR
    picked = (pick_feature[:, None] == jnp.arange(width)[None, :]).astype(bf16)
    picked = jnp.pad(picked, ((0, 16), (0, 0)))
    member_s = member[None]
    time_rows = jnp.pad(tables[1:6], ((0, 3), (0, 0)))
    space_rows = jnp.pad(tables[6:11], ((0, 3), (0, 0)))
    low_rows = jnp.pad(tables[11:16], ((0, 3), (0, 0)))

    shared_here = shared_blocks // mlp_count
    here_ids = jnp.arange(shared_here + 2 * per_tile)
    block_of = jnp.where(
        here_ids < shared_here,
        here_ids * mlp_count + member,
        here_ids - shared_here + shared_blocks + member * 2 * per_tile,
    )
    here_slots = slot_index[block_of]
    dests = (here_slots // (slots * mlp_count)) * slots + here_slots % slots
    pix, label_total, head_b, valid_p, targets_p, picked, dests = lax.optimization_barrier(
        (pix, label_total, head_b, valid_p, targets_p, picked, dests)
    )
    cube32 = jax.ShapeDtypeStruct((frames, padded, width), f32)
    cube16 = jax.ShapeDtypeStruct((frames, padded, width), bf16)
    thin32 = jax.ShapeDtypeStruct((frames, padded, 128), f32)
    row32 = jax.ShapeDtypeStruct((8, width), f32)
    group_rows = GROUPS_AT_ONCE * GROUP
    frame_rows = FRAMES_AT_ONCE * padded
    group_spec = pl.BlockSpec((frames, group_rows, width), lambda g, *_: (0, g, 0))
    group_thin = pl.BlockSpec((frames, group_rows, 128), lambda g, *_: (0, g, 0))
    patch_spec = pl.BlockSpec((group_rows, width), lambda g, *_: (g, 0))
    frame_spec = pl.BlockSpec((FRAMES_AT_ONCE, padded, width), lambda f, *_: (f, 0, 0))
    frame_thin = pl.BlockSpec((FRAMES_AT_ONCE, padded, 128), lambda f, *_: (f, 0, 0))
    gp_spec = pl.BlockSpec(
        (mlp_count, FRAMES_AT_ONCE, padded, width), lambda f, *_: (0, f, 0, 0)
    )
    time_grid = (-(-groups // GROUPS_AT_ONCE),)
    half_frames = frames // 2
    space_grid = (half_frames // FRAMES_AT_ONCE,)
    half_blocks = groups // 2 // GROUPS_AT_ONCE
    rest = groups - 2 * half_blocks * GROUPS_AT_ONCE
    half_rows = (half_blocks * GROUPS_AT_ONCE + rest) * GROUP
    back_grid = (half_blocks + (1 if rest else 0),)

    def half_index(s, m):
        ending = jnp.where(m[0] % 2 == 0, 2 * half_blocks, 2 * half_blocks - 1)
        return jnp.where(s < half_blocks, (m[0] % 2) * half_blocks + s, ending)

    back_spec = pl.BlockSpec((frames, group_rows, width), lambda s, i, m, c: (0, half_index(s, m), 0))
    back_thin = pl.BlockSpec((frames, group_rows, 128), lambda s, i, m, c: (0, half_index(s, m), 0))
    near_spec = pl.BlockSpec((half_frames, group_rows, width), lambda s, *_: (0, s, 0))
    act_spec = pl.BlockSpec((2, FRAMES_AT_ONCE, padded, width), lambda f, *_: (0, f, 0, 0))
    half16 = jax.ShapeDtypeStruct((half_frames, padded, width), bf16)
    half32 = jax.ShapeDtypeStruct((half_frames, padded, width), f32)
    half_thin = jax.ShapeDtypeStruct((half_frames, padded, 128), f32)
    frame_weight = lax.dynamic_slice_in_dim(frame_weight, half * half_frames, half_frames)

    def whole(*shape):
        return pl.BlockSpec(shape, lambda i, *_: (0,) * len(shape))

    rows_spec = whole(8, width)
    time_extra = whole(2 * frames * GROUP, PAIR)
    space_extra = whole(2 * padded, PAIR)
    pick_spec = whole(2 * share + 16, width)

    def call(
        kernel, name, units, scalars, grid, ins, in_specs, outs, out_specs, scratch, tiles=True
    ):
        return pl.pallas_call(
            kernel,
            grid_spec=pltpu.PrefetchScalarGridSpec(
                num_scalar_prefetch=len(scalars),
                grid=grid,
                in_specs=([any_spec] if tiles else []) + in_specs,
                out_specs=out_specs,
                scratch_shapes=scratch,
            ),
            out_shape=outs,
            compiler_params=params,
            cost_estimate=pl.CostEstimate(
                flops=units * 2 * frames * padded * width * width,
                bytes_accessed=16 * width * width,
                transcendentals=0,
            ),
            name=name,
        )(*scalars, *([gathered] if tiles else []), *ins)

    def tile_bufs(*shapes):
        return [pltpu.VMEM((rows * width, cols * width), bf16) for rows, cols in shapes]

    x1, hid0, hat0, rstd0, q_t, k_t, v_t, o_t = call(
        partial(time_forward, groups),
        "time_forward",
        14,
        [slot_index, member_s],
        time_grid,
        [pix, pos, trow, time_rows, time_q, time_k],
        [group_spec, patch_spec, whole(frames, width), rows_spec, time_extra, time_extra],
        [half32, cube16, cube16, thin32] + [cube16] * 4,
        [near_spec] + [group_spec] * 2 + [group_thin] + [group_spec] * 4,
        tile_bufs((1, 1), (1, 3), (1, 1))
        + [pltpu.VMEM((frames * group_rows, width), f32), pltpu.SemaphoreType.DMA((3,))],
    )
    (hid1, hat1, rstd1, q_s, k_s, v_s, o_s, hid2, hat2, rstd2, hat3, rstd3, gp, act, pool) = call(
        lambda s, fw, m, *refs: space_forward(s, fw, m, patches, *refs),
        "space_forward",
        15,
        [slot_index, frame_weight, member_s],
        space_grid,
        [x1, space_rows, low_rows, space_q, space_k],
        [frame_spec, rows_spec, rows_spec, space_extra, space_extra],
        [half16, half16, half_thin]
        + [half16] * 4
        + [half16, half16, half_thin, half16, half_thin]
        + [
            jax.ShapeDtypeStruct((mlp_count, half_frames, padded, width), bf16),
            jax.ShapeDtypeStruct((2, half_frames, padded, width), bf16),
            row32,
        ],
        [frame_spec, frame_spec, frame_thin]
        + [frame_spec] * 4
        + [frame_spec, frame_spec, frame_thin, frame_spec, frame_thin]
        + [gp_spec, act_spec, rows_spec],
        tile_bufs((1, 3), (1, 1), (1, mlp_count), (mlp_count, 1))
        + [pltpu.VMEM((frame_rows, mlp_count * width), bf16), pltpu.SemaphoreType.DMA((4,))],
    )

    pool_other = swap(pool, "mlp", 1)
    middle = width // 2
    squares16 = jax.ShapeDtypeStruct((2, 2, width, middle), bf16)
    pair16 = jax.ShapeDtypeStruct((2, half_frames, padded, width), bf16)
    dx2, g3, du, rows_low, small = call(
        lambda s, fw, m, *refs: mlp_backward(s, fw, m, patches, *refs),
        "mlp_backward",
        9,
        [slot_index, frame_weight, member_s],
        space_grid,
        [
            pool, pool_other, head_b, valid_p, targets_p, label_total[None],
            hat2, rstd2, hat3, rstd3, gp, low_rows,
        ],
        [
            rows_spec, rows_spec, whole(width, class_pad), whole(1, class_pad), whole(1, class_pad),
            pl.BlockSpec(memory_space=pltpu.SMEM),
            frame_spec, frame_thin, frame_spec, frame_thin, gp_spec, rows_spec,
        ],
        [half32, half16, pair16, row32, row32],
        [frame_spec, frame_spec, act_spec, rows_spec, rows_spec],
        tile_bufs((1, mlp_count), (mlp_count, 1))
        + [
            pltpu.VMEM((frame_rows, mlp_count * width), bf16),
            pltpu.VMEM((8, width), f32),
            pltpu.VMEM((5, 8, width), f32),
            pltpu.SemaphoreType.DMA((2,)),
        ],
    )

    grads_spec = pl.BlockSpec((FRAMES_AT_ONCE, padded, 4 * width), lambda f, *_: (f, 0, 0))
    g1, grads_space, norm_space = call(
        space_backward,
        "space_backward",
        11,
        [slot_index],
        space_grid,
        [dx2, hat1, rstd1, q_s, k_s, v_s, space_rows, space_q, space_k],
        [frame_spec] * 2 + [frame_thin] + [frame_spec] * 3 + [rows_spec, space_extra, space_extra],
        [half16, jax.ShapeDtypeStruct((half_frames, padded, 4 * width), bf16), row32],
        [frame_spec, grads_spec, rows_spec],
        tile_bufs((1, 3), (1, 1))
        + [
            pltpu.VMEM((2, 8, width), f32),
            pltpu.VMEM((frame_rows, width), bf16),
            pltpu.SemaphoreType.DMA((2,)),
        ],
    )

    def patches_of(grad, which):
        main = half_blocks * group_rows
        here = lax.dynamic_slice_in_dim(grad, which * main, main, 1)
        return jnp.concatenate([here, grad[:, 2 * main :]], axis=1)

    leaving, near, late_hid1, late_hid2 = lax.optimization_barrier(
        (patches_of(g1, 1 - half), patches_of(g1, half), hid1, hid2)
    )
    far = swap(leaving, "mlp", 1)
    clip_spec = whole(half_frames, padded, width)
    one_spec = pl.BlockSpec((1, half_frames, padded, width), lambda i, c: (i, 0, 0, 0))
    square_spec = pl.BlockSpec((1, 2, width, middle), lambda i, c: (i, 0, 0, 0))
    keep_mlp, send_mlp = call(
        mlp_weights,
        "mlp_weights",
        2,
        [core_s],
        (2,),
        [late_hid2, g3, du, act],
        [clip_spec, clip_spec, one_spec, one_spec],
        [squares16] * 2,
        [square_spec] * 2,
        [pltpu.VMEM((2, width, width), f32)],
        tiles=False,
    )
    met_mlp = swap(send_mlp, "dp", 1)
    keep_space, send_space, sums_space = call(
        space_weights,
        "space_weights",
        2,
        [core_s],
        (4,),
        [picked, late_hid1, o_s, grads_space],
        [
            pick_spec, clip_spec, clip_spec,
            pl.BlockSpec((half_frames, padded, width), lambda i, c: (0, 0, i)),
        ],
        [jax.ShapeDtypeStruct((2, 4, share, middle), bf16)] * 2
        + [jax.ShapeDtypeStruct((4, 8, width), f32)],
        [pl.BlockSpec((2, 1, share, middle), lambda i, c: (0, i, 0, 0))] * 2
        + [pl.BlockSpec((1, 8, width), lambda i, c: (i, 0, 0))],
        [pltpu.VMEM((2 * share + 16, half_frames * padded), bf16),
         pltpu.VMEM((2 * share + 16, width), f32)],
        tiles=False,
    )
    far, keep_space, send_space = lax.optimization_barrier((far, keep_space, send_space))
    met_space = swap(send_space, "dp", 1)
    chip_mlp = added(keep_mlp[1], met_mlp[1]).astype(bf16)
    chip_space = added(keep_space[1], met_space[1]).astype(bf16)
    far, chip_mlp, chip_space = lax.optimization_barrier((far, chip_mlp, chip_space))
    far_mlp = swap(chip_mlp, "mlp", 1)
    far_space = swap(chip_space, "mlp", 1)
    keep_time, send_time, rows_time, grad_pos, grad_frames = call(
        partial(time_backward, rest),
        "time_backward",
        18,
        [slot_index, member_s, core_s],
        back_grid,
        [near, far, hid0, hat0, rstd0, q_t, k_t, v_t, o_t, pix, time_rows, picked, time_q, time_k],
        [near_spec] * 2
        + [back_spec] * 2
        + [back_thin]
        + [back_spec] * 5
        + [rows_spec, pick_spec, time_extra, time_extra],
        [jax.ShapeDtypeStruct((2, 5, share, middle), bf16)] * 2
        + [
            row32,
            jax.ShapeDtypeStruct((half_rows, width), f32),
            jax.ShapeDtypeStruct((frames, width), f32),
        ],
        [whole(2, 5, share, middle)] * 2 + [rows_spec, patch_spec, whole(frames, width)],
        tile_bufs((1, 3), (1, 1))
        + [
            pltpu.VMEM((2 * share + 16, 3 * width), f32),
            pltpu.VMEM((2 * share + 16, width), f32),
        ]
        + [
            pltpu.VMEM((2 * share + 16, width), f32),
            pltpu.VMEM((2, 8, width), f32),
            pltpu.VMEM((frames, group_rows, 3 * width), bf16),
            pltpu.VMEM((frames, group_rows, width), bf16),
            pltpu.SemaphoreType.DMA((2,)),
        ],
    )

    send_time, far_mlp, far_space = lax.optimization_barrier((send_time, far_mlp, far_space))
    met_time = swap(send_time, "dp", 1)
    chip_time = added(keep_time[1], met_time[1]).astype(bf16)
    chip_time, grad_frames, grad_pos = lax.optimization_barrier(
        (chip_time, grad_frames, grad_pos)
    )
    far_time = swap(chip_time, "mlp", 1)
    grad_time = jnp.einsum("ft,fd->td", time_hot, grad_frames, precision=highest)
    main = half_blocks * group_rows
    all_pos = jnp.concatenate(
        [jnp.where(half == i, grad_pos[:main], 0.0) for i in range(2)] + [grad_pos[main:]]
    )
    table_rows = tables.shape[0]
    table_part = jnp.concatenate(
        [
            jnp.sum(grad_frames, axis=0, keepdims=True),
            rows_time[:5],
            norm_space[:2],
            sums_space[0, :1],
            sums_space[2, :1],
            sums_space[3, :1],
            rows_low[:5],
            all_pos[:patches],
            grad_time,
        ]
    )
    rows_each = -(-table_rows // (dp_count * mlp_count))
    table_part = jnp.pad(
        table_part, ((0, rows_each * dp_count * mlp_count - table_rows), (0, 0))
    ).reshape(dp_count, mlp_count, rows_each, width)

    def table_of(which):
        rows_now = lax.dynamic_index_in_dim(table_part, which, 1, False).astype(bf16)
        return jnp.pad(rows_now, ((0, 0), (0, 16 - rows_each), (0, 0)))

    table_pair = jnp.stack([table_of(member), table_of(member ^ 1)])
    columns = jnp.stack([table_pair[..., :middle], table_pair[..., middle:]])
    keep_table = lax.dynamic_index_in_dim(columns, place % 2, 0, False)
    met_table = swap(lax.dynamic_index_in_dim(columns, 1 - place % 2, 0, False), "dp", 1)
    far_table = swap(added(keep_table[1], met_table[1]).astype(bf16), "mlp", 1)

    def blocks_of(*parts):
        return [part.reshape(part.shape[0], -1, BR, middle) for part in parts]

    sources = (
        blocks_of(keep_time, keep_space, keep_mlp)
        + [keep_table]
        + blocks_of(met_time, met_space, met_mlp)
        + [met_table]
        + [part.reshape(-1, BR, middle) for part in (far_time, far_space, far_mlp)]
        + [far_table]
    )
    bits = dp_count.bit_length() - 1
    chunk = jax.ShapeDtypeStruct((dp_count // 4, slots * BR + 16, middle), bf16)
    packed = pl.pallas_call(
        partial(pack, bits),
        grid_spec=pltpu.PrefetchScalarGridSpec(
            num_scalar_prefetch=2,
            grid=(1,),
            in_specs=[
                pl.BlockSpec((1,) + part.shape[1:], lambda i, *_: (0, 0, 0, 0))
                if part.ndim == 4
                else whole(*part.shape)
                for part in sources
            ],
            out_specs=[any_spec] * 4,
            scratch_shapes=[pltpu.VMEM(part.shape, bf16) for part in sources[8:]]
            + [pltpu.SemaphoreType.DMA((4,))],
        ),
        out_shape=[chunk] * 4,
        compiler_params=params,
        name="pack",
    )(dests, place[None], *sources)
    sum_a, sum_b = (value.reshape(value.shape[-2:]) for value in halve(*packed, "dp"))
    even = place % 2 == 0
    mine = jnp.where(even, sum_a, sum_b)
    met = swap(jnp.where(even, sum_b, sum_a), "dp", 1)
    summed = jnp.concatenate([jnp.where(even, mine, met), jnp.where(even, met, mine)], axis=1)
    my_slots = (place * mlp_count + member) * slots + jnp.arange(slots)
    filled = jnp.any(slot_index[:, None] == my_slots[None, :], axis=0)
    filled = jnp.repeat(filled, BR)[:, None]
    own_grad = jnp.where(filled, summed[: slots * BR], 0.0)
    squares_own = jnp.sum(own_grad * own_grad)
    block = jnp.concatenate(
        [
            jnp.pad(summed[slots * BR : slots * BR + rows_each], ((0, 7 - rows_each), (0, 0))),
            jnp.broadcast_to(squares_own, (1, width)),
            small,
        ]
    )
    blocks = jnp.concatenate(
        [spread_four(block[:8], "mlp"), block[None, 8:]], axis=0
    )
    blocks = lax.all_gather(blocks, "dp", axis=0)
    heads, blocks = blocks[:, mlp_count], blocks[:, :mlp_count]
    grad_head = jnp.einsum("cd,ck->dk", heads[:, 0], heads[:, 1, :classes], precision=highest)
    loss_sum = jnp.sum(heads[:, 2, 0])
    grad_tables = blocks[:, :, :rows_each].reshape(-1, width)[:table_rows]
    grad_norm = jnp.sqrt(
        jnp.sum(blocks[:, :, 7, 0])
        + jnp.sum(grad_tables * grad_tables)
        + jnp.sum(grad_head * grad_head)
    )
    factor = jnp.minimum(1.0, clip_max / (grad_norm + 1e-06))
    new_slots = adamw(
        slot_weight, own_grad * factor, slot_moment1, slot_moment2, decay_rate, learn_rate
    )
    new_tabs = adamw(tables, grad_tables * factor, table_moment1, table_moment2, 0.0, table_rate)
    new_heads = adamw(
        head_weight, grad_head * factor, head_moment1, head_moment2, decay_rate, learn_rate
    )
    return (
        loss_sum,
        label_total,
        grad_norm,
        new_slots[0],
        new_slots[1],
        new_slots[2],
        new_tabs[0],
        new_tabs[1],
        new_tabs[2],
        new_heads[0],
        new_heads[1],
        new_heads[2],
    )


def solution(mesh):
    return jax.shard_map(
        local,
        mesh=mesh,
        in_specs=(
            P("dp", None, None, None),
            P("dp"),
            P("dp", None),
            P("dp", None),
            P("dp", None),
            P("dp", None),
            P(),
            P(("dp", "mlp"), None),
            P(("dp", "mlp"), None),
            P(("dp", "mlp"), None),
            P(),
            P(),
            P(),
            P(),
            P(),
            P(),
        ),
        out_specs=(
            P(),
            P(),
            P(),
            P(("dp", "mlp"), None),
            P(("dp", "mlp"), None),
            P(("dp", "mlp"), None),
            P(),
            P(),
            P(),
            P(),
            P(),
            P(),
        ),
        check_vma=False,
    )
```

```python
from functools import partial

import jax
import jax.numpy as jnp
from jax import lax
from jax.experimental import pallas as pl
from jax.experimental.pallas import tpu as pltpu
from jax.sharding import PartitionSpec as P

HEADS = 12
HEAD_DIM = 64
TROWS = 8
BR = 48
STEP = 10
GROUP = 16
PAIR = 2 * HEAD_DIM
GROUPS_AT_ONCE = 2
FRAMES_AT_ONCE = 2
VMEM_BYTES = 58 * 2**20

ln_eps = 1e-06
beta_one = 0.9
beta_two = 0.999
learn_rate = 0.05
table_rate = 0.4
decay_rate = 0.05
adam_eps = 1e-08
clip_max = 0.001
highest = lax.Precision.HIGHEST
f32 = jnp.float32
bf16 = jnp.bfloat16
gelu_a = 0.7978845608028654
gelu_b = 0.044715
masked = -1e30


def mm(left, right):
    return jnp.dot(left, right, preferred_element_type=f32)


def mm_nt(left, right):
    return lax.dot_general(left, right, (((1,), (1,)), ((), ())), preferred_element_type=f32)


def mm_tn(left, right):
    return lax.dot_general(left, right, (((0,), (0,)), ((), ())), preferred_element_type=f32)


def normed(values):
    centred = values - jnp.mean(values, axis=-1, keepdims=True)
    rstd = lax.rsqrt(jnp.mean(centred * centred, axis=-1, keepdims=True) + ln_eps)
    return centred * rstd, rstd


def norm_back(grad, xhat, rstd, gain):
    scaled = grad * gain
    return rstd * (
        scaled
        - jnp.mean(scaled, axis=-1, keepdims=True)
        - xhat * jnp.mean(scaled * xhat, axis=-1, keepdims=True)
    )


def fold(values):
    return jnp.sum(values.reshape(-1, 8, values.shape[-1]), axis=0)


def low_lanes():
    lane = lax.broadcasted_iota(jnp.int32, (1, PAIR), 1)
    low = jnp.where(lane < HEAD_DIM, 1.0, 0.0)
    return low.astype(bf16), (1.0 - low).astype(bf16)


def pick_half(stacked):
    rows = stacked.shape[0] // 2
    lane = lax.broadcasted_iota(jnp.int32, (rows, PAIR), 1)
    return jnp.where(lane < HEAD_DIM, stacked[:rows], stacked[rows:])


def fetch(slots_ref, source, target, sem, first, across):
    width = source.shape[2]
    per_tile = width // BR

    def one(i, carry):
        tile, row = i // per_tile, pl.multiple_of((i % per_tile) * BR, 16)
        place = pl.ds(row, BR)
        if across:
            into = target.at[place, pl.ds(pl.multiple_of(tile * width, width), width)]
        else:
            into = target.at[pl.ds(pl.multiple_of(tile * width, 16) + row, BR)]
        block = first(tile) * per_tile + i % per_tile
        pltpu.make_async_copy(source.at[slots_ref[block]], into, sem).start()
        return carry

    count = target.shape[0] * target.shape[1] // (width * width)
    lax.fori_loop(0, count * per_tile, one, 0)


def arrive(target, sem):
    pltpu.make_async_copy(target, target, sem).wait()


def jobs_of(count):
    pairs = [slice(p * PAIR, (p + 1) * PAIR) for p in range(HEADS // 2)]
    return [(i, lanes) for i in range(count) for lanes in pairs]


def each_row(count, begin, finish):
    def one(i, carry):
        in_flight([(i, lanes) for unused, lanes in jobs_of(1)], begin, finish)
        return carry

    lax.fori_loop(0, count, one, 0)


def in_flight(jobs, begin, finish):
    waiting = None
    for job in jobs:
        started = begin(*job)
        if waiting is not None:
            finish(*waiting)
        waiting = job + started
    finish(*waiting)


def attend(count, load, store, extra_q, extra_k):
    low, high = low_lanes()

    def begin(i, lanes):
        queries, keys, values = load(i, lanes)
        both = jnp.concatenate([queries * low, queries * high], axis=0)
        scores = mm_nt(
            jnp.concatenate([both, extra_q[...]], axis=1),
            jnp.concatenate([keys, extra_k[: keys.shape[0]]], axis=1),
        )
        return values, scores

    def finish(i, lanes, values, scores):
        top = jnp.max(scores, axis=-1, keepdims=True)
        weights = jnp.exp(scores - top).astype(bf16)
        summed = mm(weights, jnp.concatenate([values, jnp.ones_like(values)], axis=1))
        merged = pick_half(summed[:, :PAIR]) / pick_half(summed[:, PAIR:])
        store(i, lanes, merged.astype(bf16))

    in_flight(jobs_of(count), begin, finish)


def attend_back(count, load, store, extra_q, extra_k, looped=False):
    low, high = low_lanes()

    def begin(i, lanes):
        queries, keys, values, grads = load(i, lanes)
        both_k = jnp.concatenate([keys * low, keys * high], axis=0)
        both_v = jnp.concatenate([values * low, values * high], axis=0)
        scores = mm_nt(
            jnp.concatenate([both_k, extra_k[...]], axis=1),
            jnp.concatenate([queries, extra_q[: queries.shape[0]]], axis=1),
        )
        return queries, both_k, grads, scores, mm_nt(both_v, grads)

    def finish(i, lanes, queries, both_k, grads, scores, back):
        rows = queries.shape[0]
        soft, inner = [], []
        for half in (slice(0, rows), slice(rows, 2 * rows)):
            part = scores[half]
            weights = jnp.exp(part - jnp.max(part, axis=0, keepdims=True))
            weights = weights * (1.0 / jnp.sum(weights, axis=0, keepdims=True))
            delta = back[half] - jnp.sum(weights * back[half], axis=0, keepdims=True)
            soft.append(weights.astype(bf16))
            inner.append((weights * delta).astype(bf16))
        soft = jnp.concatenate(soft, axis=0)
        inner = jnp.concatenate(inner, axis=0)
        store(
            i,
            lanes,
            (mm_tn(inner, both_k) * HEAD_DIM ** (-0.5)).astype(bf16),
            pick_half(mm(inner, queries)).astype(bf16),
            pick_half(mm(soft, grads)).astype(bf16),
        )

    if looped:
        each_row(count, begin, finish)
    else:
        in_flight(jobs_of(count), begin, finish)


def project(hidden, rows, tiles):
    width = hidden.shape[1]
    joint = mm(hidden, tiles[...])
    queries = (joint[:, :width] + rows[2:3]).astype(bf16) * jnp.asarray(HEAD_DIM ** (-0.5), bf16)
    keys = joint[:, width : 2 * width].astype(bf16)
    values = (joint[:, 2 * width :] + rows[3:4]).astype(bf16)
    return queries, keys, values


def keep_norm(stream, rows, at, hid_ref, hat_ref, rstd_ref, here, cut):
    xhat, rstd = normed(stream)
    hat_ref[here] = xhat.astype(bf16).reshape(cut)
    rstd_ref[here] = jnp.broadcast_to(rstd, (rstd.shape[0], 128)).reshape(cut[:-1] + (128,))
    hidden = (xhat * rows[at : at + 1] + rows[at + 1 : at + 2]).astype(bf16)
    if hid_ref is not None:
        hid_ref[here] = hidden.reshape(cut)
    return xhat, hidden


def by_groups(block, total, work):
    step = pl.program_id(0)
    full, rest = total // block, total % block
    if rest == 0:
        work(block)
    else:
        pl.when(step < full)(lambda: work(block))
        pl.when(step == full)(lambda: work(rest))


def time_forward(
    total, slots, member, gathered, pixels, pos, trow, rows, extra_q, extra_k,
    x1_ref, hid_ref, hat_ref, rstd_ref, q_ref, k_ref, v_ref, o_ref,
    embed, joint, out, base, sems,
):
    frames, span, width = hid_ref.shape

    @pl.when(pl.program_id(0) == 0)
    def _():
        fetch(slots, gathered, embed, sems.at[0], lambda t: t, False)
        fetch(slots, gathered, joint, sems.at[1], lambda t: t + 1, True)
        fetch(slots, gathered, out, sems.at[2], lambda t: t + 4, False)
        arrive(embed, sems.at[0])

    def first(target, sem):
        pl.when(pl.program_id(0) == 0)(lambda: arrive(target, sem))

    def work(count):
        cut = (frames, count * GROUP, width)
        flat = (frames * count * GROUP, width)
        here = slice(0, count * GROUP)
        every = (slice(None), here)
        offset = (pos[here][None] + trow[...][:, None]).reshape(flat)
        stream = mm(pixels[:, here].reshape(flat), embed[...]) + offset
        base[: flat[0]] = stream
        rows_now = rows[...]
        unused, hidden = keep_norm(stream, rows_now, 0, hid_ref, hat_ref, rstd_ref, every, cut)
        first(joint, sems.at[1])
        queries, keys, values = project(hidden, rows_now, joint)
        q_ref[:, here] = queries.reshape(cut)
        k_ref[:, here] = keys.reshape(cut)
        v_ref[:, here] = values.reshape(cut)

        def load(g, lanes):
            part = slice(g * GROUP, (g + 1) * GROUP)
            return tuple(
                ref[:, part, lanes].reshape(frames * GROUP, PAIR) for ref in (q_ref, k_ref, v_ref)
            )

        def store(g, lanes, merged):
            part = slice(g * GROUP, (g + 1) * GROUP)
            o_ref[:, part, lanes] = merged.reshape(frames, GROUP, PAIR)

        attend(count, load, store, extra_q, extra_k)
        first(out, sems.at[2])
        near, some = frames // 2, flat[0] // 2
        late = member[0] % 2
        merged = o_ref[pl.ds(late * near, near), here].reshape(some, width)
        stream = base[pl.ds(pl.multiple_of(late * some, 16), some)] + mm(merged, out[...])
        x1_ref[:, here] = (stream + rows_now[4:5]).reshape(near, count * GROUP, width)

    by_groups(span // GROUP, total, work)


def space_forward(
    slots, frame_weight, member, patches, gathered, x1, rows, low_rows, extra_q, extra_k,
    hid1_ref, hat1_ref, rstd1_ref, q_ref, k_ref, v_ref, o_ref,
    hid2_ref, hat2_ref, rstd2_ref, hat3_ref, rstd3_ref, gp_ref, act_ref, pool_ref,
    joint, out, ups, downs, acts, sems,
):
    step = pl.program_id(0)
    members = gp_ref.shape[0]
    cut = x1.shape
    span, count, width = cut
    flat = (span * count, width)
    every = (slice(None),)

    @pl.when(step == 0)
    def _():
        fetch(slots, gathered, joint, sems.at[0], lambda t: t + 5, True)
        fetch(slots, gathered, out, sems.at[1], lambda t: t + 8, False)
        fetch(slots, gathered, ups, sems.at[2], lambda t: 2 * t + 9, True)
        fetch(slots, gathered, downs, sems.at[3], lambda t: 2 * t + 10, False)
        pool_ref[...] = jnp.zeros_like(pool_ref)
        arrive(joint, sems.at[0])

    rows_now = rows[...]
    unused, hidden = keep_norm(
        x1[...].reshape(flat), rows_now, 0, hid1_ref, hat1_ref, rstd1_ref, every, cut
    )
    queries, keys, values = project(hidden, rows_now, joint)
    q_ref[...] = queries.reshape(cut)
    k_ref[...] = keys.reshape(cut)
    v_ref[...] = values.reshape(cut)

    def load(f, lanes):
        return q_ref[f, :, lanes], k_ref[f, :, lanes], v_ref[f, :, lanes]

    def store(f, lanes, merged):
        o_ref[f, :, lanes] = merged

    attend(span, load, store, extra_q, extra_k)
    pl.when(step == 0)(lambda: arrive(out, sems.at[1]))
    merged = o_ref[...].reshape(flat)
    stream = x1[...].reshape(flat) + mm(merged, out[...]) + rows_now[4:5]
    low_now = low_rows[...]
    unused, hidden = keep_norm(stream, low_now, 0, hid2_ref, hat2_ref, rstd2_ref, every, cut)

    @pl.when(step == 0)
    def _():
        arrive(ups, sems.at[2])
        arrive(downs, sems.at[3])

    def begin(j, lanes):
        return (mm(hidden, ups[:, lanes]),)

    lowered = []

    def finish(j, lanes, upper):
        cubic = gelu_a * gelu_b * (upper * upper)
        gate = 0.5 + 0.5 * jnp.tanh(upper * (gelu_a + cubic))
        active = upper * gate
        slope = gate + active * (1.0 - gate) * (2.0 * gelu_a + 6.0 * cubic)
        gp_ref[j] = slope.astype(bf16).reshape(cut)
        acts[:, lanes] = active.astype(bf16)
        lowered.append(mm(acts[:, lanes], downs[lanes]))

    in_flight([(j, slice(j * width, (j + 1) * width)) for j in range(members)], begin, finish)
    for part in lowered:
        stream = stream + part
    for i in range(2):
        own = pl.ds(pl.multiple_of((member[0] ^ i) * width, 128), width)
        act_ref[i] = acts[:, own].reshape(cut)
    stream = stream + low_now[2:3]
    xhat, rstd = normed(stream)
    hat3_ref[...] = xhat.astype(bf16).reshape(cut)
    rstd3_ref[...] = jnp.broadcast_to(rstd, (flat[0], 128)).reshape(span, count, 128)
    final = xhat * low_now[3:4] + low_now[4:5]
    row = lax.broadcasted_iota(jnp.int32, (count, 1), 0)
    for f in range(span):
        part = jnp.where(row < patches, final[f * count : (f + 1) * count], 0.0)
        pool_ref[...] += fold(part) * frame_weight[step * span + f]


def mlp_backward(
    slots, frame_weight, member, patches, gathered, pool, pool_other, head, valid, targets, total,
    hat2, rstd2, hat3, rstd3, gp, low_rows,
    dx2_ref, g3_ref, du_ref, rows_ref, small_ref,
    ups, downs, dus, spread, row_sums, sems,
):
    step = pl.program_id(0)
    members = gp.shape[0]
    cut = hat2.shape
    span, count, width = cut
    flat = (span * count, width)

    @pl.when(step == 0)
    def _():
        fetch(slots, gathered, downs, sems.at[1], lambda t: 2 * t + 10, False)
        fetch(slots, gathered, ups, sems.at[0], lambda t: 2 * t + 9, True)
        pooled = jnp.sum(pool[...] + pool_other[...], axis=0, keepdims=True).astype(bf16)
        pooled8 = jnp.broadcast_to(pooled, (8, width))
        logits = mm(pooled8, head[...])
        valid_f = valid[...]
        target = targets[...]
        soft = jnp.maximum(logits, 0.0) + jnp.log(1.0 + jnp.exp(-jnp.abs(logits)))
        loss = jnp.sum(valid_f * (soft - target * logits), axis=1, keepdims=True)
        sig = 1.0 / (1.0 + jnp.exp(-logits))
        grad = (valid_f * (sig - target) / jnp.maximum(total[0], 1.0)).astype(bf16)
        spread[...] = mm_nt(grad, head[...])
        small_ref[...] = jnp.zeros_like(small_ref)
        small_ref[0:1, :] = pooled.astype(f32)
        small_ref[1:2, 0 : grad.shape[1]] = grad[0:1].astype(f32)
        small_ref[2:3, 0:128] = jnp.broadcast_to(loss[0:1], (1, 128))
        row_sums[...] = jnp.zeros_like(row_sums)
        arrive(downs, sems.at[1])

    low_now = low_rows[...]
    row = lax.broadcasted_iota(jnp.int32, (count, 1), 0)
    weight = jnp.concatenate(
        [jnp.where(row < patches, frame_weight[step * span + f], 0.0) for f in range(span)]
    )
    grad_final = spread[0:1] * weight
    xhat = hat3[...].reshape(flat).astype(f32)
    rstd = rstd3[...].reshape(flat[0], 128)[:, 0:1]
    row_sums[3] += fold(grad_final * xhat)
    row_sums[4] += fold(grad_final)
    grad_top = norm_back(grad_final, xhat, rstd, low_now[3:4])
    row_sums[2] += fold(grad_top)
    grad_b = grad_top.astype(bf16)
    g3_ref[...] = grad_b.reshape(cut)

    for j in range(members):
        lanes = slice(j * width, (j + 1) * width)
        du = mm_nt(grad_b, downs[lanes]) * gp[j].reshape(flat).astype(f32)
        dus[:, lanes] = du.astype(bf16)

    @pl.when(step == 0)
    def _():
        arrive(ups, sems.at[0])

    grad_hidden = mm_nt(dus[...], ups[...])
    for i in range(2):
        own = pl.ds(pl.multiple_of((member[0] ^ i) * width, 128), width)
        du_ref[i] = dus[:, own].reshape(cut)
    xhat = hat2[...].reshape(flat).astype(f32)
    rstd = rstd2[...].reshape(flat[0], 128)[:, 0:1]
    row_sums[0] += fold(grad_hidden * xhat)
    row_sums[1] += fold(grad_hidden)
    dx2_ref[...] = (grad_top + norm_back(grad_hidden, xhat, rstd, low_now[0:1])).reshape(cut)

    @pl.when(step == pl.num_programs(0) - 1)
    def _():
        rows_ref[...] = jnp.zeros_like(rows_ref)
        for i in range(5):
            rows_ref[i : i + 1] = jnp.sum(row_sums[i], axis=0, keepdims=True)


def mlp_weights(core, hid2, g3, du, act, keep_ref, send_ref, sums):
    rows, width = hid2.shape[0] * hid2.shape[1], hid2.shape[2]
    sums[0] = mm_tn(hid2[...].reshape(rows, width), du[0].reshape(rows, width))
    sums[1] = mm_tn(act[0].reshape(rows, width), g3[...].reshape(rows, width))
    for ref, half in zip((keep_ref, send_ref), column_halves(core[0], width)):
        for n in range(2):
            ref[0, n] = sums[n, :, half].astype(bf16)


def space_weights(core, picked, hid1, o, grads, keep_ref, send_ref, rows_ref, left, sums):
    step = pl.program_id(0)
    rows, width = hid1.shape[0] * hid1.shape[1], hid1.shape[2]
    share = keep_ref.shape[2]

    def select(source):
        chosen = mm_nt(picked[...], source[...].reshape(rows, width)).astype(bf16)
        left[...] = chosen + ones_row(picked)

    pl.when(step == 0)(lambda: select(hid1))
    pl.when(step == pl.num_programs(0) - 1)(lambda: select(o))
    sums[...] = mm(left[...], grads[...].reshape(rows, width))
    for ref, half in zip((keep_ref, send_ref), column_halves(core[0], width)):
        for n in range(2):
            ref[n, 0] = sums[n * share : (n + 1) * share, half].astype(bf16)
    rows_ref[0] = sums[2 * share : 2 * share + 8]


def close_attention(
    grad_stream, grad_b, hidden, xhat, rstd, grads, merged, rows_now, picked, ones, joint,
    joint_sum, out_sum, row_sums,
):
    grad_hidden = mm_nt(grads, joint[...])
    hidden_t = mm_nt(picked, hidden).astype(bf16) + ones
    merged_t = mm_nt(picked, merged).astype(bf16) + ones
    joint_sum[...] += mm(hidden_t, grads)
    out_sum[...] += mm(merged_t, grad_b)
    xhat = xhat.astype(f32)
    row_sums[0] += fold(grad_hidden * xhat)
    row_sums[1] += fold(grad_hidden)
    return grad_stream + norm_back(grad_hidden, xhat, rstd[:, 0:1], rows_now[0:1])


def ones_row(picked):
    row = lax.broadcasted_iota(jnp.int32, (picked.shape[0], 1), 0)
    return jnp.where(row == picked.shape[0] - 16, 1.0, 0.0).astype(bf16)


def column_halves(core, width):
    middle = width // 2
    keep = pl.ds(pl.multiple_of(core * middle, 128), middle)
    send = pl.ds(pl.multiple_of((1 - core) * middle, 128), middle)
    return keep, send


def clear(*refs):
    for ref in refs:
        ref[...] = jnp.zeros_like(ref)


def finish_attention(core, tile_refs, at, rows_ref, joint_sum, out_sum, row_sums):
    share = tile_refs[0].shape[2]
    width = out_sum.shape[1]
    rows_ref[...] = jnp.zeros_like(rows_ref)
    for tile_ref, half in zip(tile_refs, column_halves(core, width)):
        for n in range(2):
            here = slice(n * share, (n + 1) * share)
            for i in range(3):
                start = pl.multiple_of(i * width + half.start, 128)
                columns = pl.ds(start, half.size)
                tile_ref[n, at + i] = joint_sum[here, columns].astype(bf16)
            tile_ref[n, at + 3] = out_sum[here, half].astype(bf16)
    last = slice(2 * share, 2 * share + 1)
    for i in range(2):
        rows_ref[i : i + 1] = jnp.sum(row_sums[i], axis=0, keepdims=True)
    rows_ref[2:3] = joint_sum[last, :width]
    rows_ref[3:4] = joint_sum[last, 2 * width :]
    rows_ref[4:5] = out_sum[last]


def space_backward(
    main, slots, member, gathered, dx2, hat1, rstd1, q, k, v, rows, extra_q, extra_k,
    near_ref, far_ref, grads_ref, rows_ref, joint, out, row_sums, outer, g1, sems,
):
    step = pl.program_id(0)
    cut = hat1.shape
    span, count, width = cut
    flat = (span * count, width)

    @pl.when(step == 0)
    def _():
        fetch(slots, gathered, out, sems.at[1], lambda t: t + 8, False)
        fetch(slots, gathered, joint, sems.at[0], lambda t: t + 5, True)
        clear(row_sums)
        arrive(out, sems.at[1])

    grad_b = dx2[...].reshape(flat).astype(bf16)
    grads_ref[:, :, 3 * width :] = grad_b.reshape(cut)
    outer[...] = mm_nt(grad_b, out[...]).astype(bf16)

    def load(f, lanes):
        here = pl.ds(pl.multiple_of(f * count, 16), count)
        return q[f, :, lanes], k[f, :, lanes], v[f, :, lanes], outer[here, lanes]

    def store(f, lanes, *parts):
        for i, part in enumerate(parts):
            grads_ref[f, :, i * width + lanes.start : i * width + lanes.stop] = part

    attend_back(span, load, store, extra_q, extra_k, looped=True)
    pl.when(step == 0)(lambda: arrive(joint, sems.at[0]))
    grads = grads_ref[:, :, : 3 * width].reshape(flat[0], 3 * width)
    grad_hidden = mm_nt(grads, joint[...])
    xhat = hat1[...].reshape(flat).astype(f32)
    rstd = rstd1[...].reshape(flat[0], 128)[:, 0:1]
    row_sums[0] += fold(grad_hidden * xhat)
    row_sums[1] += fold(grad_hidden)
    grad_stream = dx2[...].reshape(flat) + norm_back(grad_hidden, xhat, rstd, rows[0:1])
    g1[...] = grad_stream.astype(bf16).reshape(cut)
    late = member[0] % 2
    for ref, which in ((near_ref, late), (far_ref, 1 - late)):
        ref[:, :main] = g1[:, pl.ds(pl.multiple_of(which * main, 16), main)]
        if ref.shape[1] > main:
            ref[:, main:] = g1[:, 2 * main : main + ref.shape[1]]

    @pl.when(step == pl.num_programs(0) - 1)
    def _():
        rows_ref[...] = jnp.zeros_like(rows_ref)
        for i in range(2):
            rows_ref[i : i + 1] = jnp.sum(row_sums[i], axis=0, keepdims=True)


def time_backward(
    rest, slots, member, core, gathered, near, far, hid0, hat0, rstd0, q, k, v, o, pixels, rows, picked,
    extra_q, extra_k,
    keep_ref, send_ref, rows_ref, pos_ref, frame_ref,
    joint, out, joint_sum, out_sum, embed_sum, row_sums, grads, outer, sems,
):
    step = pl.program_id(0)
    frames, span, width = hid0.shape

    @pl.when(step == 0)
    def _():
        fetch(slots, gathered, out, sems.at[1], lambda t: t + 4, False)
        fetch(slots, gathered, joint, sems.at[0], lambda t: t + 1, True)
        clear(joint_sum, out_sum, embed_sum, row_sums, frame_ref)
        arrive(out, sems.at[1])

    def work(groups):
        cut = (frames, groups * GROUP, width)
        flat = (frames * groups * GROUP, width)
        small = (frames, GROUP, PAIR)
        here = slice(0, groups * GROUP)
        first = member[0] % 2 == 0
        near_now, far_now = near[:, here], far[:, here]
        grad_b = jnp.concatenate(
            [jnp.where(first, near_now, far_now), jnp.where(first, far_now, near_now)]
        ).reshape(flat)
        outer[:, here] = mm_nt(grad_b, out[...]).astype(bf16).reshape(cut)

        def load(g, lanes):
            part = slice(g * GROUP, (g + 1) * GROUP)
            return tuple(
                ref[:, part, lanes].reshape(frames * GROUP, PAIR) for ref in (q, k, v, outer)
            )

        def store(g, lanes, *parts):
            part = slice(g * GROUP, (g + 1) * GROUP)
            for i, value in enumerate(parts):
                span_now = slice(i * width + lanes.start, i * width + lanes.stop)
                grads[:, part, span_now] = value.reshape(small)

        attend_back(groups, load, store, extra_q, extra_k)
        pl.when(step == 0)(lambda: arrive(joint, sems.at[0]))
        picked_now = picked[...]
        grad = close_attention(
            grad_b.astype(f32), grad_b, hid0[:, here].reshape(flat),
            hat0[:, here].reshape(flat), rstd0[:, here].reshape(flat[0], 128),
            grads[:, here].reshape(flat[0], 3 * width), o[:, here].reshape(flat), rows[...],
            picked_now, ones_row(picked_now), joint, joint_sum, out_sum, row_sums,
        )
        pix_t = mm_nt(picked_now, pixels[:, here].reshape(flat)).astype(bf16)
        embed_sum[...] += mm(pix_t, grad.astype(bf16))
        cube = grad.reshape(cut)
        pos_ref[here] = jnp.sum(cube, axis=0)
        frame_ref[...] += jnp.sum(cube, axis=1)

    last = step == pl.num_programs(0) - 1
    if rest == 0:
        work(span // GROUP)
    else:
        odd = member[0] % 2 == 1
        pl.when(jnp.logical_not(last))(lambda: work(span // GROUP))
        pl.when(jnp.logical_and(last, jnp.logical_not(odd)))(lambda: work(rest))

        @pl.when(jnp.logical_and(last, odd))
        def _():
            pos_ref[...] = jnp.zeros_like(pos_ref)

    @pl.when(last)
    def _():
        finish_attention(
            core[0], (keep_ref, send_ref), 1, rows_ref, joint_sum, out_sum, row_sums
        )
        share = keep_ref.shape[2]
        for ref, half in zip((keep_ref, send_ref), column_halves(core[0], width)):
            for n in range(2):
                ref[n, 0] = embed_sum[n * share : (n + 1) * share, half].astype(bf16)


def pack(bits, dests, place, *refs):
    count = (len(refs) - 5) // 4
    keeps, mets, fars = (refs[i * count : (i + 1) * count] for i in range(3))
    (stay_a, go_a, stay_b, go_b), sems = refs[3 * count : 3 * count + 4], refs[-1]
    sums = refs[-1 - count : -1]
    table_rows = sums[-1].shape[1]
    slots = (stay_a.shape[1] - table_rows) // BR
    top = bits - 1
    rest = 2 ** (bits - 2) - 1

    def route(source, chunk, rows, sem):
        differs = chunk ^ place[0]
        in_b = chunk % 2 == 1
        index_a, index_b = chunk >> 2, (chunk >> 1) & rest
        moves_a, moves_b = (differs >> 1) % 2 == 1, (differs >> top) % 2 == 1
        for flag, target, index in (
            (~in_b & ~moves_a, stay_a, index_a),
            (~in_b & moves_a, go_a, index_a),
            (in_b & ~moves_b, stay_b, index_b),
            (in_b & moves_b, go_b, index_b),
        ):

            @pl.when(flag)
            def _(target=target, index=index):
                pltpu.make_async_copy(source, target.at[index, rows], sem).start()

    first = 0
    for n, (keep, met, far, source) in enumerate(zip(keeps, mets, fars, sums)):
        table = n == count - 1

        def one(i, carry, keep=keep, met=met, far=far, source=source, first=first, n=n, table=table):
            total = keep[0, i].astype(f32) + met[0, i].astype(f32) + far[i].astype(f32)
            source[i] = total.astype(bf16)
            if table:
                route(source.at[i], i, pl.ds(slots * BR, table_rows), sems.at[n])
            else:
                dest = dests[first + i]
                row = pl.multiple_of((dest % slots) * BR, 16)
                route(source.at[i], dest // slots, pl.ds(row, BR), sems.at[n])
            return carry

        lax.fori_loop(0, source.shape[0], one, 0)
        first += source.shape[0]
    for n, source in enumerate(sums):
        pltpu.make_async_copy(source, source, sems.at[n]).wait()


def swap(value, axis, hop):
    size = lax.axis_size(axis)
    return lax.ppermute(value, axis, [(i, i ^ hop) for i in range(size)])


def added(*parts):
    total = parts[0].astype(f32)
    for part in parts[1:]:
        total = total + part.astype(f32)
    return total


def halve(stay_a, go_a, stay_b, go_b, axis):
    bits = lax.axis_size(axis).bit_length() - 1
    place = lax.axis_index(axis)
    orders = [list(range(1, bits)), list(range(bits - 1, 0, -1))]
    shape = (2,) * (bits - 2) + stay_a.shape[1:]
    going, staying = [go_a, go_b], [stay_a, stay_b]
    for stage in range(bits - 1):
        met = [swap(value, axis, 1 << order[stage]) for value, order in zip(going, orders)]
        values = [added(stay, come) for stay, come in zip(staying, met)]
        if stage == bits - 2:
            return values
        going, staying = [], []
        for value, order in zip(values, orders):
            alive = sorted(order[stage + 1 :], reverse=True)
            value = value.reshape(shape[stage:])
            at = alive.index(order[stage + 1])
            bit = (place >> order[stage + 1]) & 1
            going.append(lax.dynamic_index_in_dim(value, 1 - bit, at, False).astype(bf16))
            staying.append(lax.dynamic_index_in_dim(value, bit, at, False))


def spread_four(value, axis):
    size = lax.axis_size(axis)
    place = lax.axis_index(axis)
    value = value[None]
    hop = 1
    while hop < size:
        come = swap(value, axis, hop)
        low = (place & hop) == 0
        value = jnp.concatenate(
            [jnp.where(low, value, come), jnp.where(low, come, value)], axis=0
        )
        hop *= 2
    return value


def block_ranks(owners):
    total_blocks = owners.shape[0]
    same_owner = owners[:, None] == owners[None, :]
    earlier = jnp.arange(total_blocks)[None, :] < jnp.arange(total_blocks)[:, None]
    return jnp.sum((same_owner & earlier).astype(jnp.int32), axis=1)


def adamw(weight, gradient, moment_one, moment_two, weight_decay, rate):
    first_new = beta_one * moment_one + (1.0 - beta_one) * gradient
    second_new = beta_two * moment_two + (1.0 - beta_two) * gradient * gradient
    mean_hat = first_new / (1.0 - beta_one**STEP)
    var_hat = second_new / (1.0 - beta_two**STEP)
    updated = weight - rate * (mean_hat / (jnp.sqrt(var_hat) + adam_eps) + weight_decay * weight)
    return (updated, first_new, second_new)


def local(
    pixels,
    lengths,
    frame_mask,
    time_index,
    label_valid,
    targets,
    owners,
    slot_weight,
    slot_moment1,
    slot_moment2,
    tables,
    table_moment1,
    table_moment2,
    head_weight,
    head_moment1,
    head_moment2,
):
    dp_count = lax.axis_size("dp")
    mlp_count = lax.axis_size("mlp")
    member = lax.axis_index("mlp").astype(jnp.int32)
    width = slot_weight.shape[1]
    per_tile = width // BR
    slots = slot_weight.shape[0] // BR
    shared_blocks = 9 * per_tile
    frames, patches = pixels.shape[1], pixels.shape[2]
    padded = -(-patches // GROUP) * GROUP
    groups = padded // GROUP
    classes = head_weight.shape[1]
    class_pad = -(-classes // 128) * 128
    params = pltpu.CompilerParams(vmem_limit_bytes=VMEM_BYTES)
    any_spec = pl.BlockSpec(memory_space=pl.ANY)

    gathered = lax.all_gather(slot_weight.astype(bf16), ("dp", "mlp"), axis=0, tiled=True)
    gathered = gathered.reshape(-1, BR, width)
    slot_index = (owners * slots + block_ranks(owners)).astype(jnp.int32)

    pix = jnp.pad(pixels[0], ((0, 0), (0, padded - patches), (0, 0)))
    slot_pos = jnp.arange(frames)
    frame_live = slot_pos < lengths[0]
    key_ok = frame_live & (frame_mask[0] == 1)
    allowed = key_ok[None, :] | (slot_pos[:, None] == slot_pos[None, :])
    extra_lane = jnp.arange(HEAD_DIM)
    flat_id = jnp.arange(frames * GROUP)
    frame_id, patch_id = flat_id // GROUP, flat_id % GROUP
    lane_frame = jnp.clip(extra_lane - GROUP, 0, frames - 1)
    in_patch = (extra_lane < GROUP)[None, :]
    in_frame = ((extra_lane >= GROUP) & (extra_lane < GROUP + frames))[None, :]
    same_patch = patch_id[:, None] == extra_lane[None, :]
    same_frame = frame_id[:, None] == lane_frame[None, :]
    time_q = (in_patch & same_patch) | (in_frame & same_frame)
    time_k = (in_patch & ~same_patch) | (in_frame & ~allowed.T[frame_id][:, lane_frame])
    is_pad = (jnp.arange(padded) >= patches)[:, None]
    space_q = jnp.broadcast_to(extra_lane[None, :] == 0, (padded, HEAD_DIM))
    space_k = is_pad & (extra_lane[None, :] == 0)

    def widen(flags, value):
        block = jnp.where(flags, value, 0.0).astype(bf16)
        block = jnp.pad(block, ((0, 0), (0, PAIR - HEAD_DIM)))
        return jnp.concatenate([block, block])

    time_q, time_k = widen(time_q, 1.0), widen(time_k, masked)
    space_q, space_k = widen(space_q, 1.0), widen(space_k, masked)
    time_hot = (time_index[0][:, None] == jnp.arange(TROWS)[None, :]).astype(f32)
    trow = jnp.einsum("ft,td->fd", time_hot, tables[16 + patches :], precision=highest)
    pos = jnp.pad(tables[16 : 16 + patches] + tables[0], ((0, padded - patches), (0, 0)))
    frame_weight = jnp.where(
        frame_live, 1.0 / (lengths[0] * patches).astype(f32), 0.0
    ).astype(f32)
    valid_f = label_valid.astype(f32)
    label_total = lax.psum(jnp.sum(valid_f), "dp")
    head_b = jnp.pad(head_weight.astype(bf16), ((0, 0), (0, class_pad - classes)))
    valid_p = jnp.pad(valid_f, ((0, 0), (0, class_pad - classes)))
    targets_p = jnp.pad(targets, ((0, 0), (0, class_pad - classes)))
    share = width // mlp_count
    half = member % 2
    place = lax.axis_index("dp").astype(jnp.int32)
    core_s = (place % 2)[None]
    pick_row = jnp.arange(2 * share)
    pick_member = jnp.where(pick_row < share, member, member ^ 1)
    pick_row = pick_row % share
    pick_feature = (pick_row // BR) * (BR * mlp_count) + pick_member * BR + pick_row % BR
    picked = (pick_feature[:, None] == jnp.arange(width)[None, :]).astype(bf16)
    picked = jnp.pad(picked, ((0, 16), (0, 0)))
    member_s = member[None]
    time_rows = jnp.pad(tables[1:6], ((0, 3), (0, 0)))
    space_rows = jnp.pad(tables[6:11], ((0, 3), (0, 0)))
    low_rows = jnp.pad(tables[11:16], ((0, 3), (0, 0)))

    shared_here = shared_blocks // mlp_count
    here_ids = jnp.arange(shared_here + 2 * per_tile)
    block_of = jnp.where(
        here_ids < shared_here,
        here_ids * mlp_count + member,
        here_ids - shared_here + shared_blocks + member * 2 * per_tile,
    )
    here_slots = slot_index[block_of]
    dests = (here_slots // (slots * mlp_count)) * slots + here_slots % slots
    pix, label_total, head_b, valid_p, targets_p, picked, dests = lax.optimization_barrier(
        (pix, label_total, head_b, valid_p, targets_p, picked, dests)
    )
    cube32 = jax.ShapeDtypeStruct((frames, padded, width), f32)
    cube16 = jax.ShapeDtypeStruct((frames, padded, width), bf16)
    thin32 = jax.ShapeDtypeStruct((frames, padded, 128), f32)
    row32 = jax.ShapeDtypeStruct((8, width), f32)
    group_rows = GROUPS_AT_ONCE * GROUP
    frame_rows = FRAMES_AT_ONCE * padded
    group_spec = pl.BlockSpec((frames, group_rows, width), lambda g, *_: (0, g, 0))
    group_thin = pl.BlockSpec((frames, group_rows, 128), lambda g, *_: (0, g, 0))
    patch_spec = pl.BlockSpec((group_rows, width), lambda g, *_: (g, 0))
    frame_spec = pl.BlockSpec((FRAMES_AT_ONCE, padded, width), lambda f, *_: (f, 0, 0))
    frame_thin = pl.BlockSpec((FRAMES_AT_ONCE, padded, 128), lambda f, *_: (f, 0, 0))
    gp_spec = pl.BlockSpec(
        (mlp_count, FRAMES_AT_ONCE, padded, width), lambda f, *_: (0, f, 0, 0)
    )
    time_grid = (-(-groups // GROUPS_AT_ONCE),)
    half_frames = frames // 2
    space_grid = (half_frames // FRAMES_AT_ONCE,)
    half_blocks = groups // 2 // GROUPS_AT_ONCE
    rest = groups - 2 * half_blocks * GROUPS_AT_ONCE
    half_rows = (half_blocks * GROUPS_AT_ONCE + rest) * GROUP
    back_grid = (half_blocks + (1 if rest else 0),)

    def half_index(s, m):
        ending = jnp.where(m[0] % 2 == 0, 2 * half_blocks, 2 * half_blocks - 1)
        return jnp.where(s < half_blocks, (m[0] % 2) * half_blocks + s, ending)

    back_spec = pl.BlockSpec((frames, group_rows, width), lambda s, i, m, c: (0, half_index(s, m), 0))
    back_thin = pl.BlockSpec((frames, group_rows, 128), lambda s, i, m, c: (0, half_index(s, m), 0))
    near_spec = pl.BlockSpec((half_frames, group_rows, width), lambda s, *_: (0, s, 0))
    act_spec = pl.BlockSpec((2, FRAMES_AT_ONCE, padded, width), lambda f, *_: (0, f, 0, 0))
    half16 = jax.ShapeDtypeStruct((half_frames, padded, width), bf16)
    half32 = jax.ShapeDtypeStruct((half_frames, padded, width), f32)
    half_thin = jax.ShapeDtypeStruct((half_frames, padded, 128), f32)
    frame_weight = lax.dynamic_slice_in_dim(frame_weight, half * half_frames, half_frames)

    def whole(*shape):
        return pl.BlockSpec(shape, lambda i, *_: (0,) * len(shape))

    rows_spec = whole(8, width)
    time_extra = whole(2 * frames * GROUP, PAIR)
    space_extra = whole(2 * padded, PAIR)
    pick_spec = whole(2 * share + 16, width)

    def call(
        kernel, name, units, scalars, grid, ins, in_specs, outs, out_specs, scratch, tiles=True
    ):
        return pl.pallas_call(
            kernel,
            grid_spec=pltpu.PrefetchScalarGridSpec(
                num_scalar_prefetch=len(scalars),
                grid=grid,
                in_specs=([any_spec] if tiles else []) + in_specs,
                out_specs=out_specs,
                scratch_shapes=scratch,
            ),
            out_shape=outs,
            compiler_params=params,
            cost_estimate=pl.CostEstimate(
                flops=units * 2 * frames * padded * width * width,
                bytes_accessed=16 * width * width,
                transcendentals=0,
            ),
            name=name,
        )(*scalars, *([gathered] if tiles else []), *ins)

    def tile_bufs(*shapes):
        return [pltpu.VMEM((rows * width, cols * width), bf16) for rows, cols in shapes]

    x1, hid0, hat0, rstd0, q_t, k_t, v_t, o_t = call(
        partial(time_forward, groups),
        "time_forward",
        14,
        [slot_index, member_s],
        time_grid,
        [pix, pos, trow, time_rows, time_q, time_k],
        [group_spec, patch_spec, whole(frames, width), rows_spec, time_extra, time_extra],
        [half32, cube16, cube16, thin32] + [cube16] * 4,
        [near_spec] + [group_spec] * 2 + [group_thin] + [group_spec] * 4,
        tile_bufs((1, 1), (1, 3), (1, 1))
        + [pltpu.VMEM((frames * group_rows, width), f32), pltpu.SemaphoreType.DMA((3,))],
    )
    (hid1, hat1, rstd1, q_s, k_s, v_s, o_s, hid2, hat2, rstd2, hat3, rstd3, gp, act, pool) = call(
        lambda s, fw, m, *refs: space_forward(s, fw, m, patches, *refs),
        "space_forward",
        15,
        [slot_index, frame_weight, member_s],
        space_grid,
        [x1, space_rows, low_rows, space_q, space_k],
        [frame_spec, rows_spec, rows_spec, space_extra, space_extra],
        [half16, half16, half_thin]
        + [half16] * 4
        + [half16, half16, half_thin, half16, half_thin]
        + [
            jax.ShapeDtypeStruct((mlp_count, half_frames, padded, width), bf16),
            jax.ShapeDtypeStruct((2, half_frames, padded, width), bf16),
            row32,
        ],
        [frame_spec, frame_spec, frame_thin]
        + [frame_spec] * 4
        + [frame_spec, frame_spec, frame_thin, frame_spec, frame_thin]
        + [gp_spec, act_spec, rows_spec],
        tile_bufs((1, 3), (1, 1), (1, mlp_count), (mlp_count, 1))
        + [pltpu.VMEM((frame_rows, mlp_count * width), bf16), pltpu.SemaphoreType.DMA((4,))],
    )

    pool_other = swap(pool, "mlp", 1)
    middle = width // 2
    squares16 = jax.ShapeDtypeStruct((2, 2, width, middle), bf16)
    pair16 = jax.ShapeDtypeStruct((2, half_frames, padded, width), bf16)
    dx2, g3, du, rows_low, small = call(
        lambda s, fw, m, *refs: mlp_backward(s, fw, m, patches, *refs),
        "mlp_backward",
        9,
        [slot_index, frame_weight, member_s],
        space_grid,
        [
            pool, pool_other, head_b, valid_p, targets_p, label_total[None],
            hat2, rstd2, hat3, rstd3, gp, low_rows,
        ],
        [
            rows_spec, rows_spec, whole(width, class_pad), whole(1, class_pad), whole(1, class_pad),
            pl.BlockSpec(memory_space=pltpu.SMEM),
            frame_spec, frame_thin, frame_spec, frame_thin, gp_spec, rows_spec,
        ],
        [half32, half16, pair16, row32, row32],
        [frame_spec, frame_spec, act_spec, rows_spec, rows_spec],
        tile_bufs((1, mlp_count), (mlp_count, 1))
        + [
            pltpu.VMEM((frame_rows, mlp_count * width), bf16),
            pltpu.VMEM((8, width), f32),
            pltpu.VMEM((5, 8, width), f32),
            pltpu.SemaphoreType.DMA((2,)),
        ],
    )

    grads_spec = pl.BlockSpec((FRAMES_AT_ONCE, padded, 4 * width), lambda f, *_: (f, 0, 0))
    main = half_blocks * group_rows
    half_spec = pl.BlockSpec((FRAMES_AT_ONCE, half_rows, width), lambda f, *_: (f, 0, 0))
    swapped16 = jax.ShapeDtypeStruct((half_frames, half_rows, width), bf16)
    near, leaving, grads_space, norm_space = call(
        partial(space_backward, main),
        "space_backward",
        11,
        [slot_index, member_s],
        space_grid,
        [dx2, hat1, rstd1, q_s, k_s, v_s, space_rows, space_q, space_k],
        [frame_spec] * 2 + [frame_thin] + [frame_spec] * 3 + [rows_spec, space_extra, space_extra],
        [swapped16] * 2
        + [jax.ShapeDtypeStruct((half_frames, padded, 4 * width), bf16), row32],
        [half_spec] * 2 + [grads_spec, rows_spec],
        tile_bufs((1, 3), (1, 1))
        + [
            pltpu.VMEM((2, 8, width), f32),
            pltpu.VMEM((frame_rows, width), bf16),
            pltpu.VMEM((FRAMES_AT_ONCE, padded, width), bf16),
            pltpu.SemaphoreType.DMA((2,)),
        ],
    )

    leaving, late_hid1, late_hid2 = lax.optimization_barrier((leaving, hid1, hid2))
    far = swap(leaving, "mlp", 1)
    clip_spec = whole(half_frames, padded, width)
    one_spec = pl.BlockSpec((1, half_frames, padded, width), lambda i, c: (i, 0, 0, 0))
    square_spec = pl.BlockSpec((1, 2, width, middle), lambda i, c: (i, 0, 0, 0))
    keep_mlp, send_mlp = call(
        mlp_weights,
        "mlp_weights",
        2,
        [core_s],
        (2,),
        [late_hid2, g3, du, act],
        [clip_spec, clip_spec, one_spec, one_spec],
        [squares16] * 2,
        [square_spec] * 2,
        [pltpu.VMEM((2, width, width), f32)],
        tiles=False,
    )
    met_mlp = swap(send_mlp, "dp", 1)
    keep_space, send_space, sums_space = call(
        space_weights,
        "space_weights",
        2,
        [core_s],
        (4,),
        [picked, late_hid1, o_s, grads_space],
        [
            pick_spec, clip_spec, clip_spec,
            pl.BlockSpec((half_frames, padded, width), lambda i, c: (0, 0, i)),
        ],
        [jax.ShapeDtypeStruct((2, 4, share, middle), bf16)] * 2
        + [jax.ShapeDtypeStruct((4, 8, width), f32)],
        [pl.BlockSpec((2, 1, share, middle), lambda i, c: (0, i, 0, 0))] * 2
        + [pl.BlockSpec((1, 8, width), lambda i, c: (i, 0, 0))],
        [pltpu.VMEM((2 * share + 16, half_frames * padded), bf16),
         pltpu.VMEM((2 * share + 16, width), f32)],
        tiles=False,
    )
    far, keep_space, send_space = lax.optimization_barrier((far, keep_space, send_space))
    met_space = swap(send_space, "dp", 1)
    chip_mlp = added(keep_mlp[1], met_mlp[1]).astype(bf16)
    chip_space = added(keep_space[1], met_space[1]).astype(bf16)
    far, chip_mlp, chip_space = lax.optimization_barrier((far, chip_mlp, chip_space))
    far_mlp = swap(chip_mlp, "mlp", 1)
    far_space = swap(chip_space, "mlp", 1)
    keep_time, send_time, rows_time, grad_pos, grad_frames = call(
        partial(time_backward, rest),
        "time_backward",
        18,
        [slot_index, member_s, core_s],
        back_grid,
        [near, far, hid0, hat0, rstd0, q_t, k_t, v_t, o_t, pix, time_rows, picked, time_q, time_k],
        [near_spec] * 2
        + [back_spec] * 2
        + [back_thin]
        + [back_spec] * 5
        + [rows_spec, pick_spec, time_extra, time_extra],
        [jax.ShapeDtypeStruct((2, 5, share, middle), bf16)] * 2
        + [
            row32,
            jax.ShapeDtypeStruct((half_rows, width), f32),
            jax.ShapeDtypeStruct((frames, width), f32),
        ],
        [whole(2, 5, share, middle)] * 2 + [rows_spec, patch_spec, whole(frames, width)],
        tile_bufs((1, 3), (1, 1))
        + [
            pltpu.VMEM((2 * share + 16, 3 * width), f32),
            pltpu.VMEM((2 * share + 16, width), f32),
        ]
        + [
            pltpu.VMEM((2 * share + 16, width), f32),
            pltpu.VMEM((2, 8, width), f32),
            pltpu.VMEM((frames, group_rows, 3 * width), bf16),
            pltpu.VMEM((frames, group_rows, width), bf16),
            pltpu.SemaphoreType.DMA((2,)),
        ],
    )

    send_time, far_mlp, far_space = lax.optimization_barrier((send_time, far_mlp, far_space))
    met_time = swap(send_time, "dp", 1)
    chip_time = added(keep_time[1], met_time[1]).astype(bf16)
    chip_time, grad_frames, grad_pos = lax.optimization_barrier(
        (chip_time, grad_frames, grad_pos)
    )
    far_time = swap(chip_time, "mlp", 1)
    grad_time = jnp.einsum("ft,fd->td", time_hot, grad_frames, precision=highest)
    main = half_blocks * group_rows
    all_pos = jnp.concatenate(
        [jnp.where(half == i, grad_pos[:main], 0.0) for i in range(2)] + [grad_pos[main:]]
    )
    table_rows = tables.shape[0]
    table_part = jnp.concatenate(
        [
            jnp.sum(grad_frames, axis=0, keepdims=True),
            rows_time[:5],
            norm_space[:2],
            sums_space[0, :1],
            sums_space[2, :1],
            sums_space[3, :1],
            rows_low[:5],
            all_pos[:patches],
            grad_time,
        ]
    )
    rows_each = -(-table_rows // (dp_count * mlp_count))
    table_part = jnp.pad(
        table_part, ((0, rows_each * dp_count * mlp_count - table_rows), (0, 0))
    ).reshape(dp_count, mlp_count, rows_each, width)

    def table_of(which):
        rows_now = lax.dynamic_index_in_dim(table_part, which, 1, False).astype(bf16)
        return jnp.pad(rows_now, ((0, 0), (0, 16 - rows_each), (0, 0)))

    table_pair = jnp.stack([table_of(member), table_of(member ^ 1)])
    columns = jnp.stack([table_pair[..., :middle], table_pair[..., middle:]])
    keep_table = lax.dynamic_index_in_dim(columns, place % 2, 0, False)
    met_table = swap(lax.dynamic_index_in_dim(columns, 1 - place % 2, 0, False), "dp", 1)
    far_table = swap(added(keep_table[1], met_table[1]).astype(bf16), "mlp", 1)

    def blocks_of(*parts):
        return [part.reshape(part.shape[0], -1, BR, middle) for part in parts]

    sources = (
        blocks_of(keep_time, keep_space, keep_mlp)
        + [keep_table]
        + blocks_of(met_time, met_space, met_mlp)
        + [met_table]
        + [part.reshape(-1, BR, middle) for part in (far_time, far_space, far_mlp)]
        + [far_table]
    )
    bits = dp_count.bit_length() - 1
    chunk = jax.ShapeDtypeStruct((dp_count // 4, slots * BR + 16, middle), bf16)
    packed = pl.pallas_call(
        partial(pack, bits),
        grid_spec=pltpu.PrefetchScalarGridSpec(
            num_scalar_prefetch=2,
            grid=(1,),
            in_specs=[
                pl.BlockSpec((1,) + part.shape[1:], lambda i, *_: (0, 0, 0, 0))
                if part.ndim == 4
                else whole(*part.shape)
                for part in sources
            ],
            out_specs=[any_spec] * 4,
            scratch_shapes=[pltpu.VMEM(part.shape, bf16) for part in sources[8:]]
            + [pltpu.SemaphoreType.DMA((4,))],
        ),
        out_shape=[chunk] * 4,
        compiler_params=params,
        name="pack",
    )(dests, place[None], *sources)
    sum_a, sum_b = (value.reshape(value.shape[-2:]) for value in halve(*packed, "dp"))
    even = place % 2 == 0
    mine = jnp.where(even, sum_a, sum_b)
    met = swap(jnp.where(even, sum_b, sum_a), "dp", 1)
    summed = jnp.concatenate([jnp.where(even, mine, met), jnp.where(even, met, mine)], axis=1)
    my_slots = (place * mlp_count + member) * slots + jnp.arange(slots)
    filled = jnp.any(slot_index[:, None] == my_slots[None, :], axis=0)
    filled = jnp.repeat(filled, BR)[:, None]
    own_grad = jnp.where(filled, summed[: slots * BR], 0.0)
    squares_own = jnp.sum(own_grad * own_grad)
    block = jnp.concatenate(
        [
            jnp.pad(summed[slots * BR : slots * BR + rows_each], ((0, 7 - rows_each), (0, 0))),
            jnp.broadcast_to(squares_own, (1, width)),
            small,
        ]
    )
    blocks = jnp.concatenate(
        [spread_four(block[:8], "mlp"), block[None, 8:]], axis=0
    )
    blocks = lax.all_gather(blocks, "dp", axis=0)
    heads, blocks = blocks[:, mlp_count], blocks[:, :mlp_count]
    grad_head = jnp.einsum("cd,ck->dk", heads[:, 0], heads[:, 1, :classes], precision=highest)
    loss_sum = jnp.sum(heads[:, 2, 0])
    grad_tables = blocks[:, :, :rows_each].reshape(-1, width)[:table_rows]
    grad_norm = jnp.sqrt(
        jnp.sum(blocks[:, :, 7, 0])
        + jnp.sum(grad_tables * grad_tables)
        + jnp.sum(grad_head * grad_head)
    )
    factor = jnp.minimum(1.0, clip_max / (grad_norm + 1e-06))
    new_slots = adamw(
        slot_weight, own_grad * factor, slot_moment1, slot_moment2, decay_rate, learn_rate
    )
    new_tabs = adamw(tables, grad_tables * factor, table_moment1, table_moment2, 0.0, table_rate)
    new_heads = adamw(
        head_weight, grad_head * factor, head_moment1, head_moment2, decay_rate, learn_rate
    )
    return (
        loss_sum,
        label_total,
        grad_norm,
        new_slots[0],
        new_slots[1],
        new_slots[2],
        new_tabs[0],
        new_tabs[1],
        new_tabs[2],
        new_heads[0],
        new_heads[1],
        new_heads[2],
    )


def solution(mesh):
    return jax.shard_map(
        local,
        mesh=mesh,
        in_specs=(
            P("dp", None, None, None),
            P("dp"),
            P("dp", None),
            P("dp", None),
            P("dp", None),
            P("dp", None),
            P(),
            P(("dp", "mlp"), None),
            P(("dp", "mlp"), None),
            P(("dp", "mlp"), None),
            P(),
            P(),
            P(),
            P(),
            P(),
            P(),
        ),
        out_specs=(
            P(),
            P(),
            P(),
            P(("dp", "mlp"), None),
            P(("dp", "mlp"), None),
            P(("dp", "mlp"), None),
            P(),
            P(),
            P(),
            P(),
            P(),
            P(),
        ),
        check_vma=False,
    )
```

```python
from functools import partial

import jax
import jax.numpy as jnp
from jax import lax
from jax.experimental import pallas as pl
from jax.experimental.pallas import tpu as pltpu
from jax.sharding import PartitionSpec as P

HEADS = 12
HEAD_DIM = 64
TROWS = 8
BR = 48
STEP = 10
GROUP = 16
PAIR = 2 * HEAD_DIM
GROUPS_AT_ONCE = 2
FRAMES_AT_ONCE = 2
VMEM_BYTES = 58 * 2**20

ln_eps = 1e-06
beta_one = 0.9
beta_two = 0.999
learn_rate = 0.05
table_rate = 0.4
decay_rate = 0.05
adam_eps = 1e-08
clip_max = 0.001
highest = lax.Precision.HIGHEST
f32 = jnp.float32
bf16 = jnp.bfloat16
gelu_a = 0.7978845608028654
gelu_b = 0.044715
masked = -1e30


def mm(left, right):
    return jnp.dot(left, right, preferred_element_type=f32)


def mm_nt(left, right):
    return lax.dot_general(left, right, (((1,), (1,)), ((), ())), preferred_element_type=f32)


def mm_tn(left, right):
    return lax.dot_general(left, right, (((0,), (0,)), ((), ())), preferred_element_type=f32)


def normed(values):
    centred = values - jnp.mean(values, axis=-1, keepdims=True)
    rstd = lax.rsqrt(jnp.mean(centred * centred, axis=-1, keepdims=True) + ln_eps)
    return centred * rstd, rstd


def norm_back(grad, xhat, rstd, gain):
    scaled = grad * gain
    return rstd * (
        scaled
        - jnp.mean(scaled, axis=-1, keepdims=True)
        - xhat * jnp.mean(scaled * xhat, axis=-1, keepdims=True)
    )


def fold(values):
    return jnp.sum(values.reshape(-1, 8, values.shape[-1]), axis=0)


def low_lanes():
    lane = lax.broadcasted_iota(jnp.int32, (1, PAIR), 1)
    low = jnp.where(lane < HEAD_DIM, 1.0, 0.0)
    return low.astype(bf16), (1.0 - low).astype(bf16)


def pick_half(stacked):
    rows = stacked.shape[0] // 2
    lane = lax.broadcasted_iota(jnp.int32, (rows, PAIR), 1)
    return jnp.where(lane < HEAD_DIM, stacked[:rows], stacked[rows:])


def fetch(slots_ref, source, target, sem, first, across):
    width = source.shape[2]
    per_tile = width // BR

    count = target.shape[0] * target.shape[1] // (width * width)
    for tile in range(count):
        for i in range(per_tile):
            if across:
                into = target.at[pl.ds(i * BR, BR), pl.ds(tile * width, width)]
            else:
                into = target.at[pl.ds(tile * width + i * BR, BR)]
            block = first(tile) * per_tile + i
            pltpu.make_async_copy(source.at[slots_ref[block]], into, sem).start()


def arrive(target, sem):
    pltpu.make_async_copy(target, target, sem).wait()


def jobs_of(count):
    pairs = [slice(p * PAIR, (p + 1) * PAIR) for p in range(HEADS // 2)]
    return [(i, lanes) for i in range(count) for lanes in pairs]


def each_row(count, begin, finish):
    def one(i, carry):
        in_flight([(i, lanes) for unused, lanes in jobs_of(1)], begin, finish)
        return carry

    lax.fori_loop(0, count, one, 0)


def in_flight(jobs, begin, finish):
    waiting = None
    for job in jobs:
        started = begin(*job)
        if waiting is not None:
            finish(*waiting)
        waiting = job + started
    finish(*waiting)


def attend(count, load, store, extra_q, extra_k):
    low, high = low_lanes()

    def begin(i, lanes):
        queries, keys, values = load(i, lanes)
        both = jnp.concatenate([queries * low, queries * high], axis=0)
        scores = mm_nt(
            jnp.concatenate([both, extra_q[...]], axis=1),
            jnp.concatenate([keys, extra_k[: keys.shape[0]]], axis=1),
        )
        return values, scores

    def finish(i, lanes, values, scores):
        top = jnp.max(scores, axis=-1, keepdims=True)
        weights = jnp.exp(scores - top).astype(bf16)
        summed = mm(weights, jnp.concatenate([values, jnp.ones_like(values)], axis=1))
        merged = pick_half(summed[:, :PAIR]) / pick_half(summed[:, PAIR:])
        store(i, lanes, merged.astype(bf16))

    in_flight(jobs_of(count), begin, finish)


def attend_back(count, load, store, extra_q, extra_k, looped=False):
    low, high = low_lanes()

    def begin(i, lanes):
        queries, keys, values, grads = load(i, lanes)
        both_k = jnp.concatenate([keys * low, keys * high], axis=0)
        both_v = jnp.concatenate([values * low, values * high], axis=0)
        scores = mm_nt(
            jnp.concatenate([both_k, extra_k[...]], axis=1),
            jnp.concatenate([queries, extra_q[: queries.shape[0]]], axis=1),
        )
        return queries, both_k, grads, scores, mm_nt(both_v, grads)

    def finish(i, lanes, queries, both_k, grads, scores, back):
        rows = queries.shape[0]
        soft, inner = [], []
        for half in (slice(0, rows), slice(rows, 2 * rows)):
            part = scores[half]
            weights = jnp.exp(part - jnp.max(part, axis=0, keepdims=True))
            weights = weights * (1.0 / jnp.sum(weights, axis=0, keepdims=True))
            delta = back[half] - jnp.sum(weights * back[half], axis=0, keepdims=True)
            soft.append(weights.astype(bf16))
            inner.append((weights * delta).astype(bf16))
        soft = jnp.concatenate(soft, axis=0)
        inner = jnp.concatenate(inner, axis=0)
        store(
            i,
            lanes,
            (mm_tn(inner, both_k) * HEAD_DIM ** (-0.5)).astype(bf16),
            pick_half(mm(inner, queries)).astype(bf16),
            pick_half(mm(soft, grads)).astype(bf16),
        )

    if looped:
        each_row(count, begin, finish)
    else:
        in_flight(jobs_of(count), begin, finish)


def project(hidden, rows, tiles):
    width = hidden.shape[1]
    joint = mm(hidden, tiles[...])
    queries = (joint[:, :width] + rows[2:3]).astype(bf16) * jnp.asarray(HEAD_DIM ** (-0.5), bf16)
    keys = joint[:, width : 2 * width].astype(bf16)
    values = (joint[:, 2 * width :] + rows[3:4]).astype(bf16)
    return queries, keys, values


def keep_norm(stream, rows, at, hid_ref, hat_ref, rstd_ref, here, cut):
    xhat, rstd = normed(stream)
    hat_ref[here] = xhat.astype(bf16).reshape(cut)
    rstd_ref[here] = jnp.broadcast_to(rstd, (rstd.shape[0], 128)).reshape(cut[:-1] + (128,))
    hidden = (xhat * rows[at : at + 1] + rows[at + 1 : at + 2]).astype(bf16)
    if hid_ref is not None:
        hid_ref[here] = hidden.reshape(cut)
    return xhat, hidden


def by_groups(block, total, work):
    step = pl.program_id(0)
    full, rest = total // block, total % block
    if rest == 0:
        work(block)
    else:
        pl.when(step < full)(lambda: work(block))
        pl.when(step == full)(lambda: work(rest))


def time_forward(
    total, slots, member, gathered, pixels, pos, trow, rows, extra_q, extra_k,
    x1_ref, hid_ref, hat_ref, rstd_ref, q_ref, k_ref, v_ref, o_ref,
    embed, joint, out, base, sems,
):
    frames, span, width = hid_ref.shape

    @pl.when(pl.program_id(0) == 0)
    def _():
        fetch(slots, gathered, embed, sems.at[0], lambda t: t, False)
        fetch(slots, gathered, joint, sems.at[1], lambda t: t + 1, True)
        fetch(slots, gathered, out, sems.at[2], lambda t: t + 4, False)
        arrive(embed, sems.at[0])

    def first(target, sem):
        pl.when(pl.program_id(0) == 0)(lambda: arrive(target, sem))

    def work(count):
        cut = (frames, count * GROUP, width)
        flat = (frames * count * GROUP, width)
        here = slice(0, count * GROUP)
        every = (slice(None), here)
        offset = (pos[here][None] + trow[...][:, None]).reshape(flat)
        stream = mm(pixels[:, here].reshape(flat), embed[...]) + offset
        base[: flat[0]] = stream
        rows_now = rows[...]
        unused, hidden = keep_norm(stream, rows_now, 0, hid_ref, hat_ref, rstd_ref, every, cut)
        first(joint, sems.at[1])
        queries, keys, values = project(hidden, rows_now, joint)
        q_ref[:, here] = queries.reshape(cut)
        k_ref[:, here] = keys.reshape(cut)
        v_ref[:, here] = values.reshape(cut)

        def load(g, lanes):
            part = slice(g * GROUP, (g + 1) * GROUP)
            return tuple(
                ref[:, part, lanes].reshape(frames * GROUP, PAIR) for ref in (q_ref, k_ref, v_ref)
            )

        def store(g, lanes, merged):
            part = slice(g * GROUP, (g + 1) * GROUP)
            o_ref[:, part, lanes] = merged.reshape(frames, GROUP, PAIR)

        attend(count, load, store, extra_q, extra_k)
        first(out, sems.at[2])
        near, some = frames // 2, flat[0] // 2
        late = member[0] % 2
        merged = o_ref[pl.ds(late * near, near), here].reshape(some, width)
        stream = base[pl.ds(pl.multiple_of(late * some, 16), some)] + mm(merged, out[...])
        x1_ref[:, here] = (stream + rows_now[4:5]).reshape(near, count * GROUP, width)

    by_groups(span // GROUP, total, work)


def space_forward(
    slots, frame_weight, member, patches, gathered, x1, rows, low_rows, extra_q, extra_k,
    hid1_ref, hat1_ref, rstd1_ref, q_ref, k_ref, v_ref, o_ref,
    hid2_ref, hat2_ref, rstd2_ref, hat3_ref, rstd3_ref, gp_ref, act_ref, pool_ref,
    joint, out, ups, downs, acts, sems,
):
    step = pl.program_id(0)
    members = gp_ref.shape[0]
    cut = x1.shape
    span, count, width = cut
    flat = (span * count, width)
    every = (slice(None),)

    @pl.when(step == 0)
    def _():
        fetch(slots, gathered, joint, sems.at[0], lambda t: t + 5, True)
        fetch(slots, gathered, out, sems.at[1], lambda t: t + 8, False)
        fetch(slots, gathered, ups, sems.at[2], lambda t: 2 * t + 9, True)
        fetch(slots, gathered, downs, sems.at[3], lambda t: 2 * t + 10, False)
        pool_ref[...] = jnp.zeros_like(pool_ref)
        arrive(joint, sems.at[0])

    rows_now = rows[...]
    unused, hidden = keep_norm(
        x1[...].reshape(flat), rows_now, 0, hid1_ref, hat1_ref, rstd1_ref, every, cut
    )
    queries, keys, values = project(hidden, rows_now, joint)
    q_ref[...] = queries.reshape(cut)
    k_ref[...] = keys.reshape(cut)
    v_ref[...] = values.reshape(cut)

    def load(f, lanes):
        return q_ref[f, :, lanes], k_ref[f, :, lanes], v_ref[f, :, lanes]

    def store(f, lanes, merged):
        o_ref[f, :, lanes] = merged

    attend(span, load, store, extra_q, extra_k)
    pl.when(step == 0)(lambda: arrive(out, sems.at[1]))
    merged = o_ref[...].reshape(flat)
    stream = x1[...].reshape(flat) + mm(merged, out[...]) + rows_now[4:5]
    low_now = low_rows[...]
    unused, hidden = keep_norm(stream, low_now, 0, hid2_ref, hat2_ref, rstd2_ref, every, cut)

    @pl.when(step == 0)
    def _():
        arrive(ups, sems.at[2])
        arrive(downs, sems.at[3])

    def begin(j, lanes):
        return (mm(hidden, ups[:, lanes]),)

    lowered = []

    def finish(j, lanes, upper):
        cubic = gelu_a * gelu_b * (upper * upper)
        gate = 0.5 + 0.5 * jnp.tanh(upper * (gelu_a + cubic))
        active = upper * gate
        slope = gate + active * (1.0 - gate) * (2.0 * gelu_a + 6.0 * cubic)
        gp_ref[j] = slope.astype(bf16).reshape(cut)
        acts[:, lanes] = active.astype(bf16)
        lowered.append(mm(acts[:, lanes], downs[lanes]))

    in_flight([(j, slice(j * width, (j + 1) * width)) for j in range(members)], begin, finish)
    for part in lowered:
        stream = stream + part
    for i in range(2):
        own = pl.ds(pl.multiple_of((member[0] ^ i) * width, 128), width)
        act_ref[i] = acts[:, own].reshape(cut)
    stream = stream + low_now[2:3]
    xhat, rstd = normed(stream)
    hat3_ref[...] = xhat.astype(bf16).reshape(cut)
    rstd3_ref[...] = jnp.broadcast_to(rstd, (flat[0], 128)).reshape(span, count, 128)
    final = xhat * low_now[3:4] + low_now[4:5]
    row = lax.broadcasted_iota(jnp.int32, (count, 1), 0)
    for f in range(span):
        part = jnp.where(row < patches, final[f * count : (f + 1) * count], 0.0)
        pool_ref[...] += fold(part) * frame_weight[step * span + f]


def mlp_backward(
    slots, frame_weight, member, patches, gathered, pool, pool_other, head, valid, targets, total,
    hat2, rstd2, hat3, rstd3, gp, low_rows,
    dx2_ref, g3_ref, du_ref, rows_ref, small_ref,
    ups, downs, dus, spread, row_sums, sems,
):
    step = pl.program_id(0)
    members = gp.shape[0]
    cut = hat2.shape
    span, count, width = cut
    flat = (span * count, width)

    @pl.when(step == 0)
    def _():
        fetch(slots, gathered, downs, sems.at[1], lambda t: 2 * t + 10, False)
        fetch(slots, gathered, ups, sems.at[0], lambda t: 2 * t + 9, True)
        pooled = jnp.sum(pool[...] + pool_other[...], axis=0, keepdims=True).astype(bf16)
        pooled8 = jnp.broadcast_to(pooled, (8, width))
        logits = mm(pooled8, head[...])
        valid_f = valid[...]
        target = targets[...]
        soft = jnp.maximum(logits, 0.0) + jnp.log(1.0 + jnp.exp(-jnp.abs(logits)))
        loss = jnp.sum(valid_f * (soft - target * logits), axis=1, keepdims=True)
        sig = 1.0 / (1.0 + jnp.exp(-logits))
        grad = (valid_f * (sig - target) / jnp.maximum(total[0], 1.0)).astype(bf16)
        spread[...] = mm_nt(grad, head[...])
        small_ref[...] = jnp.zeros_like(small_ref)
        small_ref[0:1, :] = pooled.astype(f32)
        small_ref[1:2, 0 : grad.shape[1]] = grad[0:1].astype(f32)
        small_ref[2:3, 0:128] = jnp.broadcast_to(loss[0:1], (1, 128))
        row_sums[...] = jnp.zeros_like(row_sums)
        arrive(downs, sems.at[1])

    low_now = low_rows[...]
    row = lax.broadcasted_iota(jnp.int32, (count, 1), 0)
    weight = jnp.concatenate(
        [jnp.where(row < patches, frame_weight[step * span + f], 0.0) for f in range(span)]
    )
    grad_final = spread[0:1] * weight
    xhat = hat3[...].reshape(flat).astype(f32)
    rstd = rstd3[...].reshape(flat[0], 128)[:, 0:1]
    row_sums[3] += fold(grad_final * xhat)
    row_sums[4] += fold(grad_final)
    grad_top = norm_back(grad_final, xhat, rstd, low_now[3:4])
    row_sums[2] += fold(grad_top)
    grad_b = grad_top.astype(bf16)
    g3_ref[...] = grad_b.reshape(cut)

    for j in range(members):
        lanes = slice(j * width, (j + 1) * width)
        du = mm_nt(grad_b, downs[lanes]) * gp[j].reshape(flat).astype(f32)
        dus[:, lanes] = du.astype(bf16)

    @pl.when(step == 0)
    def _():
        arrive(ups, sems.at[0])

    grad_hidden = mm_nt(dus[...], ups[...])
    for i in range(2):
        own = pl.ds(pl.multiple_of((member[0] ^ i) * width, 128), width)
        du_ref[i] = dus[:, own].reshape(cut)
    xhat = hat2[...].reshape(flat).astype(f32)
    rstd = rstd2[...].reshape(flat[0], 128)[:, 0:1]
    row_sums[0] += fold(grad_hidden * xhat)
    row_sums[1] += fold(grad_hidden)
    dx2_ref[...] = (grad_top + norm_back(grad_hidden, xhat, rstd, low_now[0:1])).reshape(cut)

    @pl.when(step == pl.num_programs(0) - 1)
    def _():
        rows_ref[...] = jnp.zeros_like(rows_ref)
        for i in range(5):
            rows_ref[i : i + 1] = jnp.sum(row_sums[i], axis=0, keepdims=True)


def mlp_weights(core, hid2, g3, du, act, keep_ref, send_ref, sums):
    rows, width = hid2.shape[0] * hid2.shape[1], hid2.shape[2]
    sums[0] = mm_tn(hid2[...].reshape(rows, width), du[0].reshape(rows, width))
    sums[1] = mm_tn(act[0].reshape(rows, width), g3[...].reshape(rows, width))
    for ref, half in zip((keep_ref, send_ref), column_halves(core[0], width)):
        for n in range(2):
            ref[0, n] = sums[n, :, half].astype(bf16)


def space_weights(core, picked, hid1, o, grads, keep_ref, send_ref, rows_ref, left, sums):
    step = pl.program_id(0)
    rows, width = hid1.shape[0] * hid1.shape[1], hid1.shape[2]
    share = keep_ref.shape[2]

    def select(source):
        chosen = mm_nt(picked[...], source[...].reshape(rows, width)).astype(bf16)
        left[...] = chosen + ones_row(picked)

    pl.when(step == 0)(lambda: select(hid1))
    pl.when(step == pl.num_programs(0) - 1)(lambda: select(o))
    sums[...] = mm(left[...], grads[...].reshape(rows, width))
    for ref, half in zip((keep_ref, send_ref), column_halves(core[0], width)):
        for n in range(2):
            ref[n, 0] = sums[n * share : (n + 1) * share, half].astype(bf16)
    rows_ref[0] = sums[2 * share : 2 * share + 8]


def close_attention(
    grad_stream, grad_b, hidden, xhat, rstd, grads, merged, rows_now, picked, ones, joint,
    joint_sum, out_sum, row_sums,
):
    grad_hidden = mm_nt(grads, joint[...])
    hidden_t = mm_nt(picked, hidden).astype(bf16) + ones
    merged_t = mm_nt(picked, merged).astype(bf16) + ones
    joint_sum[...] += mm(hidden_t, grads)
    out_sum[...] += mm(merged_t, grad_b)
    xhat = xhat.astype(f32)
    row_sums[0] += fold(grad_hidden * xhat)
    row_sums[1] += fold(grad_hidden)
    return grad_stream + norm_back(grad_hidden, xhat, rstd[:, 0:1], rows_now[0:1])


def ones_row(picked):
    row = lax.broadcasted_iota(jnp.int32, (picked.shape[0], 1), 0)
    return jnp.where(row == picked.shape[0] - 16, 1.0, 0.0).astype(bf16)


def column_halves(core, width):
    middle = width // 2
    keep = pl.ds(pl.multiple_of(core * middle, 128), middle)
    send = pl.ds(pl.multiple_of((1 - core) * middle, 128), middle)
    return keep, send


def clear(*refs):
    for ref in refs:
        ref[...] = jnp.zeros_like(ref)


def finish_attention(core, tile_refs, at, rows_ref, joint_sum, out_sum, row_sums):
    share = tile_refs[0].shape[2]
    width = out_sum.shape[1]
    rows_ref[...] = jnp.zeros_like(rows_ref)
    for tile_ref, half in zip(tile_refs, column_halves(core, width)):
        for n in range(2):
            here = slice(n * share, (n + 1) * share)
            for i in range(3):
                start = pl.multiple_of(i * width + half.start, 128)
                columns = pl.ds(start, half.size)
                tile_ref[n, at + i] = joint_sum[here, columns].astype(bf16)
            tile_ref[n, at + 3] = out_sum[here, half].astype(bf16)
    last = slice(2 * share, 2 * share + 1)
    for i in range(2):
        rows_ref[i : i + 1] = jnp.sum(row_sums[i], axis=0, keepdims=True)
    rows_ref[2:3] = joint_sum[last, :width]
    rows_ref[3:4] = joint_sum[last, 2 * width :]
    rows_ref[4:5] = out_sum[last]


def space_backward(
    main, slots, member, gathered, dx2, hat1, rstd1, q, k, v, rows, extra_q, extra_k,
    near_ref, far_ref, grads_ref, rows_ref, joint, out, row_sums, outer, g1, sems,
):
    step = pl.program_id(0)
    cut = hat1.shape
    span, count, width = cut
    flat = (span * count, width)

    @pl.when(step == 0)
    def _():
        fetch(slots, gathered, out, sems.at[1], lambda t: t + 8, False)
        fetch(slots, gathered, joint, sems.at[0], lambda t: t + 5, True)
        clear(row_sums)
        arrive(out, sems.at[1])

    grad_b = dx2[...].reshape(flat).astype(bf16)
    grads_ref[:, :, 3 * width :] = grad_b.reshape(cut)
    outer[...] = mm_nt(grad_b, out[...]).astype(bf16)

    def load(f, lanes):
        here = pl.ds(pl.multiple_of(f * count, 16), count)
        return q[f, :, lanes], k[f, :, lanes], v[f, :, lanes], outer[here, lanes]

    def store(f, lanes, *parts):
        for i, part in enumerate(parts):
            grads_ref[f, :, i * width + lanes.start : i * width + lanes.stop] = part

    attend_back(span, load, store, extra_q, extra_k, looped=True)
    pl.when(step == 0)(lambda: arrive(joint, sems.at[0]))
    grads = grads_ref[:, :, : 3 * width].reshape(flat[0], 3 * width)
    grad_hidden = mm_nt(grads, joint[...])
    xhat = hat1[...].reshape(flat).astype(f32)
    rstd = rstd1[...].reshape(flat[0], 128)[:, 0:1]
    row_sums[0] += fold(grad_hidden * xhat)
    row_sums[1] += fold(grad_hidden)
    grad_stream = dx2[...].reshape(flat) + norm_back(grad_hidden, xhat, rstd, rows[0:1])
    g1[...] = grad_stream.astype(bf16).reshape(cut)
    late = member[0] % 2
    for ref, which in ((near_ref, late), (far_ref, 1 - late)):
        ref[:, :main] = g1[:, pl.ds(pl.multiple_of(which * main, 16), main)]
        if ref.shape[1] > main:
            ref[:, main:] = g1[:, 2 * main : main + ref.shape[1]]

    @pl.when(step == pl.num_programs(0) - 1)
    def _():
        rows_ref[...] = jnp.zeros_like(rows_ref)
        for i in range(2):
            rows_ref[i : i + 1] = jnp.sum(row_sums[i], axis=0, keepdims=True)


def time_backward(
    rest, slots, member, core, gathered, near, far, hid0, hat0, rstd0, q, k, v, o, pixels, rows, picked,
    extra_q, extra_k,
    keep_ref, send_ref, rows_ref, pos_ref, frame_ref,
    joint, out, joint_sum, out_sum, embed_sum, row_sums, grads, outer, sems,
):
    step = pl.program_id(0)
    frames, span, width = hid0.shape

    @pl.when(step == 0)
    def _():
        fetch(slots, gathered, out, sems.at[1], lambda t: t + 4, False)
        fetch(slots, gathered, joint, sems.at[0], lambda t: t + 1, True)
        clear(joint_sum, out_sum, embed_sum, row_sums, frame_ref)
        arrive(out, sems.at[1])

    def work(groups):
        cut = (frames, groups * GROUP, width)
        flat = (frames * groups * GROUP, width)
        small = (frames, GROUP, PAIR)
        here = slice(0, groups * GROUP)
        first = member[0] % 2 == 0
        near_now, far_now = near[:, here], far[:, here]
        grad_b = jnp.concatenate(
            [jnp.where(first, near_now, far_now), jnp.where(first, far_now, near_now)]
        ).reshape(flat)
        outer[:, here] = mm_nt(grad_b, out[...]).astype(bf16).reshape(cut)

        def load(g, lanes):
            part = slice(g * GROUP, (g + 1) * GROUP)
            return tuple(
                ref[:, part, lanes].reshape(frames * GROUP, PAIR) for ref in (q, k, v, outer)
            )

        def store(g, lanes, *parts):
            part = slice(g * GROUP, (g + 1) * GROUP)
            for i, value in enumerate(parts):
                span_now = slice(i * width + lanes.start, i * width + lanes.stop)
                grads[:, part, span_now] = value.reshape(small)

        attend_back(groups, load, store, extra_q, extra_k)
        pl.when(step == 0)(lambda: arrive(joint, sems.at[0]))
        picked_now = picked[...]
        grad = close_attention(
            grad_b.astype(f32), grad_b, hid0[:, here].reshape(flat),
            hat0[:, here].reshape(flat), rstd0[:, here].reshape(flat[0], 128),
            grads[:, here].reshape(flat[0], 3 * width), o[:, here].reshape(flat), rows[...],
            picked_now, ones_row(picked_now), joint, joint_sum, out_sum, row_sums,
        )
        pix_t = mm_nt(picked_now, pixels[:, here].reshape(flat)).astype(bf16)
        embed_sum[...] += mm(pix_t, grad.astype(bf16))
        cube = grad.reshape(cut)
        pos_ref[here] = jnp.sum(cube, axis=0)
        frame_ref[...] += jnp.sum(cube, axis=1)

    last = step == pl.num_programs(0) - 1
    if rest == 0:
        work(span // GROUP)
    else:
        odd = member[0] % 2 == 1
        pl.when(jnp.logical_not(last))(lambda: work(span // GROUP))
        pl.when(jnp.logical_and(last, jnp.logical_not(odd)))(lambda: work(rest))

        @pl.when(jnp.logical_and(last, odd))
        def _():
            pos_ref[...] = jnp.zeros_like(pos_ref)

    @pl.when(last)
    def _():
        finish_attention(
            core[0], (keep_ref, send_ref), 1, rows_ref, joint_sum, out_sum, row_sums
        )
        share = keep_ref.shape[2]
        for ref, half in zip((keep_ref, send_ref), column_halves(core[0], width)):
            for n in range(2):
                ref[n, 0] = embed_sum[n * share : (n + 1) * share, half].astype(bf16)


def pack(bits, dests, place, *refs):
    count = (len(refs) - 5) // 4
    keeps, mets, fars = (refs[i * count : (i + 1) * count] for i in range(3))
    (stay_a, go_a, stay_b, go_b), sems = refs[3 * count : 3 * count + 4], refs[-1]
    sums = refs[-1 - count : -1]
    table_rows = sums[-1].shape[1]
    slots = (stay_a.shape[1] - table_rows) // BR
    top = bits - 1
    rest = 2 ** (bits - 2) - 1

    def route(source, chunk, rows, sem):
        differs = chunk ^ place[0]
        in_b = chunk % 2 == 1
        index_a, index_b = chunk >> 2, (chunk >> 1) & rest
        moves_a, moves_b = (differs >> 1) % 2 == 1, (differs >> top) % 2 == 1
        for flag, target, index in (
            (~in_b & ~moves_a, stay_a, index_a),
            (~in_b & moves_a, go_a, index_a),
            (in_b & ~moves_b, stay_b, index_b),
            (in_b & moves_b, go_b, index_b),
        ):

            @pl.when(flag)
            def _(target=target, index=index):
                pltpu.make_async_copy(source, target.at[index, rows], sem).start()

    first = 0
    for n, (keep, met, far, source) in enumerate(zip(keeps, mets, fars, sums)):
        table = n == count - 1

        def one(i, carry, keep=keep, met=met, far=far, source=source, first=first, n=n, table=table):
            total = keep[0, i].astype(f32) + met[0, i].astype(f32) + far[i].astype(f32)
            source[i] = total.astype(bf16)
            if table:
                route(source.at[i], i, pl.ds(slots * BR, table_rows), sems.at[n])
            else:
                dest = dests[first + i]
                row = pl.multiple_of((dest % slots) * BR, 16)
                route(source.at[i], dest // slots, pl.ds(row, BR), sems.at[n])
            return carry

        lax.fori_loop(0, source.shape[0], one, 0)
        first += source.shape[0]
    for n, source in enumerate(sums):
        pltpu.make_async_copy(source, source, sems.at[n]).wait()


def swap(value, axis, hop):
    size = lax.axis_size(axis)
    return lax.ppermute(value, axis, [(i, i ^ hop) for i in range(size)])


def added(*parts):
    total = parts[0].astype(f32)
    for part in parts[1:]:
        total = total + part.astype(f32)
    return total


def halve(stay_a, go_a, stay_b, go_b, axis):
    bits = lax.axis_size(axis).bit_length() - 1
    place = lax.axis_index(axis)
    orders = [list(range(1, bits)), list(range(bits - 1, 0, -1))]
    shape = (2,) * (bits - 2) + stay_a.shape[1:]
    going, staying = [go_a, go_b], [stay_a, stay_b]
    for stage in range(bits - 1):
        met = [swap(value, axis, 1 << order[stage]) for value, order in zip(going, orders)]
        values = [added(stay, come) for stay, come in zip(staying, met)]
        if stage == bits - 2:
            return values
        going, staying = [], []
        for value, order in zip(values, orders):
            alive = sorted(order[stage + 1 :], reverse=True)
            value = value.reshape(shape[stage:])
            at = alive.index(order[stage + 1])
            bit = (place >> order[stage + 1]) & 1
            going.append(lax.dynamic_index_in_dim(value, 1 - bit, at, False).astype(bf16))
            staying.append(lax.dynamic_index_in_dim(value, bit, at, False))


def spread_four(value, axis):
    size = lax.axis_size(axis)
    place = lax.axis_index(axis)
    value = value[None]
    hop = 1
    while hop < size:
        come = swap(value, axis, hop)
        low = (place & hop) == 0
        value = jnp.concatenate(
            [jnp.where(low, value, come), jnp.where(low, come, value)], axis=0
        )
        hop *= 2
    return value


def block_ranks(owners):
    total_blocks = owners.shape[0]
    same_owner = owners[:, None] == owners[None, :]
    earlier = jnp.arange(total_blocks)[None, :] < jnp.arange(total_blocks)[:, None]
    return jnp.sum((same_owner & earlier).astype(jnp.int32), axis=1)


def adamw(weight, gradient, moment_one, moment_two, weight_decay, rate):
    first_new = beta_one * moment_one + (1.0 - beta_one) * gradient
    second_new = beta_two * moment_two + (1.0 - beta_two) * gradient * gradient
    mean_hat = first_new / (1.0 - beta_one**STEP)
    var_hat = second_new / (1.0 - beta_two**STEP)
    updated = weight - rate * (mean_hat / (jnp.sqrt(var_hat) + adam_eps) + weight_decay * weight)
    return (updated, first_new, second_new)


def local(
    pixels,
    lengths,
    frame_mask,
    time_index,
    label_valid,
    targets,
    owners,
    slot_weight,
    slot_moment1,
    slot_moment2,
    tables,
    table_moment1,
    table_moment2,
    head_weight,
    head_moment1,
    head_moment2,
):
    dp_count = lax.axis_size("dp")
    mlp_count = lax.axis_size("mlp")
    member = lax.axis_index("mlp").astype(jnp.int32)
    width = slot_weight.shape[1]
    per_tile = width // BR
    slots = slot_weight.shape[0] // BR
    shared_blocks = 9 * per_tile
    frames, patches = pixels.shape[1], pixels.shape[2]
    padded = -(-patches // GROUP) * GROUP
    groups = padded // GROUP
    classes = head_weight.shape[1]
    class_pad = -(-classes // 128) * 128
    params = pltpu.CompilerParams(vmem_limit_bytes=VMEM_BYTES)
    any_spec = pl.BlockSpec(memory_space=pl.ANY)

    gathered = lax.all_gather(slot_weight.astype(bf16), ("dp", "mlp"), axis=0, tiled=True)
    gathered = gathered.reshape(-1, BR, width)
    slot_index = (owners * slots + block_ranks(owners)).astype(jnp.int32)

    pix = jnp.pad(pixels[0], ((0, 0), (0, padded - patches), (0, 0)))
    slot_pos = jnp.arange(frames)
    frame_live = slot_pos < lengths[0]
    key_ok = frame_live & (frame_mask[0] == 1)
    allowed = key_ok[None, :] | (slot_pos[:, None] == slot_pos[None, :])
    extra_lane = jnp.arange(HEAD_DIM)
    flat_id = jnp.arange(frames * GROUP)
    frame_id, patch_id = flat_id // GROUP, flat_id % GROUP
    lane_frame = jnp.clip(extra_lane - GROUP, 0, frames - 1)
    in_patch = (extra_lane < GROUP)[None, :]
    in_frame = ((extra_lane >= GROUP) & (extra_lane < GROUP + frames))[None, :]
    same_patch = patch_id[:, None] == extra_lane[None, :]
    same_frame = frame_id[:, None] == lane_frame[None, :]
    time_q = (in_patch & same_patch) | (in_frame & same_frame)
    time_k = (in_patch & ~same_patch) | (in_frame & ~allowed.T[frame_id][:, lane_frame])
    is_pad = (jnp.arange(padded) >= patches)[:, None]
    space_q = jnp.broadcast_to(extra_lane[None, :] == 0, (padded, HEAD_DIM))
    space_k = is_pad & (extra_lane[None, :] == 0)

    def widen(flags, value):
        block = jnp.where(flags, value, 0.0).astype(bf16)
        block = jnp.pad(block, ((0, 0), (0, PAIR - HEAD_DIM)))
        return jnp.concatenate([block, block])

    time_q, time_k = widen(time_q, 1.0), widen(time_k, masked)
    space_q, space_k = widen(space_q, 1.0), widen(space_k, masked)
    time_hot = (time_index[0][:, None] == jnp.arange(TROWS)[None, :]).astype(f32)
    trow = jnp.einsum("ft,td->fd", time_hot, tables[16 + patches :], precision=highest)
    pos = jnp.pad(tables[16 : 16 + patches] + tables[0], ((0, padded - patches), (0, 0)))
    frame_weight = jnp.where(
        frame_live, 1.0 / (lengths[0] * patches).astype(f32), 0.0
    ).astype(f32)
    valid_f = label_valid.astype(f32)
    label_total = lax.psum(jnp.sum(valid_f), "dp")
    head_b = jnp.pad(head_weight.astype(bf16), ((0, 0), (0, class_pad - classes)))
    valid_p = jnp.pad(valid_f, ((0, 0), (0, class_pad - classes)))
    targets_p = jnp.pad(targets, ((0, 0), (0, class_pad - classes)))
    share = width // mlp_count
    half = member % 2
    place = lax.axis_index("dp").astype(jnp.int32)
    core_s = (place % 2)[None]
    pick_row = jnp.arange(2 * share)
    pick_member = jnp.where(pick_row < share, member, member ^ 1)
    pick_row = pick_row % share
    pick_feature = (pick_row // BR) * (BR * mlp_count) + pick_member * BR + pick_row % BR
    picked = (pick_feature[:, None] == jnp.arange(width)[None, :]).astype(bf16)
    picked = jnp.pad(picked, ((0, 16), (0, 0)))
    member_s = member[None]
    time_rows = jnp.pad(tables[1:6], ((0, 3), (0, 0)))
    space_rows = jnp.pad(tables[6:11], ((0, 3), (0, 0)))
    low_rows = jnp.pad(tables[11:16], ((0, 3), (0, 0)))

    shared_here = shared_blocks // mlp_count
    here_ids = jnp.arange(shared_here + 2 * per_tile)
    block_of = jnp.where(
        here_ids < shared_here,
        here_ids * mlp_count + member,
        here_ids - shared_here + shared_blocks + member * 2 * per_tile,
    )
    here_slots = slot_index[block_of]
    dests = (here_slots // (slots * mlp_count)) * slots + here_slots % slots
    pix, label_total, head_b, valid_p, targets_p, picked, dests = lax.optimization_barrier(
        (pix, label_total, head_b, valid_p, targets_p, picked, dests)
    )
    cube32 = jax.ShapeDtypeStruct((frames, padded, width), f32)
    cube16 = jax.ShapeDtypeStruct((frames, padded, width), bf16)
    thin32 = jax.ShapeDtypeStruct((frames, padded, 128), f32)
    row32 = jax.ShapeDtypeStruct((8, width), f32)
    group_rows = GROUPS_AT_ONCE * GROUP
    frame_rows = FRAMES_AT_ONCE * padded
    group_spec = pl.BlockSpec((frames, group_rows, width), lambda g, *_: (0, g, 0))
    group_thin = pl.BlockSpec((frames, group_rows, 128), lambda g, *_: (0, g, 0))
    patch_spec = pl.BlockSpec((group_rows, width), lambda g, *_: (g, 0))
    frame_spec = pl.BlockSpec((FRAMES_AT_ONCE, padded, width), lambda f, *_: (f, 0, 0))
    frame_thin = pl.BlockSpec((FRAMES_AT_ONCE, padded, 128), lambda f, *_: (f, 0, 0))
    gp_spec = pl.BlockSpec(
        (mlp_count, FRAMES_AT_ONCE, padded, width), lambda f, *_: (0, f, 0, 0)
    )
    time_grid = (-(-groups // GROUPS_AT_ONCE),)
    half_frames = frames // 2
    space_grid = (half_frames // FRAMES_AT_ONCE,)
    half_blocks = groups // 2 // GROUPS_AT_ONCE
    rest = groups - 2 * half_blocks * GROUPS_AT_ONCE
    half_rows = (half_blocks * GROUPS_AT_ONCE + rest) * GROUP
    back_grid = (half_blocks + (1 if rest else 0),)

    def half_index(s, m):
        ending = jnp.where(m[0] % 2 == 0, 2 * half_blocks, 2 * half_blocks - 1)
        return jnp.where(s < half_blocks, (m[0] % 2) * half_blocks + s, ending)

    back_spec = pl.BlockSpec((frames, group_rows, width), lambda s, i, m, c: (0, half_index(s, m), 0))
    back_thin = pl.BlockSpec((frames, group_rows, 128), lambda s, i, m, c: (0, half_index(s, m), 0))
    near_spec = pl.BlockSpec((half_frames, group_rows, width), lambda s, *_: (0, s, 0))
    act_spec = pl.BlockSpec((2, FRAMES_AT_ONCE, padded, width), lambda f, *_: (0, f, 0, 0))
    half16 = jax.ShapeDtypeStruct((half_frames, padded, width), bf16)
    half32 = jax.ShapeDtypeStruct((half_frames, padded, width), f32)
    half_thin = jax.ShapeDtypeStruct((half_frames, padded, 128), f32)
    frame_weight = lax.dynamic_slice_in_dim(frame_weight, half * half_frames, half_frames)

    def whole(*shape):
        return pl.BlockSpec(shape, lambda i, *_: (0,) * len(shape))

    rows_spec = whole(8, width)
    time_extra = whole(2 * frames * GROUP, PAIR)
    space_extra = whole(2 * padded, PAIR)
    pick_spec = whole(2 * share + 16, width)

    def call(
        kernel, name, units, scalars, grid, ins, in_specs, outs, out_specs, scratch, tiles=True
    ):
        return pl.pallas_call(
            kernel,
            grid_spec=pltpu.PrefetchScalarGridSpec(
                num_scalar_prefetch=len(scalars),
                grid=grid,
                in_specs=([any_spec] if tiles else []) + in_specs,
                out_specs=out_specs,
                scratch_shapes=scratch,
            ),
            out_shape=outs,
            compiler_params=params,
            cost_estimate=pl.CostEstimate(
                flops=units * 2 * frames * padded * width * width,
                bytes_accessed=16 * width * width,
                transcendentals=0,
            ),
            name=name,
        )(*scalars, *([gathered] if tiles else []), *ins)

    def tile_bufs(*shapes):
        return [pltpu.VMEM((rows * width, cols * width), bf16) for rows, cols in shapes]

    x1, hid0, hat0, rstd0, q_t, k_t, v_t, o_t = call(
        partial(time_forward, groups),
        "time_forward",
        14,
        [slot_index, member_s],
        time_grid,
        [pix, pos, trow, time_rows, time_q, time_k],
        [group_spec, patch_spec, whole(frames, width), rows_spec, time_extra, time_extra],
        [half32, cube16, cube16, thin32] + [cube16] * 4,
        [near_spec] + [group_spec] * 2 + [group_thin] + [group_spec] * 4,
        tile_bufs((1, 1), (1, 3), (1, 1))
        + [pltpu.VMEM((frames * group_rows, width), f32), pltpu.SemaphoreType.DMA((3,))],
    )
    (hid1, hat1, rstd1, q_s, k_s, v_s, o_s, hid2, hat2, rstd2, hat3, rstd3, gp, act, pool) = call(
        lambda s, fw, m, *refs: space_forward(s, fw, m, patches, *refs),
        "space_forward",
        15,
        [slot_index, frame_weight, member_s],
        space_grid,
        [x1, space_rows, low_rows, space_q, space_k],
        [frame_spec, rows_spec, rows_spec, space_extra, space_extra],
        [half16, half16, half_thin]
        + [half16] * 4
        + [half16, half16, half_thin, half16, half_thin]
        + [
            jax.ShapeDtypeStruct((mlp_count, half_frames, padded, width), bf16),
            jax.ShapeDtypeStruct((2, half_frames, padded, width), bf16),
            row32,
        ],
        [frame_spec, frame_spec, frame_thin]
        + [frame_spec] * 4
        + [frame_spec, frame_spec, frame_thin, frame_spec, frame_thin]
        + [gp_spec, act_spec, rows_spec],
        tile_bufs((1, 3), (1, 1), (1, mlp_count), (mlp_count, 1))
        + [pltpu.VMEM((frame_rows, mlp_count * width), bf16), pltpu.SemaphoreType.DMA((4,))],
    )

    pool_other = swap(pool, "mlp", 1)
    middle = width // 2
    squares16 = jax.ShapeDtypeStruct((2, 2, width, middle), bf16)
    pair16 = jax.ShapeDtypeStruct((2, half_frames, padded, width), bf16)
    dx2, g3, du, rows_low, small = call(
        lambda s, fw, m, *refs: mlp_backward(s, fw, m, patches, *refs),
        "mlp_backward",
        9,
        [slot_index, frame_weight, member_s],
        space_grid,
        [
            pool, pool_other, head_b, valid_p, targets_p, label_total[None],
            hat2, rstd2, hat3, rstd3, gp, low_rows,
        ],
        [
            rows_spec, rows_spec, whole(width, class_pad), whole(1, class_pad), whole(1, class_pad),
            pl.BlockSpec(memory_space=pltpu.SMEM),
            frame_spec, frame_thin, frame_spec, frame_thin, gp_spec, rows_spec,
        ],
        [half32, half16, pair16, row32, row32],
        [frame_spec, frame_spec, act_spec, rows_spec, rows_spec],
        tile_bufs((1, mlp_count), (mlp_count, 1))
        + [
            pltpu.VMEM((frame_rows, mlp_count * width), bf16),
            pltpu.VMEM((8, width), f32),
            pltpu.VMEM((5, 8, width), f32),
            pltpu.SemaphoreType.DMA((2,)),
        ],
    )

    grads_spec = pl.BlockSpec((FRAMES_AT_ONCE, padded, 4 * width), lambda f, *_: (f, 0, 0))
    main = half_blocks * group_rows
    half_spec = pl.BlockSpec((FRAMES_AT_ONCE, half_rows, width), lambda f, *_: (f, 0, 0))
    swapped16 = jax.ShapeDtypeStruct((half_frames, half_rows, width), bf16)
    near, leaving, grads_space, norm_space = call(
        partial(space_backward, main),
        "space_backward",
        11,
        [slot_index, member_s],
        space_grid,
        [dx2, hat1, rstd1, q_s, k_s, v_s, space_rows, space_q, space_k],
        [frame_spec] * 2 + [frame_thin] + [frame_spec] * 3 + [rows_spec, space_extra, space_extra],
        [swapped16] * 2
        + [jax.ShapeDtypeStruct((half_frames, padded, 4 * width), bf16), row32],
        [half_spec] * 2 + [grads_spec, rows_spec],
        tile_bufs((1, 3), (1, 1))
        + [
            pltpu.VMEM((2, 8, width), f32),
            pltpu.VMEM((frame_rows, width), bf16),
            pltpu.VMEM((FRAMES_AT_ONCE, padded, width), bf16),
            pltpu.SemaphoreType.DMA((2,)),
        ],
    )

    leaving, late_hid1, late_hid2 = lax.optimization_barrier((leaving, hid1, hid2))
    far = swap(leaving, "mlp", 1)
    clip_spec = whole(half_frames, padded, width)
    one_spec = pl.BlockSpec((1, half_frames, padded, width), lambda i, c: (i, 0, 0, 0))
    square_spec = pl.BlockSpec((1, 2, width, middle), lambda i, c: (i, 0, 0, 0))
    keep_mlp, send_mlp = call(
        mlp_weights,
        "mlp_weights",
        2,
        [core_s],
        (2,),
        [late_hid2, g3, du, act],
        [clip_spec, clip_spec, one_spec, one_spec],
        [squares16] * 2,
        [square_spec] * 2,
        [pltpu.VMEM((2, width, width), f32)],
        tiles=False,
    )
    met_mlp = swap(send_mlp, "dp", 1)
    keep_space, send_space, sums_space = call(
        space_weights,
        "space_weights",
        2,
        [core_s],
        (4,),
        [picked, late_hid1, o_s, grads_space],
        [
            pick_spec, clip_spec, clip_spec,
            pl.BlockSpec((half_frames, padded, width), lambda i, c: (0, 0, i)),
        ],
        [jax.ShapeDtypeStruct((2, 4, share, middle), bf16)] * 2
        + [jax.ShapeDtypeStruct((4, 8, width), f32)],
        [pl.BlockSpec((2, 1, share, middle), lambda i, c: (0, i, 0, 0))] * 2
        + [pl.BlockSpec((1, 8, width), lambda i, c: (i, 0, 0))],
        [pltpu.VMEM((2 * share + 16, half_frames * padded), bf16),
         pltpu.VMEM((2 * share + 16, width), f32)],
        tiles=False,
    )
    far, keep_space, send_space = lax.optimization_barrier((far, keep_space, send_space))
    met_space = swap(send_space, "dp", 1)
    chip_mlp = added(keep_mlp[1], met_mlp[1]).astype(bf16)
    chip_space = added(keep_space[1], met_space[1]).astype(bf16)
    far, chip_mlp, chip_space = lax.optimization_barrier((far, chip_mlp, chip_space))
    far_mlp = swap(chip_mlp, "mlp", 1)
    far_space = swap(chip_space, "mlp", 1)
    keep_time, send_time, rows_time, grad_pos, grad_frames = call(
        partial(time_backward, rest),
        "time_backward",
        18,
        [slot_index, member_s, core_s],
        back_grid,
        [near, far, hid0, hat0, rstd0, q_t, k_t, v_t, o_t, pix, time_rows, picked, time_q, time_k],
        [near_spec] * 2
        + [back_spec] * 2
        + [back_thin]
        + [back_spec] * 5
        + [rows_spec, pick_spec, time_extra, time_extra],
        [jax.ShapeDtypeStruct((2, 5, share, middle), bf16)] * 2
        + [
            row32,
            jax.ShapeDtypeStruct((half_rows, width), f32),
            jax.ShapeDtypeStruct((frames, width), f32),
        ],
        [whole(2, 5, share, middle)] * 2 + [rows_spec, patch_spec, whole(frames, width)],
        tile_bufs((1, 3), (1, 1))
        + [
            pltpu.VMEM((2 * share + 16, 3 * width), f32),
            pltpu.VMEM((2 * share + 16, width), f32),
        ]
        + [
            pltpu.VMEM((2 * share + 16, width), f32),
            pltpu.VMEM((2, 8, width), f32),
            pltpu.VMEM((frames, group_rows, 3 * width), bf16),
            pltpu.VMEM((frames, group_rows, width), bf16),
            pltpu.SemaphoreType.DMA((2,)),
        ],
    )

    send_time, far_mlp, far_space = lax.optimization_barrier((send_time, far_mlp, far_space))
    met_time = swap(send_time, "dp", 1)
    chip_time = added(keep_time[1], met_time[1]).astype(bf16)
    chip_time, grad_frames, grad_pos = lax.optimization_barrier(
        (chip_time, grad_frames, grad_pos)
    )
    far_time = swap(chip_time, "mlp", 1)
    grad_time = jnp.einsum("ft,fd->td", time_hot, grad_frames, precision=highest)
    main = half_blocks * group_rows
    all_pos = jnp.concatenate(
        [jnp.where(half == i, grad_pos[:main], 0.0) for i in range(2)] + [grad_pos[main:]]
    )
    table_rows = tables.shape[0]
    table_part = jnp.concatenate(
        [
            jnp.sum(grad_frames, axis=0, keepdims=True),
            rows_time[:5],
            norm_space[:2],
            sums_space[0, :1],
            sums_space[2, :1],
            sums_space[3, :1],
            rows_low[:5],
            all_pos[:patches],
            grad_time,
        ]
    )
    rows_each = -(-table_rows // (dp_count * mlp_count))
    table_part = jnp.pad(
        table_part, ((0, rows_each * dp_count * mlp_count - table_rows), (0, 0))
    ).reshape(dp_count, mlp_count, rows_each, width)

    def table_of(which):
        rows_now = lax.dynamic_index_in_dim(table_part, which, 1, False).astype(bf16)
        return jnp.pad(rows_now, ((0, 0), (0, 16 - rows_each), (0, 0)))

    table_pair = jnp.stack([table_of(member), table_of(member ^ 1)])
    columns = jnp.stack([table_pair[..., :middle], table_pair[..., middle:]])
    keep_table = lax.dynamic_index_in_dim(columns, place % 2, 0, False)
    met_table = swap(lax.dynamic_index_in_dim(columns, 1 - place % 2, 0, False), "dp", 1)
    far_table = swap(added(keep_table[1], met_table[1]).astype(bf16), "mlp", 1)

    def blocks_of(*parts):
        return [part.reshape(part.shape[0], -1, BR, middle) for part in parts]

    sources = (
        blocks_of(keep_time, keep_space, keep_mlp)
        + [keep_table]
        + blocks_of(met_time, met_space, met_mlp)
        + [met_table]
        + [part.reshape(-1, BR, middle) for part in (far_time, far_space, far_mlp)]
        + [far_table]
    )
    bits = dp_count.bit_length() - 1
    chunk = jax.ShapeDtypeStruct((dp_count // 4, slots * BR + 16, middle), bf16)
    packed = pl.pallas_call(
        partial(pack, bits),
        grid_spec=pltpu.PrefetchScalarGridSpec(
            num_scalar_prefetch=2,
            grid=(1,),
            in_specs=[
                pl.BlockSpec((1,) + part.shape[1:], lambda i, *_: (0, 0, 0, 0))
                if part.ndim == 4
                else whole(*part.shape)
                for part in sources
            ],
            out_specs=[any_spec] * 4,
            scratch_shapes=[pltpu.VMEM(part.shape, bf16) for part in sources[8:]]
            + [pltpu.SemaphoreType.DMA((4,))],
        ),
        out_shape=[chunk] * 4,
        compiler_params=params,
        name="pack",
    )(dests, place[None], *sources)
    sum_a, sum_b = (value.reshape(value.shape[-2:]) for value in halve(*packed, "dp"))
    even = place % 2 == 0
    mine = jnp.where(even, sum_a, sum_b)
    met = swap(jnp.where(even, sum_b, sum_a), "dp", 1)
    summed = jnp.concatenate([jnp.where(even, mine, met), jnp.where(even, met, mine)], axis=1)
    my_slots = (place * mlp_count + member) * slots + jnp.arange(slots)
    filled = jnp.any(slot_index[:, None] == my_slots[None, :], axis=0)
    filled = jnp.repeat(filled, BR)[:, None]
    own_grad = jnp.where(filled, summed[: slots * BR], 0.0)
    squares_own = jnp.sum(own_grad * own_grad)
    block = jnp.concatenate(
        [
            jnp.pad(summed[slots * BR : slots * BR + rows_each], ((0, 7 - rows_each), (0, 0))),
            jnp.broadcast_to(squares_own, (1, width)),
            small,
        ]
    )
    blocks = jnp.concatenate(
        [spread_four(block[:8], "mlp"), block[None, 8:]], axis=0
    )
    blocks = lax.all_gather(blocks, "dp", axis=0)
    heads, blocks = blocks[:, mlp_count], blocks[:, :mlp_count]
    grad_head = jnp.einsum("cd,ck->dk", heads[:, 0], heads[:, 1, :classes], precision=highest)
    loss_sum = jnp.sum(heads[:, 2, 0])
    grad_tables = blocks[:, :, :rows_each].reshape(-1, width)[:table_rows]
    grad_norm = jnp.sqrt(
        jnp.sum(blocks[:, :, 7, 0])
        + jnp.sum(grad_tables * grad_tables)
        + jnp.sum(grad_head * grad_head)
    )
    factor = jnp.minimum(1.0, clip_max / (grad_norm + 1e-06))
    new_slots = adamw(
        slot_weight, own_grad * factor, slot_moment1, slot_moment2, decay_rate, learn_rate
    )
    new_tabs = adamw(tables, grad_tables * factor, table_moment1, table_moment2, 0.0, table_rate)
    new_heads = adamw(
        head_weight, grad_head * factor, head_moment1, head_moment2, decay_rate, learn_rate
    )
    return (
        loss_sum,
        label_total,
        grad_norm,
        new_slots[0],
        new_slots[1],
        new_slots[2],
        new_tabs[0],
        new_tabs[1],
        new_tabs[2],
        new_heads[0],
        new_heads[1],
        new_heads[2],
    )


def solution(mesh):
    return jax.shard_map(
        local,
        mesh=mesh,
        in_specs=(
            P("dp", None, None, None),
            P("dp"),
            P("dp", None),
            P("dp", None),
            P("dp", None),
            P("dp", None),
            P(),
            P(("dp", "mlp"), None),
            P(("dp", "mlp"), None),
            P(("dp", "mlp"), None),
            P(),
            P(),
            P(),
            P(),
            P(),
            P(),
        ),
        out_specs=(
            P(),
            P(),
            P(),
            P(("dp", "mlp"), None),
            P(("dp", "mlp"), None),
            P(("dp", "mlp"), None),
            P(),
            P(),
            P(),
            P(),
            P(),
            P(),
        ),
        check_vma=False,
    )
```
